32 devices in a mesh: grp: 2 (over x), bits: 16 (over z, y, core).
Axes of the slice: x: 2, y: 2, z: 4, core: 2. Of those that a mesh axis runs over, the one named last changes fastest.
Arguments:
- prefix: bfloat16 [128, 16, 1024], P(('grp', 'bits')), parts along dimension 0, may hold values from -6 to 6
- first_suffix: bfloat16 [8, 2, 512, 512], P('grp', None, 'bits'), parts along dimension 0, may hold values from -0.109375 to 0.109375
- pair_prefix: int32 [256, 3], P(('grp', 'bits')), parts along dimension 0, may hold values from 0 to 3
- pair_suffix: int32 [256, 3], P(('grp', 'bits')), parts along dimension 0, may hold values from 0 to 3, all different within a row
- merge_count: int32 [256], P(('grp', 'bits')), parts along dimension 0, may hold values from 1 to 3, as said below
- suffix: bfloat16 [32, 2, 512, 512], P(('grp', 'bits')), parts along dimension 0, may hold values from -0.1875 to 0.1875
- routes: int32 [256, 12], P(('grp', 'bits')), parts along dimension 0, may hold values from 0 to 15, all different within a row; in each aligned block of 8 rows (0 to 7, 8 to 15, ...) at most 8 rows name the same one
- cap: bfloat16 [2, 512, 64], replicated, may hold values from -0.0546875 to 0.0546875
Outputs:
- capped: float32 [256, 16, 128], P(('grp', 'bits')), parts along dimension 0
The draws below stay inside these ranges and needn't reach their ends.
There are 2 independent parts, one for each index of `grp`. The reference program is written for one: setup_inputs(seed, part) draws one part's arguments, and reference() takes and returns one part's arrays. A program takes and returns all parts, laid end to end along the dimension named above; an argument that names none is the same for every part. Nothing has to cross between parts.
Inputs may be any that keep to these rules, and one draw needn't show every extreme that they name: `pair_suffix`: each row names 3 different lifetime-one blocks. `merge_count`: some piece has exactly 3 merges and some exactly one. `routes`: each row names 12 different suffixes; in each aligned block of 8 rows no suffix is named by more than 8 rows, a bound that some block reaches.
All inputs are finite; a program needn't handle non-finite values.
Results may differ from the reference program's by a relative error of at most 0.005.
Values may be sent and summed in bfloat16 or wider, within the bound.
No kernel may reach another device: no remote copies, remote signals or barrier semaphores. Data moves between devices by JAX's collectives and lax.ppermute only.
A program may use at most 64 MiB of HBM per device.

```python
import math
import jax
import jax.numpy as jnp
import numpy as np
from jax import lax

W = 512
CAPW = 64
PR = 16
PIECES_DEV = 8
PRE_DEV = 4
NA = 4
K1 = 3
TOP = 12
NSUF = 16
PIECES = 128
NPRE = 64
MOST = 8


def draw_merge_count(key, part):
    counts = jax.random.randint(key, (PIECES,), 1, K1 + 1)
    chosen = jax.random.randint(jax.random.fold_in(key, 7), (), 0, PIECES)
    counts = counts.at[chosen].set(K1)
    counts = counts.at[(chosen + 1) % PIECES].set(1)
    return counts.astype(jnp.int32)


def touch_ends(array, own_key, low, high):
    longest = array.shape.index(max(array.shape))
    spots = []
    for shift in (0, 1):
        where = [jax.random.randint(jax.random.fold_in(own_key, axis), (), 0, length) for axis, length in enumerate(array.shape)]
        where[longest] = (where[longest] + shift) % array.shape[longest]
        spots.append(tuple(where))
    return array.at[spots[0]].set(low).at[spots[1]].set(high)


def level_of(key, shape, cuts, least, high):
    gain = 1.0
    for axis_at, blocks in cuts:
        heights = jax.random.uniform(jax.random.fold_in(jax.random.fold_in(key, 6), axis_at), (blocks,), jnp.float32, least / len(cuts), high / len(cuts))
        gain = gain * jnp.repeat(jnp.exp(heights), shape[axis_at] // blocks).reshape((-1,) + (1,) * (len(shape) - 1 - axis_at))
    return gain


def picks_of(own_key, rows, amount, top, lift):
    order = jax.random.permutation(jax.random.fold_in(own_key, 1), amount)
    favour = order
    for power in range(3):
        favour = favour * favour // amount
    favour = favour * lift // amount
    chance = jax.random.randint(jax.random.fold_in(own_key, 2), (rows, amount), 0, 4096) + favour
    fixed_rows = jax.random.permutation(jax.random.fold_in(own_key, 3), rows)[jnp.arange(amount) % rows]
    chance = jnp.where(jnp.arange(rows)[:, None] == fixed_rows[None, :], 1 << 14, chance)
    score = chance * amount + jnp.arange(amount)
    return lax.top_k(score.astype(jnp.int32), top)[1].astype(jnp.int32)


def routed_block(key, own, number, rows, number_of, top, bound, slope):
    order = jax.random.permutation(key, number_of)
    crowded, ordinary = portions_of(number_of, rows * top, bound, slope, True), portions_of(number_of, rows * top, bound, slope, False)
    places = jnp.arange(number_of)

    def named(sizes, turn):
        used = int((sizes > 0).sum())
        fixed = max(1, used // 4)
        passed = fixed + (places - fixed + turn * (used - fixed)) % max(1, number_of - fixed)
        return jnp.zeros((number_of,), jnp.int32).at[order[jnp.where(places < fixed, places, passed)]].set(jnp.asarray(sizes, jnp.int32))

    sizes = jnp.where(number % 4 == 0, named(crowded, number // 4), named(ordinary, number - number // 4 - 1))
    mixed = jax.random.permutation(jax.random.fold_in(own, 3), number_of)
    donor, taker = mixed[0:number_of // 2 * 2:2], mixed[1:number_of // 2 * 2:2]
    margin = jnp.minimum(sizes[donor] - 1, bound - sizes[taker]) // 2
    margin = jnp.where((donor == order[0]) | (taker == order[0]) | (sizes[taker] == 0), 0, jnp.maximum(margin, 0))
    passed = jax.random.randint(jax.random.fold_in(own, 4), (number_of // 2,), 0, 1 << 20) % (margin + 1)
    sizes = sizes.at[donor].add(-passed).at[taker].add(passed)
    items = jnp.searchsorted(jnp.cumsum(sizes), jnp.arange(rows * top), side="right").astype(jnp.int32)
    listing = items.reshape(top, rows).T
    listing = listing[jax.random.permutation(jax.random.fold_in(own, 1), rows)]
    turn = jax.random.randint(jax.random.fold_in(own, 2), (rows, 1), 0, top)
    return jnp.take_along_axis(listing, (jnp.arange(top)[None, :] + turn) % top, axis=1)


def portions_of(amount, total, reach, lean, full):
    portions = [(1 << 20) // math.isqrt(rank ** lean) + 1 for rank in range(1, amount + 1)]
    largest = reach if full else min(reach, max(-(-total // amount), total * portions[0] // sum(portions)))
    least = 1 if total - largest >= amount - 1 else 0
    given, surplus = [largest] + [least] * (amount - 1), total - largest - least * (amount - 1)
    while surplus > 0:
        free = [i for i in range(1, amount) if given[i] < largest] or [i for i in range(1, amount) if given[i] < reach]
        pool, left = sum([portions[i] for i in free]), surplus
        for i in free:
            extra = min(reach - given[i], max(1, left * portions[i] // pool), surplus)
            given[i] = given[i] + extra
            surplus = surplus - extra
    return np.array(given)


def centred(stream_key, extent, spread, bound, shards=(), held_as=jnp.bfloat16):
    entries = jax.random.normal(stream_key, extent, jnp.float32) * spread
    if len(shards) > 0:
        entries = level_of(stream_key, extent, shards, -0.22, 0.18) * entries
    return jnp.clip(entries, min=-bound, max=bound).astype(held_as)


def setup_inputs(seed: int = 0, part: int = 0) -> dict:
    arg_keys = jax.random.split(jax.random.key(seed), 9)
    part_keys = jax.random.split(jax.random.fold_in(arg_keys[8], part), 9)
    prefix = centred(part_keys[0], (NPRE, PR, 2 * W), 1.0, 6.0, ((0, 16),))
    first_suffix = centred(part_keys[1], (NA, 2, W, W), (2 * W * K1) ** -0.5, 0.109375, ((2, 16),))
    pair_prefix = touch_ends(jax.random.randint(part_keys[2], (PIECES, K1), 0, PRE_DEV), jax.random.fold_in(part_keys[2], 1), 0, PRE_DEV - 1).astype(jnp.int32)
    pair_suffix = picks_of(part_keys[3], PIECES, NA, K1, 0)
    merge_count = draw_merge_count(jax.random.fold_in(jax.random.fold_in(arg_keys[8], part), 71), part)
    suffix = centred(part_keys[5], (NSUF, 2, W, W), (2 * W) ** -0.5, 0.1875, ((0, 16),))
    routes_keys = jax.random.split(jax.random.fold_in(part_keys[6], 1), PIECES // PIECES_DEV)
    routes_turns = jax.random.permutation(jax.random.fold_in(part_keys[6], 3), PIECES // PIECES_DEV)
    routes = jax.vmap(lambda own, number: routed_block(jax.random.fold_in(part_keys[6], 2), own, number, PIECES_DEV, NSUF, TOP, MOST, 2))(routes_keys, routes_turns).reshape((PIECES, TOP))
    cap = centred(arg_keys[7], (2, W, CAPW), (2 * W * TOP) ** -0.5, 0.0546875)
    return dict(prefix=prefix, first_suffix=first_suffix, pair_prefix=pair_prefix, pair_suffix=pair_suffix, merge_count=merge_count, suffix=suffix, routes=routes, cap=cap)


HIGHEST_PRECISION = lax.Precision.HIGHEST


def complex_form(blocks):
    real_part = blocks[..., 0, :, :]
    imag_part = blocks[..., 1, :, :]
    upper_half = jnp.concatenate([real_part, imag_part], axis=-1)
    lower_half = jnp.concatenate([-imag_part, real_part], axis=-1)
    return jnp.concatenate([upper_half, lower_half], axis=-2)


def reference(prefix, first_suffix, pair_prefix, pair_suffix, merge_count, suffix, routes, cap):
    first_forms = complex_form(first_suffix.astype(jnp.float32))
    cap_form = complex_form(cap.astype(jnp.float32))

    def one_piece(piece_index):
        owner_index = piece_index // PIECES_DEV
        prefix_rows = prefix[PRE_DEV * owner_index + pair_prefix[piece_index]].astype(jnp.float32)
        block_forms = first_forms[pair_suffix[piece_index]]
        live_mask = (jnp.arange(K1, dtype=jnp.int32) < merge_count[piece_index]).astype(jnp.float32)
        merge_terms = jnp.einsum("krc,kcw->krw", prefix_rows, block_forms, precision=HIGHEST_PRECISION)
        state_rows = jnp.sum(merge_terms * live_mask[:, None, None], axis=0).astype(jnp.bfloat16)
        state_rows = lax.optimization_barrier(state_rows).astype(jnp.float32)
        chosen = complex_form(suffix[routes[piece_index]].astype(jnp.float32))
        partial_value = jnp.einsum("rc,kcw->krw", state_rows, chosen, precision=HIGHEST_PRECISION).astype(jnp.bfloat16)
        partial_value = lax.optimization_barrier(partial_value).astype(jnp.float32)
        merged = jnp.sum(partial_value, axis=0)
        return jnp.dot(merged, cap_form, precision=HIGHEST_PRECISION)

    return lax.map(one_piece, jnp.arange(PIECES, dtype=jnp.int32))
```

```python
import functools

import jax
import jax.numpy as jnp
from jax import lax
from jax.experimental import pallas as pl
from jax.experimental.pallas import tpu as pltpu
from jax.sharding import PartitionSpec as P

HIGHEST_PRECISION = lax.Precision.HIGHEST
LANES = 128
PLANE = 4
VMEM_BYTES = 32 * 1024 * 1024


def complex_form(blocks):
    real_part = blocks[..., 0, :, :]
    imag_part = blocks[..., 1, :, :]
    upper_half = jnp.concatenate([real_part, imag_part], axis=-1)
    lower_half = jnp.concatenate([-imag_part, real_part], axis=-1)
    return jnp.concatenate([upper_half, lower_half], axis=-2)


def swap(x, bit):
    owners = lax.axis_size("bits")
    return lax.ppermute(x, "bits", [(i, i ^ bit) for i in range(owners)])


def pack_kernel(planes, suffix_ref, cap_ref, first_ref, plan_ref, *packs):
    me = lax.axis_index("bits")
    plane = me // PLANE
    cap_real = cap_ref[0].astype(jnp.float32)
    cap_imag = cap_ref[1].astype(jnp.float32)
    upper = jnp.concatenate([cap_real, cap_imag], axis=1).astype(jnp.bfloat16)
    lower = jnp.concatenate([-cap_imag, cap_real], axis=1).astype(jnp.bfloat16)
    blocks, _, depth, width = first_ref.shape
    part = width // planes
    for k in range(planes):
        there = pl.ds(pl.multiple_of((plane ^ k) * part, part), part)
        for a in range(blocks):
            for c in range(2):
                packs[k][2 * a + c] = first_ref[a, c, :, there]
        closed = jnp.dot(suffix_ref[0, there, :], upper, preferred_element_type=jnp.float32)
        closed += jnp.dot(suffix_ref[1, there, :], lower, preferred_element_type=jnp.float32)
        closed = closed.astype(jnp.bfloat16)
        for c in range(part // depth):
            packs[k][2 * blocks + c] = closed[c * depth:(c + 1) * depth]
        packs[k][2 * blocks + part // depth] = plan_ref[...]


def work_kernel(planes, blocks, merges, listed, plan_ref, *refs):
    slots = planes * PLANE
    packs, prefixes = refs[:slots], refs[slots:slots + planes]
    outs = refs[slots + planes:slots + 2 * planes]
    forms, closed, rows, products, state, wide, terms, sems = refs[slots + 2 * planes:]
    me = lax.axis_index("bits")
    depth = packs[0].shape[1]
    part = closed.shape[1] * depth
    held = prefixes[0].shape[0]
    rows_piece = prefixes[0].shape[1]
    half = prefixes[0].shape[2] // 2
    pieces = outs[0].shape[0]
    copies = []
    for j in range(slots):
        there = pl.ds(pl.multiple_of((me ^ j) * depth, depth), depth)
        copies.append(pltpu.make_async_copy(packs[j].at[0:2 * blocks], forms.at[:, there, :], sems.at[2 * j]))
        copies.append(
            pltpu.make_async_copy(
                packs[j].at[2 * blocks:2 * blocks + part // depth], closed.at[j], sems.at[2 * j + 1]
            )
        )
    for k in range(planes):
        copies.append(pltpu.make_async_copy(prefixes[k], rows.at[k], sems.at[2 * slots + k]))
    for copy in copies:
        copy.start()
    for copy in copies:
        copy.wait()
    left = rows[...].reshape(planes * held * rows_piece, 2 * half)
    for a in range(blocks):
        right = jnp.concatenate([forms[2 * a], forms[2 * a + 1]], axis=1)
        real = jnp.dot(left[:, :half], right, preferred_element_type=jnp.float32)
        imag = jnp.dot(left[:, half:], right, preferred_element_type=jnp.float32)
        products[a, :, :part] = real[:, :part] - imag[:, part:]
        products[a, :, part:] = real[:, part:] + imag[:, :part]
    for i in range(planes * pieces):
        total = None
        for m in range(merges):
            row = (i // pieces * held + plan_ref[i, m]) * rows_piece
            term = products[plan_ref[i, merges + m], pl.ds(pl.multiple_of(row, rows_piece), rows_piece), :]
            term = jnp.where(m < plan_ref[i, 2 * merges], term, 0.0)
            total = term if total is None else total + term
        state[i * rows_piece:(i + 1) * rows_piece, :] = total.astype(jnp.bfloat16)
    lane = lax.broadcasted_iota(jnp.int32, (part, LANES), 1)
    for j in range(slots):
        real_rows = closed[j].reshape(part, LANES)
        turned = pltpu.roll(real_rows.astype(jnp.float32), LANES // 2, 1)
        turned = jnp.where(lane < LANES // 2, -turned, turned)
        wide[:part, j * LANES:(j + 1) * LANES] = real_rows
        wide[part:, j * LANES:(j + 1) * LANES] = turned.astype(jnp.bfloat16)
    for j in range(0, slots, 2):
        both = jnp.dot(state[...], wide[:, j * LANES:(j + 2) * LANES], preferred_element_type=jnp.float32)
        terms[j] = both[:, :LANES]
        terms[j + 1] = both[:, LANES:]
    for i in range(planes * pieces):
        total = None
        for k in range(listed):
            slot = plan_ref[i, 2 * merges + 1 + k] ^ me
            term = terms[slot, i * rows_piece:(i + 1) * rows_piece, :]
            total = term if total is None else total + term
        out = outs[i // pieces]
        out[i % pieces] = total.astype(out.dtype)


def in_planes(prefix, first_suffix, pair_prefix, pair_suffix, merge_count, suffix, routes, cap):
    owners = lax.axis_size("bits")
    planes = owners // PLANE
    pieces, merges = pair_prefix.shape
    listed = routes.shape[1]
    held, rows_piece, twice_width = prefix.shape
    blocks, _, depth, width = first_suffix.shape
    part = width // planes
    vmem = pl.BlockSpec(memory_space=pltpu.VMEM)
    anywhere = pl.BlockSpec(memory_space=pl.ANY)
    plan = jnp.concatenate([pair_prefix, pair_suffix, merge_count[:, None], routes], axis=1)
    entries = plan.shape[1]
    plan = jnp.pad(plan, ((0, depth - pieces), (0, LANES - entries))).astype(jnp.bfloat16)
    pack = jax.ShapeDtypeStruct((2 * blocks + part // depth + 1, depth, LANES), jnp.bfloat16)
    packs = pl.pallas_call(
        functools.partial(pack_kernel, planes),
        out_shape=[pack] * planes,
        in_specs=[vmem] * 4,
        out_specs=[vmem] * planes,
        compiler_params=pltpu.CompilerParams(vmem_limit_bytes=VMEM_BYTES),
        name="pack",
    )(suffix[0], cap, first_suffix, plan)
    packs = [packs[0]] + [swap(packs[k], k * PLANE) for k in range(1, planes)]
    prefixes = [prefix] + [swap(prefix, k * PLANE) for k in range(1, planes)]
    across = [swap(p, 2) for p in packs]
    beside = [swap(p, 1) for p in packs]
    corner = [swap(p, 1) for p in across]
    everyone = [group[k] for k in range(planes) for group in (packs, beside, across, corner)]
    routing = jnp.concatenate([p[-1, :pieces, :entries] for p in packs], axis=0).astype(jnp.int32)
    slots = owners
    rows = planes * held * rows_piece
    state_rows = planes * pieces * rows_piece
    outs = pl.pallas_call(
        functools.partial(work_kernel, planes, blocks, merges, listed),
        out_shape=[
            jax.ShapeDtypeStruct((pieces, rows_piece, LANES), jnp.float32 if k == 0 else jnp.bfloat16)
            for k in range(planes)
        ],
        in_specs=[pl.BlockSpec(memory_space=pltpu.SMEM)] + [anywhere] * (slots + planes),
        out_specs=[vmem] * planes,
        scratch_shapes=[
            pltpu.VMEM((2 * blocks, width, LANES), jnp.bfloat16),
            pltpu.VMEM((slots, part // depth, depth, LANES), jnp.bfloat16),
            pltpu.VMEM((planes, held, rows_piece, twice_width), jnp.bfloat16),
            pltpu.VMEM((blocks, rows, 2 * part), jnp.float32),
            pltpu.VMEM((state_rows, 2 * part), jnp.bfloat16),
            pltpu.VMEM((2 * part, slots * LANES), jnp.bfloat16),
            pltpu.VMEM((slots, state_rows, LANES), jnp.float32),
            pltpu.SemaphoreType.DMA((2 * slots + planes,)),
        ],
        compiler_params=pltpu.CompilerParams(vmem_limit_bytes=VMEM_BYTES),
        name="work",
    )(routing, *everyone, *prefixes)
    total = outs[0]
    for k in range(1, planes):
        total = total + swap(outs[k], k * PLANE).astype(jnp.float32)
    return total


def by_owner(prefix, first_suffix, pair_prefix, pair_suffix, merge_count, suffix, routes, cap):
    pieces = pair_prefix.shape[0]
    merges = pair_prefix.shape[1]
    held_blocks = prefix.shape[0]
    rows_piece = prefix.shape[1]
    twice_width = prefix.shape[2]
    half_width = twice_width // 2
    first_count = first_suffix.shape[0]
    listed = routes.shape[1]
    owners = lax.axis_size("bits")
    slot_count = min(pieces, max(2, (2 * pieces * listed + owners - 1) // owners))
    live_mask = lax.broadcasted_iota(jnp.int32, (pieces, merges), 1) < merge_count[:, None]
    matches = (
        pair_suffix[:, :, None] == lax.broadcasted_iota(jnp.int32, (pieces, merges, first_count), 2)
    ) & live_mask[:, :, None]
    which_block = pair_prefix[:, :, None] == lax.broadcasted_iota(
        jnp.int32, (pieces, merges, held_blocks), 2
    )
    prefix_picks = jnp.einsum(
        "ika,ikp->iap", matches.astype(jnp.float32), which_block.astype(jnp.float32)
    ).astype(jnp.bfloat16)
    selected = jnp.einsum(
        "iap,prc->airc", prefix_picks, prefix, preferred_element_type=jnp.float32
    ).astype(jnp.bfloat16)
    selected = selected.reshape(first_count, pieces * rows_piece, twice_width)
    portion = lax.all_gather(first_suffix, "bits", axis=2, tiled=True)
    count_rows = portion.shape[2]
    real_cols = lax.slice_in_dim(selected, 0, count_rows, axis=2)
    imag_cols = lax.dynamic_slice_in_dim(selected, half_width, count_rows, 2)
    left_side = jnp.concatenate([real_cols, imag_cols], axis=2)
    upper_half = jnp.concatenate([portion[:, 0], portion[:, 1]], axis=2)
    lower_half = jnp.concatenate([-portion[:, 1], portion[:, 0]], axis=2)
    right_side = jnp.concatenate([upper_half, lower_half], axis=1)
    state_rows = jnp.einsum(
        "arc,acw->rw", left_side, right_side, preferred_element_type=jnp.float32
    )
    state_rows = state_rows.astype(jnp.bfloat16).reshape(pieces, rows_piece, twice_width)
    named_by = jnp.sum(
        (routes[:, :, None] == lax.broadcasted_iota(jnp.int32, (pieces, listed, owners), 2)).astype(
            jnp.int32
        ),
        axis=1,
    )
    slot_rank = jnp.cumsum(named_by, axis=0) - named_by
    slot_hit = (
        slot_rank[:, :, None] == lax.broadcasted_iota(jnp.int32, (pieces, owners, slot_count), 2)
    ) & (named_by[:, :, None] > 0)
    dispatch = jnp.transpose(slot_hit, (1, 2, 0)).astype(jnp.bfloat16)
    outgoing = jnp.einsum(
        "dmi,irc->dmrc", dispatch, state_rows, preferred_element_type=jnp.float32
    ).astype(jnp.bfloat16)
    own_form = complex_form(suffix[0])
    cap_form = complex_form(cap)
    products = jnp.einsum(
        "smrc,cw->smrw",
        lax.all_to_all(outgoing, "bits", split_axis=0, concat_axis=0, tiled=True),
        own_form,
        preferred_element_type=jnp.float32,
    ).astype(jnp.bfloat16)
    capped_terms = jnp.einsum(
        "smrw,wv->smrv", products, cap_form, preferred_element_type=jnp.float32
    )
    returned = lax.all_to_all(
        capped_terms.astype(jnp.bfloat16), "bits", split_axis=0, concat_axis=0, tiled=True
    ).astype(capped_terms.dtype)
    return jnp.einsum(
        "dmi,dmrv->irv", dispatch.astype(jnp.float32), returned, precision=HIGHEST_PRECISION
    )


def on_device(*args):
    prefix, first_suffix, cap = args[0], args[1], args[7]
    planes = lax.axis_size("bits") // PLANE
    width = first_suffix.shape[3]
    depth = first_suffix.shape[2]
    if planes & (planes - 1) == 0 and planes > 0 and width == planes * LANES and 2 * cap.shape[2] == LANES and depth % 32 == 0:
        return in_planes(*args)
    return by_owner(*args)


def solution(mesh):
    return jax.shard_map(
        on_device,
        mesh=mesh,
        in_specs=(
            P(("grp", "bits"), None, None),
            P("grp", None, "bits", None),
            P(("grp", "bits"), None),
            P(("grp", "bits"), None),
            P(("grp", "bits")),
            P(("grp", "bits"), None, None, None),
            P(("grp", "bits"), None),
            P(),
        ),
        out_specs=P(("grp", "bits"), None, None),
        check_vma=False,
    )
```

```python
import functools

import jax
import jax.numpy as jnp
from jax import lax
from jax.experimental import pallas as pl
from jax.experimental.pallas import tpu as pltpu
from jax.sharding import PartitionSpec as P

HIGHEST_PRECISION = lax.Precision.HIGHEST
LANES = 128
PLANE = 4
VMEM_BYTES = 32 * 1024 * 1024
PACK_BYTES = 60 * 1024 * 1024
HEAD = 8


def complex_form(blocks):
    real_part = blocks[..., 0, :, :]
    imag_part = blocks[..., 1, :, :]
    upper_half = jnp.concatenate([real_part, imag_part], axis=-1)
    lower_half = jnp.concatenate([-imag_part, real_part], axis=-1)
    return jnp.concatenate([upper_half, lower_half], axis=-2)


def swap(x, bit):
    owners = lax.axis_size("bits")
    return lax.ppermute(x, "bits", [(i, i ^ bit) for i in range(owners)])


def pack_kernel(planes, *refs):
    sources, outs = refs[:8], refs[8:9 + planes]
    plan, closed, *copied, sems = refs[9 + planes:]
    suffix_ref, cap_ref, first_ref, prefix_ref, *numbers = copied
    pair_prefix_ref, pair_suffix_ref, count_ref, routes_ref = numbers
    plane = lax.axis_index("bits") // PLANE
    copies = [pltpu.make_async_copy(source, ref, sems.at[n]) for n, (source, ref) in enumerate(zip(sources, copied))]
    for copy in copies:
        copy.start()
    merges, pieces = pair_prefix_ref.shape
    listed = routes_ref.shape[1]
    plan[...] = jnp.zeros_like(plan)
    for copy in copies[4:]:
        copy.wait()
    plan[:merges, :pieces] = pair_prefix_ref[...]
    plan[merges:2 * merges, :pieces] = pair_suffix_ref[...]
    plan[2 * merges:2 * merges + 1, :pieces] = count_ref[...]
    plan[HEAD:HEAD + pieces, :listed] = routes_ref[...]
    routing = plan[...].astype(jnp.float32).astype(jnp.bfloat16)
    copies[1].wait()
    upper = jnp.concatenate([cap_ref[0], cap_ref[1]], axis=0)
    lower = jnp.concatenate([-cap_ref[1], cap_ref[0]], axis=0)
    blocks, _, depth, width = first_ref.shape
    part, span = width // 2, width // (planes // 2)
    turned = (((1,), (1,)), ((), ()))
    copies[0].wait()
    both = lax.dot_general(suffix_ref[0], upper, turned, preferred_element_type=jnp.float32)
    both += lax.dot_general(suffix_ref[1], lower, turned, preferred_element_type=jnp.float32)
    closed[...] = both.astype(jnp.bfloat16)
    copies[2].wait()
    copies[3].wait()
    held, rows_piece, twice_width = prefix_ref.shape
    per = depth // rows_piece
    for k in range(planes):
        low, high = plane % 2 ^ k % 2, plane // 2 ^ k // 2
        entries = []
        if k < 2:
            for a in range(blocks):
                for c in range(2):
                    for n in range(0, part, LANES):
                        entries.append(first_ref[a, c, :, pl.ds(pl.multiple_of(low * part + n, LANES), LANES)])
        for n in range(0, part, depth):
            entries.append(closed[pl.ds(pl.multiple_of(low * part + n, depth), depth), :])
        relayed = len(entries)
        entries.append(routing)
        for start in range(0, twice_width, width):
            for n in range(0, span, LANES):
                columns = pl.ds(pl.multiple_of(high * span + (start + n), LANES), LANES)
                for row in range(0, held, per):
                    entries.append(prefix_ref[row:row + per, :, columns].reshape(depth, LANES))
        for n, entry in enumerate(entries):
            if k == 0 and n >= relayed:
                outs[planes][n - relayed] = entry
            else:
                outs[k][n] = entry


def take_kernel(count, *refs):
    out = refs[count]
    for k in range(count):
        out[k] = refs[k][:out.shape[1]]


def take(packs, size):
    vmem = pl.BlockSpec(memory_space=pltpu.VMEM)
    return pl.pallas_call(
        functools.partial(take_kernel, len(packs)),
        out_shape=jax.ShapeDtypeStruct((len(packs), size) + packs[0].shape[1:], packs[0].dtype),
        in_specs=[vmem] * len(packs),
        out_specs=vmem,
        compiler_params=pltpu.CompilerParams(vmem_limit_bytes=VMEM_BYTES),
        cost_estimate=pl.CostEstimate(flops=0, bytes_accessed=2 ** 12, transcendentals=0),
        name="take",
    )(*packs)


def state_kernel(planes, blocks, merges, pieces, rows_piece, held, *refs):
    relays, packs = refs[:2 * PLANE], refs[2 * PLANE:2 * PLANE + planes]
    state, plan_out, forms, products, plan, sem = refs[2 * PLANE + planes:]
    me = lax.axis_index("bits")
    depth = packs[0].shape[1]
    span, twice_part = forms.shape[1:]
    part = twice_part // 2
    locals_ = []
    tail = 1 + 2 * (span // LANES) * (held * rows_piece // depth)
    for k in range(planes):
        first = packs[k].shape[0] - tail
        plan_out[k] = packs[k][first].astype(jnp.float32).astype(jnp.int32)
        locals_.append(packs[k].at[first + 1:first + tail])
    copy = pltpu.make_async_copy(plan_out, plan, sem)
    copy.start()
    for j in range(2 * PLANE):
        there = pl.ds(pl.multiple_of((me ^ j) % (2 * PLANE) * depth, depth), depth)
        for a in range(blocks):
            for n in range(twice_part // LANES):
                forms[a, there, n * LANES:(n + 1) * LANES] = relays[j][0, a * (twice_part // LANES) + n]
    chunks = held * rows_piece // depth
    rows = held * rows_piece
    left = []
    for c in range(2):
        for k in range(planes):
            columns = []
            for n in range(span // LANES):
                first = (c * (span // LANES) + n) * chunks
                columns.append(locals_[k][first:first + chunks].reshape(rows, LANES))
            left.append(jnp.concatenate(columns, axis=1))
    left = jnp.concatenate(left, axis=0)
    rows *= planes
    for a in range(blocks):
        both = jnp.dot(left, forms[a], preferred_element_type=jnp.float32)
        products[a, :, :part] = both[:rows, :part] - both[rows:, part:]
        products[a, :, part:] = both[:rows, part:] + both[rows:, :part]
    copy.wait()
    for i in range(planes * pieces):
        k, n = divmod(i, pieces)
        total = None
        for m in range(merges):
            row = pl.multiple_of((k * held + plan[k, m, n]) * rows_piece, rows_piece)
            term = products[plan[k, merges + m, n], pl.ds(row, rows_piece), :]
            term = jnp.where(m < plan[k, 2 * merges, n], term, 0.0)
            total = term if total is None else total + term
        state[i * rows_piece:(i + 1) * rows_piece, :] = total.astype(jnp.bfloat16)


def close_kernel(planes, listed, pieces, rows_piece, plan, state, *refs):
    slots = planes * PLANE
    relays, outs = refs[:2 * PLANE + PLANE], refs[3 * PLANE:3 * PLANE + planes]
    wide, terms = refs[3 * PLANE + planes:]
    me = lax.axis_index("bits")
    part = wide.shape[0] // 2
    lane = lax.broadcasted_iota(jnp.int32, (part, LANES), 1)
    for j in range(slots):
        n, b = divmod(j, PLANE)
        relay = relays[min(n, 2) * PLANE + b]
        first = relay.shape[1] - part // relay.shape[2]
        real_rows = relay[max(n - 2, 0), first:].reshape(part, LANES)
        turned = pltpu.roll(real_rows.astype(jnp.float32), LANES // 2, 1)
        turned = jnp.where(lane < LANES // 2, -turned, turned)
        wide[:part, j * LANES:(j + 1) * LANES] = real_rows
        wide[part:, j * LANES:(j + 1) * LANES] = turned.astype(jnp.bfloat16)
    for j in range(0, slots, 2):
        both = jnp.dot(state[...], wide[:, j * LANES:(j + 2) * LANES], preferred_element_type=jnp.float32)
        terms[j] = both[:, :LANES]
        terms[j + 1] = both[:, LANES:]
    for i in range(planes * pieces):
        k, n = divmod(i, pieces)
        total = None
        for m in range(listed):
            slot = plan[k, HEAD + n, m] ^ me
            term = terms[slot, i * rows_piece:(i + 1) * rows_piece, :]
            total = term if total is None else total + term
        outs[k][n] = total.astype(outs[k].dtype)


def in_planes(prefix, first_suffix, pair_prefix, pair_suffix, merge_count, suffix, routes, cap):
    owners = lax.axis_size("bits")
    planes = owners // PLANE
    pieces, merges = pair_prefix.shape
    listed = routes.shape[1]
    held, rows_piece, twice_width = prefix.shape
    blocks, _, depth, width = first_suffix.shape
    part, span = width // 2, width // (planes // 2)
    vmem = pl.BlockSpec(memory_space=pltpu.VMEM)
    smem = pl.BlockSpec(memory_space=pltpu.SMEM)
    params = pltpu.CompilerParams(vmem_limit_bytes=VMEM_BYTES)
    forms_size, closed_size = 2 * blocks * (part // LANES), part // depth
    tail = 1 + 2 * (span // LANES) * (held * rows_piece // depth)
    sources = (
        suffix[0],
        jnp.swapaxes(cap, 1, 2),
        first_suffix,
        prefix,
        pair_prefix.T,
        pair_suffix.T,
        merge_count[None],
        routes,
    )
    sizes = [forms_size + closed_size, forms_size + closed_size + tail] + [closed_size + tail] * (planes - 2) + [tail]
    *packs, local = pl.pallas_call(
        functools.partial(pack_kernel, planes),
        out_shape=[jax.ShapeDtypeStruct((size, depth, LANES), jnp.bfloat16) for size in sizes],
        in_specs=[pl.BlockSpec(memory_space=pl.ANY)] * len(sources),
        out_specs=[vmem] * len(sizes),
        scratch_shapes=[pltpu.VMEM((depth, LANES), jnp.int32), pltpu.VMEM((width, LANES), jnp.bfloat16)]
        + [pltpu.VMEM(source.shape, source.dtype) for source in sources]
        + [pltpu.SemaphoreType.DMA((len(sources),))],
        compiler_params=pltpu.CompilerParams(vmem_limit_bytes=PACK_BYTES),
        cost_estimate=pl.CostEstimate(flops=2 ** 20, bytes_accessed=2 ** 12, transcendentals=0),
        name="pack",
    )(*sources)
    relay = packs[0][None]
    packs = [local] + [swap(packs[k], k * PLANE) for k in range(1, planes)]
    relays = [relay, take(packs[1:2], forms_size + closed_size), take(packs[2:], closed_size)]
    relays = [(r, swap(r, 1), y, swap(y, 1)) for r, y in [(r, swap(r, 2)) for r in relays]]
    rows = planes * pieces * rows_piece
    state, plan = pl.pallas_call(
        functools.partial(state_kernel, planes, blocks, merges, pieces, rows_piece, held),
        out_shape=[
            jax.ShapeDtypeStruct((rows, 2 * part), jnp.bfloat16),
            jax.ShapeDtypeStruct((planes, depth, LANES), jnp.int32),
        ],
        in_specs=[vmem] * (2 * PLANE + planes),
        out_specs=[vmem] * 2,
        scratch_shapes=[
            pltpu.VMEM((blocks, span, 2 * part), jnp.bfloat16),
            pltpu.VMEM((blocks, planes * held * rows_piece, 2 * part), jnp.float32),
            pltpu.SMEM((planes, depth, LANES), jnp.int32),
            pltpu.SemaphoreType.DMA,
        ],
        compiler_params=params,
        name="state",
    )(*relays[0], *relays[1], *packs)
    sums = pl.pallas_call(
        functools.partial(close_kernel, planes, listed, pieces, rows_piece),
        out_shape=[
            jax.ShapeDtypeStruct((pieces, rows_piece, LANES), jnp.float32 if k == 0 else jnp.bfloat16)
            for k in range(planes)
        ],
        in_specs=[smem] + [vmem] * (1 + 3 * PLANE),
        out_specs=[vmem] * planes,
        scratch_shapes=[
            pltpu.VMEM((2 * part, owners * LANES), jnp.bfloat16),
            pltpu.VMEM((owners, rows, LANES), jnp.float32),
        ],
        compiler_params=params,
        name="close",
    )(plan, state, *relays[0], *relays[1], *relays[2])
    total = sums[0]
    for k in range(1, planes):
        total = total + swap(sums[k], k * PLANE).astype(jnp.float32)
    return total


def by_owner(prefix, first_suffix, pair_prefix, pair_suffix, merge_count, suffix, routes, cap):
    pieces = pair_prefix.shape[0]
    merges = pair_prefix.shape[1]
    held_blocks = prefix.shape[0]
    rows_piece = prefix.shape[1]
    twice_width = prefix.shape[2]
    half_width = twice_width // 2
    first_count = first_suffix.shape[0]
    listed = routes.shape[1]
    owners = lax.axis_size("bits")
    slot_count = min(pieces, max(2, (2 * pieces * listed + owners - 1) // owners))
    live_mask = lax.broadcasted_iota(jnp.int32, (pieces, merges), 1) < merge_count[:, None]
    matches = (
        pair_suffix[:, :, None] == lax.broadcasted_iota(jnp.int32, (pieces, merges, first_count), 2)
    ) & live_mask[:, :, None]
    which_block = pair_prefix[:, :, None] == lax.broadcasted_iota(
        jnp.int32, (pieces, merges, held_blocks), 2
    )
    prefix_picks = jnp.einsum(
        "ika,ikp->iap", matches.astype(jnp.float32), which_block.astype(jnp.float32)
    ).astype(jnp.bfloat16)
    selected = jnp.einsum(
        "iap,prc->airc", prefix_picks, prefix, preferred_element_type=jnp.float32
    ).astype(jnp.bfloat16)
    selected = selected.reshape(first_count, pieces * rows_piece, twice_width)
    portion = lax.all_gather(first_suffix, "bits", axis=2, tiled=True)
    count_rows = portion.shape[2]
    real_cols = lax.slice_in_dim(selected, 0, count_rows, axis=2)
    imag_cols = lax.dynamic_slice_in_dim(selected, half_width, count_rows, 2)
    left_side = jnp.concatenate([real_cols, imag_cols], axis=2)
    upper_half = jnp.concatenate([portion[:, 0], portion[:, 1]], axis=2)
    lower_half = jnp.concatenate([-portion[:, 1], portion[:, 0]], axis=2)
    right_side = jnp.concatenate([upper_half, lower_half], axis=1)
    state_rows = jnp.einsum(
        "arc,acw->rw", left_side, right_side, preferred_element_type=jnp.float32
    )
    state_rows = state_rows.astype(jnp.bfloat16).reshape(pieces, rows_piece, twice_width)
    named_by = jnp.sum(
        (routes[:, :, None] == lax.broadcasted_iota(jnp.int32, (pieces, listed, owners), 2)).astype(
            jnp.int32
        ),
        axis=1,
    )
    slot_rank = jnp.cumsum(named_by, axis=0) - named_by
    slot_hit = (
        slot_rank[:, :, None] == lax.broadcasted_iota(jnp.int32, (pieces, owners, slot_count), 2)
    ) & (named_by[:, :, None] > 0)
    dispatch = jnp.transpose(slot_hit, (1, 2, 0)).astype(jnp.bfloat16)
    outgoing = jnp.einsum(
        "dmi,irc->dmrc", dispatch, state_rows, preferred_element_type=jnp.float32
    ).astype(jnp.bfloat16)
    own_form = complex_form(suffix[0])
    cap_form = complex_form(cap)
    products = jnp.einsum(
        "smrc,cw->smrw",
        lax.all_to_all(outgoing, "bits", split_axis=0, concat_axis=0, tiled=True),
        own_form,
        preferred_element_type=jnp.float32,
    ).astype(jnp.bfloat16)
    capped_terms = jnp.einsum(
        "smrw,wv->smrv", products, cap_form, preferred_element_type=jnp.float32
    )
    returned = lax.all_to_all(
        capped_terms.astype(jnp.bfloat16), "bits", split_axis=0, concat_axis=0, tiled=True
    ).astype(capped_terms.dtype)
    return jnp.einsum(
        "dmi,dmrv->irv", dispatch.astype(jnp.float32), returned, precision=HIGHEST_PRECISION
    )


def on_device(*args):
    prefix, first_suffix, pair_prefix, routes, cap = args[0], args[1], args[2], args[6], args[7]
    owners = lax.axis_size("bits")
    planes = owners // PLANE
    depth, width = first_suffix.shape[2:]
    pieces, merges = pair_prefix.shape
    fits = (
        planes > 2
        and planes & (planes - 1) == 0
        and owners <= 256
        and width == owners * depth
        and width % (planes // 2 * LANES) == 0
        and width // 2 % LANES == 0
        and 2 * cap.shape[2] == LANES
        and depth % 16 == 0
        and LANES % depth == 0
        and depth % prefix.shape[1] == 0
        and prefix.shape[0] * prefix.shape[1] % depth == 0
        and prefix.shape[1] % 16 == 0
        and 2 * merges < HEAD
        and HEAD + pieces <= depth
        and max(pieces, routes.shape[1]) <= LANES
    )
    return in_planes(*args) if fits else by_owner(*args)


def solution(mesh):
    return jax.shard_map(
        on_device,
        mesh=mesh,
        in_specs=(
            P(("grp", "bits"), None, None),
            P("grp", None, "bits", None),
            P(("grp", "bits"), None),
            P(("grp", "bits"), None),
            P(("grp", "bits")),
            P(("grp", "bits"), None, None, None),
            P(("grp", "bits"), None),
            P(),
        ),
        out_specs=P(("grp", "bits"), None, None),
        check_vma=False,
    )
```

```python
import functools

import jax
import jax.numpy as jnp
from jax import lax
from jax.experimental import pallas as pl
from jax.experimental.pallas import tpu as pltpu
from jax.sharding import PartitionSpec as P

HIGHEST_PRECISION = lax.Precision.HIGHEST
LANES = 128
PLANE = 4
VMEM_BYTES = 32 * 1024 * 1024
PACK_BYTES = 60 * 1024 * 1024
HEAD = 8


def complex_form(blocks):
    real_part = blocks[..., 0, :, :]
    imag_part = blocks[..., 1, :, :]
    upper_half = jnp.concatenate([real_part, imag_part], axis=-1)
    lower_half = jnp.concatenate([-imag_part, real_part], axis=-1)
    return jnp.concatenate([upper_half, lower_half], axis=-2)


def swap(x, bit):
    owners = lax.axis_size("bits")
    return lax.ppermute(x, "bits", [(i, i ^ bit) for i in range(owners)])


def after(x, others):
    return lax.optimization_barrier((x, others))[0]


def pack_kernel(planes, *refs):
    sources, outs = refs[:8], refs[8:10 + planes]
    plan, closed, *copied, sems = refs[10 + planes:]
    suffix_ref, cap_ref, first_ref, prefix_ref, *numbers = copied
    pair_prefix_ref, pair_suffix_ref, count_ref, routes_ref = numbers
    plane = lax.axis_index("bits") // PLANE
    copies = [pltpu.make_async_copy(source, ref, sems.at[n]) for n, (source, ref) in enumerate(zip(sources, copied))]
    for copy in copies:
        copy.start()
    merges, pieces = pair_prefix_ref.shape
    plan[...] = jnp.zeros_like(plan)
    for copy in copies[4:]:
        copy.wait()
    plan[:merges, :pieces] = pair_prefix_ref[...]
    plan[merges:2 * merges, :pieces] = pair_suffix_ref[...]
    plan[2 * merges:2 * merges + 1, :pieces] = count_ref[...]
    lane = lax.broadcasted_iota(jnp.int32, (pieces, LANES), 1)
    named = jnp.zeros((pieces, LANES), jnp.int32)
    for owner in range(planes * PLANE):
        hits = jnp.sum((routes_ref[...] == owner).astype(jnp.int32), axis=1, keepdims=True)
        named = jnp.where(lane == owner, hits, named)
    plan[HEAD:HEAD + pieces, :] = named
    routing = plan[...].astype(jnp.float32).astype(jnp.bfloat16)
    blocks, _, depth, width = first_ref.shape
    part, span = width // 2, width // (planes // 2)
    held, rows_piece, twice_width = prefix_ref.shape
    per = depth // rows_piece
    firsts = 2 * blocks * (part // LANES)
    relayed = [(firsts if k < 2 else 0) + part // depth for k in range(planes)]
    lows = [plane % 2 ^ k % 2 for k in range(planes)]
    copies[2].wait()
    for k in range(2):
        n = 0
        for a in range(blocks):
            for c in range(2):
                for start in range(0, part, LANES):
                    columns = pl.ds(pl.multiple_of(lows[k] * part + start, LANES), LANES)
                    outs[k][n] = first_ref[a, c, :, columns]
                    n += 1
    copies[3].wait()
    for k in range(planes):
        high = plane // 2 ^ k // 2
        tail = [routing]
        for start in range(0, twice_width, width):
            for n in range(0, span, LANES):
                columns = pl.ds(pl.multiple_of(high * span + (start + n), LANES), LANES)
                for row in range(0, held, per):
                    tail.append(prefix_ref[row:row + per, :, columns].reshape(depth, LANES))
        for n, entry in enumerate(tail):
            if k < 2:
                outs[planes + k][n] = entry
            else:
                outs[k][relayed[k] + n] = entry
    copies[1].wait()
    upper = jnp.concatenate([cap_ref[0], cap_ref[1]], axis=0)
    lower = jnp.concatenate([-cap_ref[1], cap_ref[0]], axis=0)
    turned = (((1,), (1,)), ((), ()))
    copies[0].wait()
    both = lax.dot_general(suffix_ref[0], upper, turned, preferred_element_type=jnp.float32)
    both += lax.dot_general(suffix_ref[1], lower, turned, preferred_element_type=jnp.float32)
    closed[...] = both.astype(jnp.bfloat16)
    for k in range(planes):
        for n in range(part // depth):
            there = pl.ds(pl.multiple_of(lows[k] * part + n * depth, depth), depth)
            outs[k][relayed[k] - part // depth + n] = closed[there, :]


def own_kernel(*refs):
    count = len(refs) // 2
    for source, out in zip(refs[:count], refs[count:]):
        out[...] = source[...]


def own_copy(*arrays):
    vmem = pl.BlockSpec(memory_space=pltpu.VMEM)
    return pl.pallas_call(
        own_kernel,
        out_shape=[jax.ShapeDtypeStruct(a.shape, a.dtype) for a in arrays],
        in_specs=[vmem] * len(arrays),
        out_specs=[vmem] * len(arrays),
        compiler_params=pltpu.CompilerParams(vmem_limit_bytes=VMEM_BYTES),
        cost_estimate=pl.CostEstimate(flops=0, bytes_accessed=2 ** 12, transcendentals=0),
        name="own",
    )(*arrays)


def join_kernel(*refs):
    for k, ref in enumerate(refs[:-1]):
        refs[-1][k] = ref[:refs[-1].shape[1]]


def join(packs, size):
    vmem = pl.BlockSpec(memory_space=pltpu.VMEM)
    return pl.pallas_call(
        join_kernel,
        out_shape=jax.ShapeDtypeStruct((len(packs), size) + packs[0].shape[1:], packs[0].dtype),
        in_specs=[vmem] * len(packs),
        out_specs=vmem,
        compiler_params=pltpu.CompilerParams(vmem_limit_bytes=VMEM_BYTES),
        cost_estimate=pl.CostEstimate(flops=0, bytes_accessed=2 ** 12, transcendentals=0),
        name="join",
    )(*packs)


def state_kernel(planes, blocks, merges, pieces, rows_piece, held, *refs):
    relays, packs = refs[:2 * PLANE], refs[2 * PLANE:2 * PLANE + planes]
    state, named, plan_out, forms, products, plan, sem = refs[2 * PLANE + planes:]
    me = lax.axis_index("bits")
    depth = packs[0].shape[1]
    span, twice_part = forms.shape[1:]
    part = twice_part // 2
    locals_ = []
    rows = planes * held * rows_piece
    index = lax.broadcasted_iota(jnp.int32, (merges, LANES), 0)
    tail = 1 + 2 * (span // LANES) * (held * rows_piece // depth)
    for k in range(planes):
        first = packs[k].shape[0] - tail
        numbers = packs[k][first].astype(jnp.float32)
        named[k] = numbers[HEAD:HEAD + pieces]
        plan_out[k] = numbers.astype(jnp.int32)
        live = index < plan_out[k, 2 * merges:2 * merges + 1]
        picked = plan_out[k, merges:2 * merges] * rows + (plan_out[k, :merges] + k * held) * rows_piece
        plan_out[k, :merges] = jnp.where(live, picked, blocks * rows)
        locals_.append(packs[k].at[first + 1:first + tail])
    copy = pltpu.make_async_copy(plan_out, plan, sem)
    copy.start()
    for j in range(2 * PLANE):
        there = pl.ds(pl.multiple_of((me ^ j) % (2 * PLANE) * depth, depth), depth)
        for a in range(blocks):
            for n in range(twice_part // LANES):
                forms[a, there, n * LANES:(n + 1) * LANES] = relays[j][0, a * (twice_part // LANES) + n]
    chunks = held * rows_piece // depth
    left = []
    for c in range(2):
        for k in range(planes):
            columns = []
            for n in range(span // LANES):
                first = (c * (span // LANES) + n) * chunks
                columns.append(locals_[k][first:first + chunks].reshape(rows // planes, LANES))
            left.append(jnp.concatenate(columns, axis=1))
    left = jnp.concatenate(left, axis=0)
    products[blocks * rows:, :] = jnp.zeros((rows_piece, twice_part), jnp.float32)
    for a in range(blocks):
        both = jnp.dot(left, forms[a], preferred_element_type=jnp.float32)
        products[a * rows:(a + 1) * rows, :part] = both[:rows, :part] - both[rows:, part:]
        products[a * rows:(a + 1) * rows, part:] = both[:rows, part:] + both[rows:, :part]
    copy.wait()
    for i in range(planes * pieces):
        k, n = divmod(i, pieces)
        total = None
        for m in range(merges):
            term = products[pl.ds(pl.multiple_of(plan[k, m, n], rows_piece), rows_piece), :]
            total = term if total is None else total + term
        state[i * rows_piece:(i + 1) * rows_piece, :] = total.astype(jnp.bfloat16)


def close(first_slot, named, state, relays, sums, wide):
    me = lax.axis_index("bits")
    planes, pieces, _ = named.shape
    part = wide.shape[0] // 2
    rows_piece = state.shape[0] // (planes * pieces)
    lane = lax.broadcasted_iota(jnp.int32, (part, LANES), 1)
    slot = 0
    for unit in range(0, len(relays), PLANE):
        for k in range(relays[unit].shape[0]):
            for relay in relays[unit:unit + PLANE]:
                first = relay.shape[1] - part // relay.shape[2]
                real_rows = relay[k, first:].reshape(part, LANES)
                turned = pltpu.roll(real_rows.astype(jnp.float32), LANES // 2, 1)
                turned = jnp.where(lane < LANES // 2, -turned, turned)
                wide[:part, slot * LANES:(slot + 1) * LANES] = real_rows
                wide[part:, slot * LANES:(slot + 1) * LANES] = turned.astype(jnp.bfloat16)
                slot += 1
    for j in range(0, slot, 2):
        both = jnp.dot(state[...], wide[:, j * LANES:(j + 2) * LANES], preferred_element_type=jnp.float32)
        owner = (first_slot + j) ^ me
        for i in range(planes * pieces):
            k, n = divmod(i, pieces)
            here = slice(i * rows_piece, (i + 1) * rows_piece)
            add = both[here, :LANES] * named[k, n, owner] + both[here, LANES:] * named[k, n, owner ^ 1]
            sums[here, :] = add if first_slot + j == 0 else sums[here, :] + add


def close_first_kernel(named, state, *refs):
    close(0, named, state, refs[:-2], *refs[-2:])


def close_rest_kernel(planes, named, state, sums_in, *refs):
    relays, outs = refs[:PLANE], refs[PLANE:PLANE + planes]
    sums, wide = refs[PLANE + planes:]
    sums[...] = sums_in[...]
    close(2 * PLANE, named, state, relays, sums, wide)
    for out, start in zip(outs, range(0, sums.shape[0], sums.shape[0] // planes)):
        out[...] = sums[start:start + sums.shape[0] // planes, :].reshape(out.shape).astype(out.dtype)


def in_planes(prefix, first_suffix, pair_prefix, pair_suffix, merge_count, suffix, routes, cap):
    owners = lax.axis_size("bits")
    planes = owners // PLANE
    pieces, merges = pair_prefix.shape
    listed = routes.shape[1]
    held, rows_piece, twice_width = prefix.shape
    blocks, _, depth, width = first_suffix.shape
    part, span = width // 2, width // (planes // 2)
    vmem = pl.BlockSpec(memory_space=pltpu.VMEM)
    smem = pl.BlockSpec(memory_space=pltpu.SMEM)
    params = pltpu.CompilerParams(vmem_limit_bytes=VMEM_BYTES)
    forms_size, closed_size = 2 * blocks * (part // LANES), part // depth
    tail = 1 + 2 * (span // LANES) * (held * rows_piece // depth)
    sources = (
        suffix[0],
        jnp.swapaxes(cap, 1, 2),
        first_suffix,
        prefix,
        pair_prefix.T,
        pair_suffix.T,
        merge_count[None],
        routes,
    )
    sizes = [forms_size + closed_size] * 2 + [closed_size + tail] * (planes - 2) + [tail] * 2
    packs = pl.pallas_call(
        functools.partial(pack_kernel, planes),
        out_shape=[jax.ShapeDtypeStruct((size, depth, LANES), jnp.bfloat16) for size in sizes],
        in_specs=[pl.BlockSpec(memory_space=pl.ANY)] * len(sources),
        out_specs=[vmem] * len(sizes),
        scratch_shapes=[pltpu.VMEM((depth, LANES), jnp.int32), pltpu.VMEM((width, LANES), jnp.bfloat16)]
        + [pltpu.VMEM(source.shape, source.dtype) for source in sources]
        + [pltpu.SemaphoreType.DMA((len(sources),))],
        compiler_params=pltpu.CompilerParams(vmem_limit_bytes=PACK_BYTES),
        cost_estimate=pl.CostEstimate(flops=2 ** 20, bytes_accessed=2 ** 12, transcendentals=0),
        name="pack",
    )(*sources)
    far = [swap(packs[k], k * PLANE) for k in range(2, planes)]
    near = swap(packs[planes + 1], PLANE)
    relays = [packs[0][None], swap(packs[1], PLANE)[None], join([after(far[0], near)] + far[1:], closed_size)]
    across = [swap(r, 2) for r in relays]
    own, local = own_copy(relays[0], packs[planes])
    relays[0] = own
    packs = [local, near] + far
    beside = [swap(r, 1) for r in relays]
    corner = [swap(across[0], 1), swap(after(across[1], beside[2]), 1)]
    rows = planes * pieces * rows_piece
    state, named = pl.pallas_call(
        functools.partial(state_kernel, planes, blocks, merges, pieces, rows_piece, held),
        out_shape=[
            jax.ShapeDtypeStruct((rows, 2 * part), jnp.bfloat16),
            jax.ShapeDtypeStruct((planes, pieces, LANES), jnp.float32),
        ],
        in_specs=[vmem] * (2 * PLANE + planes),
        out_specs=[vmem] * 2,
        scratch_shapes=[
            pltpu.VMEM((planes, depth, LANES), jnp.int32),
            pltpu.VMEM((blocks, span, 2 * part), jnp.bfloat16),
            pltpu.VMEM(((blocks * planes * held + 1) * rows_piece, 2 * part), jnp.float32),
            pltpu.SMEM((planes, depth, LANES), jnp.int32),
            pltpu.SemaphoreType.DMA,
        ],
        compiler_params=params,
        cost_estimate=pl.CostEstimate(flops=0, bytes_accessed=2 ** 12, transcendentals=0),
        name="state",
    )(*[group[n] for n in range(2) for group in (relays, beside, across, corner)], *packs)
    corner.append(swap(after(across[2], state), 1))
    relays = list(zip(relays, beside, across, corner))
    early = 2 * PLANE
    sums = pl.pallas_call(
        close_first_kernel,
        out_shape=jax.ShapeDtypeStruct((rows, LANES), jnp.float32),
        in_specs=[smem] + [vmem] * (1 + 2 * PLANE),
        out_specs=vmem,
        scratch_shapes=[pltpu.VMEM((2 * part, early * LANES), jnp.bfloat16)],
        compiler_params=params,
        name="close_first",
    )(named, state, *relays[0], *relays[1])
    sums = pl.pallas_call(
        functools.partial(close_rest_kernel, planes),
        out_shape=[
            jax.ShapeDtypeStruct((pieces, rows_piece, LANES), jnp.float32 if k == 0 else jnp.bfloat16)
            for k in range(planes)
        ],
        in_specs=[smem] + [vmem] * (2 + PLANE),
        out_specs=[vmem] * planes,
        scratch_shapes=[
            pltpu.VMEM((rows, LANES), jnp.float32),
            pltpu.VMEM((2 * part, (owners - early) * LANES), jnp.bfloat16),
        ],
        compiler_params=params,
        name="close_rest",
    )(named, state, sums, *relays[2])
    total = sums[0]
    for k in range(1, planes):
        total = total + swap(sums[k], k * PLANE).astype(jnp.float32)
    return total


def by_owner(prefix, first_suffix, pair_prefix, pair_suffix, merge_count, suffix, routes, cap):
    pieces = pair_prefix.shape[0]
    merges = pair_prefix.shape[1]
    held_blocks = prefix.shape[0]
    rows_piece = prefix.shape[1]
    twice_width = prefix.shape[2]
    half_width = twice_width // 2
    first_count = first_suffix.shape[0]
    listed = routes.shape[1]
    owners = lax.axis_size("bits")
    slot_count = min(pieces, max(2, (2 * pieces * listed + owners - 1) // owners))
    live_mask = lax.broadcasted_iota(jnp.int32, (pieces, merges), 1) < merge_count[:, None]
    matches = (
        pair_suffix[:, :, None] == lax.broadcasted_iota(jnp.int32, (pieces, merges, first_count), 2)
    ) & live_mask[:, :, None]
    which_block = pair_prefix[:, :, None] == lax.broadcasted_iota(
        jnp.int32, (pieces, merges, held_blocks), 2
    )
    prefix_picks = jnp.einsum(
        "ika,ikp->iap", matches.astype(jnp.float32), which_block.astype(jnp.float32)
    ).astype(jnp.bfloat16)
    selected = jnp.einsum(
        "iap,prc->airc", prefix_picks, prefix, preferred_element_type=jnp.float32
    ).astype(jnp.bfloat16)
    selected = selected.reshape(first_count, pieces * rows_piece, twice_width)
    portion = lax.all_gather(first_suffix, "bits", axis=2, tiled=True)
    count_rows = portion.shape[2]
    real_cols = lax.slice_in_dim(selected, 0, count_rows, axis=2)
    imag_cols = lax.dynamic_slice_in_dim(selected, half_width, count_rows, 2)
    left_side = jnp.concatenate([real_cols, imag_cols], axis=2)
    upper_half = jnp.concatenate([portion[:, 0], portion[:, 1]], axis=2)
    lower_half = jnp.concatenate([-portion[:, 1], portion[:, 0]], axis=2)
    right_side = jnp.concatenate([upper_half, lower_half], axis=1)
    state_rows = jnp.einsum(
        "arc,acw->rw", left_side, right_side, preferred_element_type=jnp.float32
    )
    state_rows = state_rows.astype(jnp.bfloat16).reshape(pieces, rows_piece, twice_width)
    named_by = jnp.sum(
        (routes[:, :, None] == lax.broadcasted_iota(jnp.int32, (pieces, listed, owners), 2)).astype(
            jnp.int32
        ),
        axis=1,
    )
    slot_rank = jnp.cumsum(named_by, axis=0) - named_by
    slot_hit = (
        slot_rank[:, :, None] == lax.broadcasted_iota(jnp.int32, (pieces, owners, slot_count), 2)
    ) & (named_by[:, :, None] > 0)
    dispatch = jnp.transpose(slot_hit, (1, 2, 0)).astype(jnp.bfloat16)
    outgoing = jnp.einsum(
        "dmi,irc->dmrc", dispatch, state_rows, preferred_element_type=jnp.float32
    ).astype(jnp.bfloat16)
    own_form = complex_form(suffix[0])
    cap_form = complex_form(cap)
    products = jnp.einsum(
        "smrc,cw->smrw",
        lax.all_to_all(outgoing, "bits", split_axis=0, concat_axis=0, tiled=True),
        own_form,
        preferred_element_type=jnp.float32,
    ).astype(jnp.bfloat16)
    capped_terms = jnp.einsum(
        "smrw,wv->smrv", products, cap_form, preferred_element_type=jnp.float32
    )
    returned = lax.all_to_all(
        capped_terms.astype(jnp.bfloat16), "bits", split_axis=0, concat_axis=0, tiled=True
    ).astype(capped_terms.dtype)
    return jnp.einsum(
        "dmi,dmrv->irv", dispatch.astype(jnp.float32), returned, precision=HIGHEST_PRECISION
    )


def on_device(*args):
    prefix, first_suffix, pair_prefix, routes, cap = args[0], args[1], args[2], args[6], args[7]
    owners = lax.axis_size("bits")
    planes = owners // PLANE
    depth, width = first_suffix.shape[2:]
    pieces, merges = pair_prefix.shape
    fits = (
        planes > 2
        and planes & (planes - 1) == 0
        and owners <= 256
        and width == owners * depth
        and width % (planes // 2 * LANES) == 0
        and width // 2 % LANES == 0
        and 2 * cap.shape[2] == LANES
        and depth % 16 == 0
        and LANES % depth == 0
        and depth % prefix.shape[1] == 0
        and prefix.shape[0] * prefix.shape[1] % depth == 0
        and prefix.shape[1] % 16 == 0
        and 2 * merges < HEAD
        and HEAD + pieces <= depth
        and max(pieces, owners) <= LANES
    )
    return in_planes(*args) if fits else by_owner(*args)


def solution(mesh):
    return jax.shard_map(
        on_device,
        mesh=mesh,
        in_specs=(
            P(("grp", "bits"), None, None),
            P("grp", None, "bits", None),
            P(("grp", "bits"), None),
            P(("grp", "bits"), None),
            P(("grp", "bits")),
            P(("grp", "bits"), None, None, None),
            P(("grp", "bits"), None),
            P(),
        ),
        out_specs=P(("grp", "bits"), None, None),
        check_vma=False,
    )
```

```python
import functools

import jax
import jax.numpy as jnp
from jax import lax
from jax.experimental import pallas as pl
from jax.experimental.pallas import tpu as pltpu
from jax.sharding import PartitionSpec as P

HIGHEST_PRECISION = lax.Precision.HIGHEST
LANES = 128
PLANE = 4
VMEM_BYTES = 32 * 1024 * 1024
PACK_BYTES = 60 * 1024 * 1024
HEAD = 8


def complex_form(blocks):
    real_part = blocks[..., 0, :, :]
    imag_part = blocks[..., 1, :, :]
    upper_half = jnp.concatenate([real_part, imag_part], axis=-1)
    lower_half = jnp.concatenate([-imag_part, real_part], axis=-1)
    return jnp.concatenate([upper_half, lower_half], axis=-2)


def swap(x, bit):
    owners = lax.axis_size("bits")
    return lax.ppermute(x, "bits", [(i, i ^ bit) for i in range(owners)])


def after(x, others):
    return lax.optimization_barrier((x, others))[0]


def pack_kernel(planes, *refs):
    sources, outs = refs[:8], refs[8:10 + planes]
    plan, closed, *copied, sems = refs[10 + planes:]
    suffix_ref, cap_ref, first_ref, prefix_ref, *numbers = copied
    pair_prefix_ref, pair_suffix_ref, count_ref, routes_ref = numbers
    plane = lax.axis_index("bits") // PLANE
    copies = [pltpu.make_async_copy(source, ref, sems.at[n]) for n, (source, ref) in enumerate(zip(sources, copied))]
    for copy in copies:
        copy.start()
    merges, pieces = pair_prefix_ref.shape
    plan[...] = jnp.zeros_like(plan)
    for copy in copies[4:]:
        copy.wait()
    plan[:merges, :pieces] = pair_prefix_ref[...]
    plan[merges:2 * merges, :pieces] = pair_suffix_ref[...]
    plan[2 * merges:2 * merges + 1, :pieces] = count_ref[...]
    me = lax.axis_index("bits")
    lane = lax.broadcasted_iota(jnp.int32, (pieces, LANES), 1)
    named = [jnp.zeros((pieces, LANES), jnp.int32)] * planes
    for slot in range(planes * PLANE):
        hits = jnp.sum((routes_ref[...] == slot ^ me).astype(jnp.int32), axis=1, keepdims=True)
        named = [jnp.where(lane == slot ^ k * PLANE, hits, there) for k, there in enumerate(named)]
    routing = []
    for k in range(planes):
        plan[HEAD:HEAD + pieces, :] = named[k]
        routing.append(plan[...].astype(jnp.float32).astype(jnp.bfloat16))
    blocks, _, depth, width = first_ref.shape
    part, span = width // 2, width // (planes // 2)
    held, rows_piece, twice_width = prefix_ref.shape
    per = depth // rows_piece
    firsts = 2 * blocks * (part // LANES)
    relayed = [(firsts if k < 2 else 0) + part // depth for k in range(planes)]
    lows = [plane % 2 ^ k % 2 for k in range(planes)]
    copies[2].wait()
    for k in range(2):
        n = 0
        for a in range(blocks):
            for c in range(2):
                for start in range(0, part, LANES):
                    columns = pl.ds(pl.multiple_of(lows[k] * part + start, LANES), LANES)
                    outs[k][n] = first_ref[a, c, :, columns]
                    n += 1
    copies[3].wait()
    for k in range(planes):
        high = plane // 2 ^ k // 2
        tail = [routing[k]]
        for start in range(0, twice_width, width):
            for n in range(0, span, LANES):
                columns = pl.ds(pl.multiple_of(high * span + (start + n), LANES), LANES)
                for row in range(0, held, per):
                    tail.append(prefix_ref[row:row + per, :, columns].reshape(depth, LANES))
        for n, entry in enumerate(tail):
            if k < 2:
                outs[planes + k][n] = entry
            else:
                outs[k][relayed[k] + n] = entry
    copies[1].wait()
    upper = jnp.concatenate([cap_ref[0], cap_ref[1]], axis=0)
    lower = jnp.concatenate([-cap_ref[1], cap_ref[0]], axis=0)
    turned = (((1,), (1,)), ((), ()))
    copies[0].wait()
    both = lax.dot_general(suffix_ref[0], upper, turned, preferred_element_type=jnp.float32)
    both += lax.dot_general(suffix_ref[1], lower, turned, preferred_element_type=jnp.float32)
    closed[...] = both.astype(jnp.bfloat16)
    for k in range(planes):
        for n in range(part // depth):
            there = pl.ds(pl.multiple_of(lows[k] * part + n * depth, depth), depth)
            outs[k][relayed[k] - part // depth + n] = closed[there, :]


def own_kernel(*refs):
    count = len(refs) // 2
    for source, out in zip(refs[:count], refs[count:]):
        out[...] = source[...]


def own_copy(*arrays):
    vmem = pl.BlockSpec(memory_space=pltpu.VMEM)
    return pl.pallas_call(
        own_kernel,
        out_shape=[jax.ShapeDtypeStruct(a.shape, a.dtype) for a in arrays],
        in_specs=[vmem] * len(arrays),
        out_specs=[vmem] * len(arrays),
        compiler_params=pltpu.CompilerParams(vmem_limit_bytes=VMEM_BYTES),
        cost_estimate=pl.CostEstimate(flops=0, bytes_accessed=2 ** 12, transcendentals=0),
        name="own",
    )(*arrays)


def join_kernel(*refs):
    for k, ref in enumerate(refs[:-1]):
        refs[-1][k] = ref[:refs[-1].shape[1]]


def join(packs, size):
    vmem = pl.BlockSpec(memory_space=pltpu.VMEM)
    return pl.pallas_call(
        join_kernel,
        out_shape=jax.ShapeDtypeStruct((len(packs), size) + packs[0].shape[1:], packs[0].dtype),
        in_specs=[vmem] * len(packs),
        out_specs=vmem,
        compiler_params=pltpu.CompilerParams(vmem_limit_bytes=VMEM_BYTES),
        cost_estimate=pl.CostEstimate(flops=0, bytes_accessed=2 ** 12, transcendentals=0),
        name="join",
    )(*packs)


def state_kernel(planes, blocks, merges, pieces, rows_piece, held, *refs):
    relays, packs = refs[:2 * PLANE], refs[2 * PLANE:2 * PLANE + planes]
    state, named, plan_out, forms, products, plan, sem = refs[2 * PLANE + planes:]
    me = lax.axis_index("bits")
    depth = packs[0].shape[1]
    span, twice_part = forms.shape[1:]
    part = twice_part // 2
    locals_ = []
    rows = planes * held * rows_piece
    index = lax.broadcasted_iota(jnp.int32, (merges, LANES), 0)
    tail = 1 + 2 * (span // LANES) * (held * rows_piece // depth)
    for k in range(planes):
        first = packs[k].shape[0] - tail
        numbers = packs[k][first].astype(jnp.float32)
        for n in range(pieces):
            here = slice((k * pieces + n) * rows_piece, (k * pieces + n + 1) * rows_piece)
            named[here, :] = jnp.broadcast_to(numbers[HEAD + n:HEAD + n + 1], (rows_piece, LANES))
        plan_out[k] = numbers.astype(jnp.int32)
        live = index < plan_out[k, 2 * merges:2 * merges + 1]
        picked = plan_out[k, merges:2 * merges] * rows + (plan_out[k, :merges] + k * held) * rows_piece
        plan_out[k, :merges] = jnp.where(live, picked, blocks * rows)
        locals_.append(packs[k].at[first + 1:first + tail])
    copy = pltpu.make_async_copy(plan_out, plan, sem)
    copy.start()
    for j in range(2 * PLANE):
        there = pl.ds(pl.multiple_of((me ^ j) % (2 * PLANE) * depth, depth), depth)
        for a in range(blocks):
            for n in range(twice_part // LANES):
                forms[a, there, n * LANES:(n + 1) * LANES] = relays[j][0, a * (twice_part // LANES) + n]
    chunks = held * rows_piece // depth
    left = []
    for c in range(2):
        for k in range(planes):
            columns = []
            for n in range(span // LANES):
                first = (c * (span // LANES) + n) * chunks
                columns.append(locals_[k][first:first + chunks].reshape(rows // planes, LANES))
            left.append(jnp.concatenate(columns, axis=1))
    left = jnp.concatenate(left, axis=0)
    products[blocks * rows:, :] = jnp.zeros((rows_piece, twice_part), jnp.float32)
    for a in range(blocks):
        both = jnp.dot(left, forms[a], preferred_element_type=jnp.float32)
        products[a * rows:(a + 1) * rows, :part] = both[:rows, :part] - both[rows:, part:]
        products[a * rows:(a + 1) * rows, part:] = both[:rows, part:] + both[rows:, :part]
    copy.wait()
    for i in range(planes * pieces):
        k, n = divmod(i, pieces)
        total = None
        for m in range(merges):
            term = products[pl.ds(pl.multiple_of(plan[k, m, n], rows_piece), rows_piece), :]
            total = term if total is None else total + term
        state[i * rows_piece:(i + 1) * rows_piece, :] = total.astype(jnp.bfloat16)


def close(order, named, state, relays, sums, wide):
    part, rows = wide.shape[0] // 2, state.shape[0]
    lane = lax.broadcasted_iota(jnp.int32, (part, LANES), 1)
    slot = 0
    for relay in relays:
        for k in range(relay.shape[0]):
            first = relay.shape[1] - part // relay.shape[2]
            real_rows = relay[k, first:].reshape(part, LANES)
            turned = pltpu.roll(real_rows.astype(jnp.float32), LANES // 2, 1)
            turned = jnp.where(lane < LANES // 2, -turned, turned)
            wide[:part, slot * LANES:(slot + 1) * LANES] = real_rows
            wide[part:, slot * LANES:(slot + 1) * LANES] = turned.astype(jnp.bfloat16)
            slot += 1
    for j in range(0, slot, 2):
        both = jnp.dot(state[...], wide[:, j * LANES:(j + 2) * LANES], preferred_element_type=jnp.float32)
        for side, slot in enumerate(order[j:j + 2]):
            factor = jnp.broadcast_to(named[:, slot:slot + 1], (rows, LANES))
            add = both[:, side * LANES:(side + 1) * LANES] * factor
            sums[...] = add if slot == 0 else sums[...] + add


def close_first_kernel(named, state, *refs):
    close(range(2 * PLANE), named, state, refs[:-2], *refs[-2:])


def close_more_kernel(order, named, state, sums_in, *refs):
    relays, sums, wide = refs[:-2], refs[-2], refs[-1]
    sums[...] = sums_in[...]
    close(order, named, state, relays, sums, wide)


def close_last_kernel(planes, order, named, state, sums_in, relay, *refs):
    outs, sums, wide = refs[:planes], refs[planes], refs[planes + 1]
    sums[...] = sums_in[...]
    close(order, named, state, [relay], sums, wide)
    for out, start in zip(outs, range(0, sums.shape[0], sums.shape[0] // planes)):
        out[...] = sums[start:start + sums.shape[0] // planes, :].reshape(out.shape).astype(out.dtype)


def in_planes(prefix, first_suffix, pair_prefix, pair_suffix, merge_count, suffix, routes, cap):
    owners = lax.axis_size("bits")
    planes = owners // PLANE
    pieces, merges = pair_prefix.shape
    listed = routes.shape[1]
    held, rows_piece, twice_width = prefix.shape
    blocks, _, depth, width = first_suffix.shape
    part, span = width // 2, width // (planes // 2)
    vmem = pl.BlockSpec(memory_space=pltpu.VMEM)
    params = pltpu.CompilerParams(vmem_limit_bytes=VMEM_BYTES)
    forms_size, closed_size = 2 * blocks * (part // LANES), part // depth
    tail = 1 + 2 * (span // LANES) * (held * rows_piece // depth)
    sources = (
        suffix[0],
        jnp.swapaxes(cap, 1, 2),
        first_suffix,
        prefix,
        pair_prefix.T,
        pair_suffix.T,
        merge_count[None],
        routes,
    )
    sizes = [forms_size + closed_size] * 2 + [closed_size + tail] * (planes - 2) + [tail] * 2
    packs = pl.pallas_call(
        functools.partial(pack_kernel, planes),
        out_shape=[jax.ShapeDtypeStruct((size, depth, LANES), jnp.bfloat16) for size in sizes],
        in_specs=[pl.BlockSpec(memory_space=pl.ANY)] * len(sources),
        out_specs=[vmem] * len(sizes),
        scratch_shapes=[pltpu.VMEM((depth, LANES), jnp.int32), pltpu.VMEM((width, LANES), jnp.bfloat16)]
        + [pltpu.VMEM(source.shape, source.dtype) for source in sources]
        + [pltpu.SemaphoreType.DMA((len(sources),))],
        compiler_params=pltpu.CompilerParams(vmem_limit_bytes=PACK_BYTES),
        cost_estimate=pl.CostEstimate(flops=2 ** 20, bytes_accessed=2 ** 12, transcendentals=0),
        name="pack",
    )(*sources)
    far = [swap(packs[k], k * PLANE) for k in range(2, planes)]
    near = swap(packs[planes + 1], PLANE)
    relays = [packs[0][None], swap(packs[1], PLANE)[None], join([after(far[0], near)] + far[1:], closed_size)]
    own, local = own_copy(relays[0], packs[planes])
    across = [swap(r, 2) for r in relays[:2]]
    relays[0] = own
    packs = [local, near] + far
    beside = [swap(r, 1) for r in relays]
    corner = [swap(y, 1) for y in across]
    across.append(swap(relays[2], 2))
    rows = planes * pieces * rows_piece
    state, named = pl.pallas_call(
        functools.partial(state_kernel, planes, blocks, merges, pieces, rows_piece, held),
        out_shape=[
            jax.ShapeDtypeStruct((rows, 2 * part), jnp.bfloat16),
            jax.ShapeDtypeStruct((rows, LANES), jnp.float32),
        ],
        in_specs=[vmem] * (2 * PLANE + planes),
        out_specs=[vmem] * 2,
        scratch_shapes=[
            pltpu.VMEM((planes, depth, LANES), jnp.int32),
            pltpu.VMEM((blocks, span, 2 * part), jnp.bfloat16),
            pltpu.VMEM(((blocks * planes * held + 1) * rows_piece, 2 * part), jnp.float32),
            pltpu.SMEM((planes, depth, LANES), jnp.int32),
            pltpu.SemaphoreType.DMA,
        ],
        compiler_params=params,
        cost_estimate=pl.CostEstimate(flops=0, bytes_accessed=2 ** 12, transcendentals=0),
        name="state",
    )(*[group[n] for n in range(2) for group in (relays, beside, across, corner)], *packs)
    early = 2 * PLANE
    tiny = pl.CostEstimate(flops=0, bytes_accessed=2 ** 12, transcendentals=0)
    sums = pl.pallas_call(
        close_first_kernel,
        out_shape=jax.ShapeDtypeStruct((rows, LANES), jnp.float32),
        in_specs=[vmem] * (2 + early),
        out_specs=vmem,
        scratch_shapes=[pltpu.VMEM((2 * part, early * LANES), jnp.bfloat16)],
        compiler_params=params,
        cost_estimate=tiny,
        name="close_first",
    )(named, state, *[group[n] for n in range(2) for group in (relays, beside, across, corner)])
    corner.append(swap(across[2], 1))
    far_slots = range(early, owners, PLANE)
    order = [k + n for n in (0, 1, 2) for k in far_slots]
    sums = pl.pallas_call(
        functools.partial(close_more_kernel, order),
        out_shape=jax.ShapeDtypeStruct((rows, LANES), jnp.float32),
        in_specs=[vmem] * (3 + 3),
        out_specs=vmem,
        scratch_shapes=[pltpu.VMEM((2 * part, len(order) * LANES), jnp.bfloat16)],
        compiler_params=params,
        name="close_more",
    )(named, state, sums, relays[2], beside[2], across[2])
    order = [k + 3 for k in far_slots]
    sums = pl.pallas_call(
        functools.partial(close_last_kernel, planes, order),
        out_shape=[
            jax.ShapeDtypeStruct((pieces, rows_piece, LANES), jnp.float32 if k == 0 else jnp.bfloat16)
            for k in range(planes)
        ],
        in_specs=[vmem] * 4,
        out_specs=[vmem] * planes,
        scratch_shapes=[
            pltpu.VMEM((rows, LANES), jnp.float32),
            pltpu.VMEM((2 * part, len(order) * LANES), jnp.bfloat16),
        ],
        compiler_params=params,
        name="close_last",
    )(named, state, sums, corner[2])
    total = sums[0]
    for k in range(1, planes):
        total = total + swap(sums[k], k * PLANE).astype(jnp.float32)
    return total


def by_owner(prefix, first_suffix, pair_prefix, pair_suffix, merge_count, suffix, routes, cap):
    pieces = pair_prefix.shape[0]
    merges = pair_prefix.shape[1]
    held_blocks = prefix.shape[0]
    rows_piece = prefix.shape[1]
    twice_width = prefix.shape[2]
    half_width = twice_width // 2
    first_count = first_suffix.shape[0]
    listed = routes.shape[1]
    owners = lax.axis_size("bits")
    slot_count = min(pieces, max(2, (2 * pieces * listed + owners - 1) // owners))
    live_mask = lax.broadcasted_iota(jnp.int32, (pieces, merges), 1) < merge_count[:, None]
    matches = (
        pair_suffix[:, :, None] == lax.broadcasted_iota(jnp.int32, (pieces, merges, first_count), 2)
    ) & live_mask[:, :, None]
    which_block = pair_prefix[:, :, None] == lax.broadcasted_iota(
        jnp.int32, (pieces, merges, held_blocks), 2
    )
    prefix_picks = jnp.einsum(
        "ika,ikp->iap", matches.astype(jnp.float32), which_block.astype(jnp.float32)
    ).astype(jnp.bfloat16)
    selected = jnp.einsum(
        "iap,prc->airc", prefix_picks, prefix, preferred_element_type=jnp.float32
    ).astype(jnp.bfloat16)
    selected = selected.reshape(first_count, pieces * rows_piece, twice_width)
    portion = lax.all_gather(first_suffix, "bits", axis=2, tiled=True)
    count_rows = portion.shape[2]
    real_cols = lax.slice_in_dim(selected, 0, count_rows, axis=2)
    imag_cols = lax.dynamic_slice_in_dim(selected, half_width, count_rows, 2)
    left_side = jnp.concatenate([real_cols, imag_cols], axis=2)
    upper_half = jnp.concatenate([portion[:, 0], portion[:, 1]], axis=2)
    lower_half = jnp.concatenate([-portion[:, 1], portion[:, 0]], axis=2)
    right_side = jnp.concatenate([upper_half, lower_half], axis=1)
    state_rows = jnp.einsum(
        "arc,acw->rw", left_side, right_side, preferred_element_type=jnp.float32
    )
    state_rows = state_rows.astype(jnp.bfloat16).reshape(pieces, rows_piece, twice_width)
    named_by = jnp.sum(
        (routes[:, :, None] == lax.broadcasted_iota(jnp.int32, (pieces, listed, owners), 2)).astype(
            jnp.int32
        ),
        axis=1,
    )
    slot_rank = jnp.cumsum(named_by, axis=0) - named_by
    slot_hit = (
        slot_rank[:, :, None] == lax.broadcasted_iota(jnp.int32, (pieces, owners, slot_count), 2)
    ) & (named_by[:, :, None] > 0)
    dispatch = jnp.transpose(slot_hit, (1, 2, 0)).astype(jnp.bfloat16)
    outgoing = jnp.einsum(
        "dmi,irc->dmrc", dispatch, state_rows, preferred_element_type=jnp.float32
    ).astype(jnp.bfloat16)
    own_form = complex_form(suffix[0])
    cap_form = complex_form(cap)
    products = jnp.einsum(
        "smrc,cw->smrw",
        lax.all_to_all(outgoing, "bits", split_axis=0, concat_axis=0, tiled=True),
        own_form,
        preferred_element_type=jnp.float32,
    ).astype(jnp.bfloat16)
    capped_terms = jnp.einsum(
        "smrw,wv->smrv", products, cap_form, preferred_element_type=jnp.float32
    )
    returned = lax.all_to_all(
        capped_terms.astype(jnp.bfloat16), "bits", split_axis=0, concat_axis=0, tiled=True
    ).astype(capped_terms.dtype)
    return jnp.einsum(
        "dmi,dmrv->irv", dispatch.astype(jnp.float32), returned, precision=HIGHEST_PRECISION
    )


def on_device(*args):
    prefix, first_suffix, pair_prefix, routes, cap = args[0], args[1], args[2], args[6], args[7]
    owners = lax.axis_size("bits")
    planes = owners // PLANE
    depth, width = first_suffix.shape[2:]
    pieces, merges = pair_prefix.shape
    fits = (
        planes > 2
        and planes & (planes - 1) == 0
        and owners <= 256
        and width == owners * depth
        and width % (planes // 2 * LANES) == 0
        and width // 2 % LANES == 0
        and 2 * cap.shape[2] == LANES
        and depth % 16 == 0
        and LANES % depth == 0
        and depth % prefix.shape[1] == 0
        and prefix.shape[0] * prefix.shape[1] % depth == 0
        and prefix.shape[1] % 16 == 0
        and 2 * merges < HEAD
        and HEAD + pieces <= depth
        and max(pieces, owners) <= LANES
    )
    return in_planes(*args) if fits else by_owner(*args)


def solution(mesh):
    return jax.shard_map(
        on_device,
        mesh=mesh,
        in_specs=(
            P(("grp", "bits"), None, None),
            P("grp", None, "bits", None),
            P(("grp", "bits"), None),
            P(("grp", "bits"), None),
            P(("grp", "bits")),
            P(("grp", "bits"), None, None, None),
            P(("grp", "bits"), None),
            P(),
        ),
        out_specs=P(("grp", "bits"), None, None),
        check_vma=False,
    )
```

```python
import functools

import jax
import jax.numpy as jnp
from jax import lax
from jax.experimental import pallas as pl
from jax.experimental.pallas import tpu as pltpu
from jax.sharding import PartitionSpec as P

HIGHEST_PRECISION = lax.Precision.HIGHEST
LANES = 128
PLANE = 4
VMEM_BYTES = 32 * 1024 * 1024
PACK_BYTES = 60 * 1024 * 1024


def complex_form(blocks):
    real_part = blocks[..., 0, :, :]
    imag_part = blocks[..., 1, :, :]
    upper_half = jnp.concatenate([real_part, imag_part], axis=-1)
    lower_half = jnp.concatenate([-imag_part, real_part], axis=-1)
    return jnp.concatenate([upper_half, lower_half], axis=-2)


def swap(x, bit):
    owners = lax.axis_size("bits")
    return lax.ppermute(x, "bits", [(i, i ^ bit) for i in range(owners)])


def after(x, others):
    return lax.optimization_barrier((x, others))[0]


def pack_kernel(planes, *refs):
    sources, outs = refs[:8], refs[8:10 + planes]
    plan, closed, *copied, sems = refs[10 + planes:]
    suffix_ref, cap_ref, first_ref, prefix_ref, *numbers = copied
    pair_prefix_ref, pair_suffix_ref, count_ref, routes_ref = numbers
    plane = lax.axis_index("bits") // PLANE
    copies = [pltpu.make_async_copy(source, ref, sems.at[n]) for n, (source, ref) in enumerate(zip(sources, copied))]
    for copy in copies:
        copy.start()
    merges, pieces = pair_prefix_ref.shape
    blocks, held, slots = first_ref.shape[0], prefix_ref.shape[0], planes * PLANE
    for copy in copies[4:]:
        copy.wait()
    me = lax.axis_index("bits")
    lane = lax.broadcasted_iota(jnp.int32, (pieces, LANES), 1)
    named = [jnp.zeros((pieces, LANES), jnp.int32)] * planes
    for slot in range(slots):
        hits = jnp.sum((routes_ref[...] == slot ^ me).astype(jnp.int32), axis=1, keepdims=True)
        named = [jnp.where(lane == slot ^ k * PLANE, hits, there) for k, there in enumerate(named)]
    own_lane = lax.broadcasted_iota(jnp.int32, (pieces, pieces), 0) == lax.broadcasted_iota(jnp.int32, (pieces, pieces), 1)
    picks = jnp.zeros((pieces, LANES), jnp.int32)
    for m in range(merges):
        pick = pair_suffix_ref[m:m + 1, :] * held + pair_prefix_ref[m:m + 1, :]
        pick = jnp.where(m < count_ref[...], slots + pick, -1)
        pick = jnp.sum(jnp.where(own_lane, jnp.broadcast_to(pick, (pieces, pieces)), 0), axis=1, keepdims=True)
        picks += (lane == pick).astype(jnp.int32)
    plan[...] = jnp.zeros_like(plan)
    routing = []
    for k in range(planes):
        plan[:pieces, :] = (named[k] + picks).astype(jnp.float32)
        routing.append(plan[...].astype(jnp.bfloat16))
    blocks, _, depth, width = first_ref.shape
    part, span = width // 2, width // (planes // 2)
    rows_piece, twice_width = prefix_ref.shape[1:]
    per = depth // rows_piece
    firsts = 2 * blocks * (part // LANES)
    relayed = [(firsts if k < 2 else 0) + part // depth for k in range(planes)]
    lows = [plane % 2 ^ k % 2 for k in range(planes)]
    copies[2].wait()
    for k in range(2):
        n = 0
        for a in range(blocks):
            for c in range(2):
                for start in range(0, part, LANES):
                    columns = pl.ds(pl.multiple_of(lows[k] * part + start, LANES), LANES)
                    outs[k][n] = first_ref[a, c, :, columns]
                    n += 1
    copies[3].wait()
    for k in range(planes):
        high = plane // 2 ^ k // 2
        tail = [routing[k]]
        for start in range(0, twice_width, width):
            for n in range(0, span, LANES):
                columns = pl.ds(pl.multiple_of(high * span + (start + n), LANES), LANES)
                for row in range(0, held, per):
                    tail.append(prefix_ref[row:row + per, :, columns].reshape(depth, LANES))
        for n, entry in enumerate(tail):
            if k < 2:
                outs[planes + k][n] = entry
            else:
                outs[k][relayed[k] + n] = entry
    copies[1].wait()
    upper = jnp.concatenate([cap_ref[0], cap_ref[1]], axis=0)
    lower = jnp.concatenate([-cap_ref[1], cap_ref[0]], axis=0)
    turned = (((1,), (1,)), ((), ()))
    copies[0].wait()
    both = lax.dot_general(suffix_ref[0], upper, turned, preferred_element_type=jnp.float32)
    both += lax.dot_general(suffix_ref[1], lower, turned, preferred_element_type=jnp.float32)
    closed[...] = both.astype(jnp.bfloat16)
    for k in range(planes):
        for n in range(part // depth):
            there = pl.ds(pl.multiple_of(lows[k] * part + n * depth, depth), depth)
            outs[k][relayed[k] - part // depth + n] = closed[there, :]


def own_kernel(*refs):
    count = len(refs) // 2
    for source, out in zip(refs[:count], refs[count:]):
        out[...] = source[...]


def own_copy(*arrays):
    vmem = pl.BlockSpec(memory_space=pltpu.VMEM)
    return pl.pallas_call(
        own_kernel,
        out_shape=[jax.ShapeDtypeStruct(a.shape, a.dtype) for a in arrays],
        in_specs=[vmem] * len(arrays),
        out_specs=[vmem] * len(arrays),
        compiler_params=pltpu.CompilerParams(vmem_limit_bytes=VMEM_BYTES),
        cost_estimate=pl.CostEstimate(flops=0, bytes_accessed=2 ** 12, transcendentals=0),
        name="own",
    )(*arrays)


def join_kernel(*refs):
    for k, ref in enumerate(refs[:-1]):
        refs[-1][k] = ref[:refs[-1].shape[1]]


def join(packs, size):
    vmem = pl.BlockSpec(memory_space=pltpu.VMEM)
    return pl.pallas_call(
        join_kernel,
        out_shape=jax.ShapeDtypeStruct((len(packs), size) + packs[0].shape[1:], packs[0].dtype),
        in_specs=[vmem] * len(packs),
        out_specs=vmem,
        compiler_params=pltpu.CompilerParams(vmem_limit_bytes=VMEM_BYTES),
        cost_estimate=pl.CostEstimate(flops=0, bytes_accessed=2 ** 12, transcendentals=0),
        name="join",
    )(*packs)


def state_kernel(planes, blocks, pieces, rows_piece, held, *refs):
    relays, packs = refs[:2 * PLANE], refs[2 * PLANE:2 * PLANE + planes]
    state, named, forms, high, low = refs[2 * PLANE + planes:]
    me = lax.axis_index("bits")
    depth = packs[0].shape[1]
    span, twice_part = forms.shape[1:]
    part = twice_part // 2
    rows = held * rows_piece
    locals_ = []
    tail = 1 + 2 * (span // LANES) * (rows // depth)
    for k in range(planes):
        first = packs[k].shape[0] - tail
        numbers = packs[k][first].astype(jnp.float32)
        for n in range(pieces):
            here = slice((k * pieces + n) * rows_piece, (k * pieces + n + 1) * rows_piece)
            named[here, :] = jnp.broadcast_to(numbers[n:n + 1], (rows_piece, LANES))
        locals_.append(packs[k].at[first + 1:first + tail])
    wide = (LANES, blocks * rows)
    spread = lax.broadcasted_iota(jnp.int32, wide, 0) - planes * PLANE == lax.broadcasted_iota(jnp.int32, wide, 1) // rows_piece
    spread = spread.astype(jnp.float32).astype(jnp.bfloat16)
    wide = (planes * pieces * rows_piece, blocks * rows)
    same_row = lax.broadcasted_iota(jnp.int32, wide, 0) % rows_piece == lax.broadcasted_iota(jnp.int32, wide, 1) % rows_piece
    picks = jnp.dot(named[...].astype(jnp.bfloat16), spread, preferred_element_type=jnp.float32)
    picks = jnp.where(same_row, picks, 0.0).astype(jnp.bfloat16)
    for j in range(2 * PLANE):
        there = pl.ds(pl.multiple_of((me ^ j) % (2 * PLANE) * depth, depth), depth)
        for a in range(blocks):
            for n in range(twice_part // LANES):
                forms[a, there, n * LANES:(n + 1) * LANES] = relays[j][0, a * (twice_part // LANES) + n]
    chunks = rows // depth
    left = []
    for c in range(2):
        for k in range(planes):
            columns = []
            for n in range(span // LANES):
                first = (c * (span // LANES) + n) * chunks
                columns.append(locals_[k][first:first + chunks].reshape(rows, LANES))
            left.append(jnp.concatenate(columns, axis=1))
    left = jnp.concatenate(left, axis=0)
    for a in range(blocks):
        both = jnp.dot(left, forms[a], preferred_element_type=jnp.float32)
        real, imag = both[:planes * rows], both[planes * rows:]
        product = jnp.concatenate([real[:, :part] - imag[:, part:], real[:, part:] + imag[:, :part]], axis=1)
        rounded = product.astype(jnp.bfloat16)
        rest = (product - rounded.astype(jnp.float32)).astype(jnp.bfloat16)
        for k in range(planes):
            high[k, a * rows:(a + 1) * rows, :] = rounded[k * rows:(k + 1) * rows]
            low[k, a * rows:(a + 1) * rows, :] = rest[k * rows:(k + 1) * rows]
    size = pieces * rows_piece
    for k in range(planes):
        pick = picks[k * size:(k + 1) * size]
        total = jnp.dot(pick, high[k], preferred_element_type=jnp.float32)
        total += jnp.dot(pick, low[k], preferred_element_type=jnp.float32)
        state[k * size:(k + 1) * size, :] = total.astype(jnp.bfloat16)


def close(order, named, state, relays, sums, wide):
    part, rows = wide.shape[0] // 2, state.shape[0]
    lane = lax.broadcasted_iota(jnp.int32, (part, LANES), 1)
    slot = 0
    for relay in relays:
        for k in range(relay.shape[0]):
            first = relay.shape[1] - part // relay.shape[2]
            real_rows = relay[k, first:].reshape(part, LANES)
            turned = pltpu.roll(real_rows.astype(jnp.float32), LANES // 2, 1)
            turned = jnp.where(lane < LANES // 2, -turned, turned)
            wide[:part, slot * LANES:(slot + 1) * LANES] = real_rows
            wide[part:, slot * LANES:(slot + 1) * LANES] = turned.astype(jnp.bfloat16)
            slot += 1
    for j in range(0, slot, 2):
        both = jnp.dot(state[...], wide[:, j * LANES:(j + 2) * LANES], preferred_element_type=jnp.float32)
        for side, slot in enumerate(order[j:j + 2]):
            factor = jnp.broadcast_to(named[:, slot:slot + 1], (rows, LANES))
            add = both[:, side * LANES:(side + 1) * LANES] * factor
            sums[...] = add if slot == 0 else sums[...] + add


def close_first_kernel(named, state, *refs):
    close(range(2 * PLANE), named, state, refs[:-2], *refs[-2:])


def close_more_kernel(order, named, state, sums_in, *refs):
    relays, sums, wide = refs[:-2], refs[-2], refs[-1]
    sums[...] = sums_in[...]
    close(order, named, state, relays, sums, wide)


def close_last_kernel(planes, order, named, state, sums_in, relay, *refs):
    outs, sums, wide = refs[:planes], refs[planes], refs[planes + 1]
    sums[...] = sums_in[...]
    close(order, named, state, [relay], sums, wide)
    for out, start in zip(outs, range(0, sums.shape[0], sums.shape[0] // planes)):
        out[...] = sums[start:start + sums.shape[0] // planes, :].reshape(out.shape).astype(out.dtype)


def in_planes(prefix, first_suffix, pair_prefix, pair_suffix, merge_count, suffix, routes, cap):
    owners = lax.axis_size("bits")
    planes = owners // PLANE
    pieces, merges = pair_prefix.shape
    listed = routes.shape[1]
    held, rows_piece, twice_width = prefix.shape
    blocks, _, depth, width = first_suffix.shape
    part, span = width // 2, width // (planes // 2)
    vmem = pl.BlockSpec(memory_space=pltpu.VMEM)
    params = pltpu.CompilerParams(vmem_limit_bytes=VMEM_BYTES)
    forms_size, closed_size = 2 * blocks * (part // LANES), part // depth
    tail = 1 + 2 * (span // LANES) * (held * rows_piece // depth)
    sources = (
        suffix[0],
        jnp.swapaxes(cap, 1, 2),
        first_suffix,
        prefix,
        pair_prefix.T,
        pair_suffix.T,
        merge_count[None],
        routes,
    )
    sizes = [forms_size + closed_size] * 2 + [closed_size + tail] * (planes - 2) + [tail] * 2
    packs = pl.pallas_call(
        functools.partial(pack_kernel, planes),
        out_shape=[jax.ShapeDtypeStruct((size, depth, LANES), jnp.bfloat16) for size in sizes],
        in_specs=[pl.BlockSpec(memory_space=pl.ANY)] * len(sources),
        out_specs=[vmem] * len(sizes),
        scratch_shapes=[pltpu.VMEM((depth, LANES), jnp.float32), pltpu.VMEM((width, LANES), jnp.bfloat16)]
        + [pltpu.VMEM(source.shape, source.dtype) for source in sources]
        + [pltpu.SemaphoreType.DMA((len(sources),))],
        compiler_params=pltpu.CompilerParams(vmem_limit_bytes=PACK_BYTES),
        cost_estimate=pl.CostEstimate(flops=2 ** 20, bytes_accessed=2 ** 12, transcendentals=0),
        name="pack",
    )(*sources)
    far = [swap(packs[k], k * PLANE) for k in range(2, planes)]
    near = swap(packs[planes + 1], PLANE)
    relays = [packs[0][None], swap(packs[1], PLANE)[None], join([after(far[0], near)] + far[1:], closed_size)]
    own, local = own_copy(relays[0], packs[planes])
    across = [swap(r, 2) for r in relays[:2]]
    relays[0] = own
    packs = [local, near] + far
    beside = [swap(r, 1) for r in relays]
    corner = [swap(y, 1) for y in across]
    across.append(swap(relays[2], 2))
    rows = planes * pieces * rows_piece
    state, named = pl.pallas_call(
        functools.partial(state_kernel, planes, blocks, pieces, rows_piece, held),
        out_shape=[
            jax.ShapeDtypeStruct((rows, 2 * part), jnp.bfloat16),
            jax.ShapeDtypeStruct((rows, LANES), jnp.float32),
        ],
        in_specs=[vmem] * (2 * PLANE + planes),
        out_specs=[vmem] * 2,
        scratch_shapes=[
            pltpu.VMEM((blocks, span, 2 * part), jnp.bfloat16),
            pltpu.VMEM((planes, blocks * held * rows_piece, 2 * part), jnp.bfloat16),
            pltpu.VMEM((planes, blocks * held * rows_piece, 2 * part), jnp.bfloat16),
        ],
        compiler_params=params,
        cost_estimate=pl.CostEstimate(flops=0, bytes_accessed=2 ** 12, transcendentals=0),
        name="state",
    )(*[group[n] for n in range(2) for group in (relays, beside, across, corner)], *packs)
    early = 2 * PLANE
    tiny = pl.CostEstimate(flops=0, bytes_accessed=2 ** 12, transcendentals=0)
    sums = pl.pallas_call(
        close_first_kernel,
        out_shape=jax.ShapeDtypeStruct((rows, LANES), jnp.float32),
        in_specs=[vmem] * (2 + early),
        out_specs=vmem,
        scratch_shapes=[pltpu.VMEM((2 * part, early * LANES), jnp.bfloat16)],
        compiler_params=params,
        cost_estimate=tiny,
        name="close_first",
    )(named, state, *[group[n] for n in range(2) for group in (relays, beside, across, corner)])
    corner.append(swap(across[2], 1))
    far_slots = range(early, owners, PLANE)
    order = [k + n for n in (0, 1, 2) for k in far_slots]
    sums = pl.pallas_call(
        functools.partial(close_more_kernel, order),
        out_shape=jax.ShapeDtypeStruct((rows, LANES), jnp.float32),
        in_specs=[vmem] * (3 + 3),
        out_specs=vmem,
        scratch_shapes=[pltpu.VMEM((2 * part, len(order) * LANES), jnp.bfloat16)],
        compiler_params=params,
        name="close_more",
    )(named, state, sums, relays[2], beside[2], across[2])
    order = [k + 3 for k in far_slots]
    sums = pl.pallas_call(
        functools.partial(close_last_kernel, planes, order),
        out_shape=[
            jax.ShapeDtypeStruct((pieces, rows_piece, LANES), jnp.float32 if k == 0 else jnp.bfloat16)
            for k in range(planes)
        ],
        in_specs=[vmem] * 4,
        out_specs=[vmem] * planes,
        scratch_shapes=[
            pltpu.VMEM((rows, LANES), jnp.float32),
            pltpu.VMEM((2 * part, len(order) * LANES), jnp.bfloat16),
        ],
        compiler_params=params,
        name="close_last",
    )(named, state, sums, corner[2])
    total = sums[0]
    for k in range(1, planes):
        total = total + swap(sums[k], k * PLANE).astype(jnp.float32)
    return total


def by_owner(prefix, first_suffix, pair_prefix, pair_suffix, merge_count, suffix, routes, cap):
    pieces = pair_prefix.shape[0]
    merges = pair_prefix.shape[1]
    held_blocks = prefix.shape[0]
    rows_piece = prefix.shape[1]
    twice_width = prefix.shape[2]
    half_width = twice_width // 2
    first_count = first_suffix.shape[0]
    listed = routes.shape[1]
    owners = lax.axis_size("bits")
    slot_count = min(pieces, max(2, (2 * pieces * listed + owners - 1) // owners))
    live_mask = lax.broadcasted_iota(jnp.int32, (pieces, merges), 1) < merge_count[:, None]
    matches = (
        pair_suffix[:, :, None] == lax.broadcasted_iota(jnp.int32, (pieces, merges, first_count), 2)
    ) & live_mask[:, :, None]
    which_block = pair_prefix[:, :, None] == lax.broadcasted_iota(
        jnp.int32, (pieces, merges, held_blocks), 2
    )
    prefix_picks = jnp.einsum(
        "ika,ikp->iap", matches.astype(jnp.float32), which_block.astype(jnp.float32)
    ).astype(jnp.bfloat16)
    selected = jnp.einsum(
        "iap,prc->airc", prefix_picks, prefix, preferred_element_type=jnp.float32
    ).astype(jnp.bfloat16)
    selected = selected.reshape(first_count, pieces * rows_piece, twice_width)
    portion = lax.all_gather(first_suffix, "bits", axis=2, tiled=True)
    count_rows = portion.shape[2]
    real_cols = lax.slice_in_dim(selected, 0, count_rows, axis=2)
    imag_cols = lax.dynamic_slice_in_dim(selected, half_width, count_rows, 2)
    left_side = jnp.concatenate([real_cols, imag_cols], axis=2)
    upper_half = jnp.concatenate([portion[:, 0], portion[:, 1]], axis=2)
    lower_half = jnp.concatenate([-portion[:, 1], portion[:, 0]], axis=2)
    right_side = jnp.concatenate([upper_half, lower_half], axis=1)
    state_rows = jnp.einsum(
        "arc,acw->rw", left_side, right_side, preferred_element_type=jnp.float32
    )
    state_rows = state_rows.astype(jnp.bfloat16).reshape(pieces, rows_piece, twice_width)
    named_by = jnp.sum(
        (routes[:, :, None] == lax.broadcasted_iota(jnp.int32, (pieces, listed, owners), 2)).astype(
            jnp.int32
        ),
        axis=1,
    )
    slot_rank = jnp.cumsum(named_by, axis=0) - named_by
    slot_hit = (
        slot_rank[:, :, None] == lax.broadcasted_iota(jnp.int32, (pieces, owners, slot_count), 2)
    ) & (named_by[:, :, None] > 0)
    dispatch = jnp.transpose(slot_hit, (1, 2, 0)).astype(jnp.bfloat16)
    outgoing = jnp.einsum(
        "dmi,irc->dmrc", dispatch, state_rows, preferred_element_type=jnp.float32
    ).astype(jnp.bfloat16)
    own_form = complex_form(suffix[0])
    cap_form = complex_form(cap)
    products = jnp.einsum(
        "smrc,cw->smrw",
        lax.all_to_all(outgoing, "bits", split_axis=0, concat_axis=0, tiled=True),
        own_form,
        preferred_element_type=jnp.float32,
    ).astype(jnp.bfloat16)
    capped_terms = jnp.einsum(
        "smrw,wv->smrv", products, cap_form, preferred_element_type=jnp.float32
    )
    returned = lax.all_to_all(
        capped_terms.astype(jnp.bfloat16), "bits", split_axis=0, concat_axis=0, tiled=True
    ).astype(capped_terms.dtype)
    return jnp.einsum(
        "dmi,dmrv->irv", dispatch.astype(jnp.float32), returned, precision=HIGHEST_PRECISION
    )


def on_device(*args):
    prefix, first_suffix, pair_prefix, routes, cap = args[0], args[1], args[2], args[6], args[7]
    owners = lax.axis_size("bits")
    planes = owners // PLANE
    depth, width = first_suffix.shape[2:]
    pieces = pair_prefix.shape[0]
    fits = (
        planes > 2
        and planes & (planes - 1) == 0
        and owners <= 256
        and width == owners * depth
        and width % (planes // 2 * LANES) == 0
        and width // 2 % LANES == 0
        and 2 * cap.shape[2] == LANES
        and depth % 16 == 0
        and LANES % depth == 0
        and depth % prefix.shape[1] == 0
        and prefix.shape[0] * prefix.shape[1] % depth == 0
        and prefix.shape[1] % 16 == 0
        and pieces <= min(depth, LANES)
        and owners + first_suffix.shape[0] * prefix.shape[0] <= LANES
    )
    return in_planes(*args) if fits else by_owner(*args)


def solution(mesh):
    return jax.shard_map(
        on_device,
        mesh=mesh,
        in_specs=(
            P(("grp", "bits"), None, None),
            P("grp", None, "bits", None),
            P(("grp", "bits"), None),
            P(("grp", "bits"), None),
            P(("grp", "bits")),
            P(("grp", "bits"), None, None, None),
            P(("grp", "bits"), None),
            P(),
        ),
        out_specs=P(("grp", "bits"), None, None),
        check_vma=False,
    )
```

```python
import functools

import jax
import jax.numpy as jnp
from jax import lax
from jax.experimental import pallas as pl
from jax.experimental.pallas import tpu as pltpu
from jax.sharding import PartitionSpec as P

HIGHEST_PRECISION = lax.Precision.HIGHEST
LANES = 128
PLANE = 4
VMEM_BYTES = 32 * 1024 * 1024
PACK_BYTES = 60 * 1024 * 1024


def complex_form(blocks):
    real_part = blocks[..., 0, :, :]
    imag_part = blocks[..., 1, :, :]
    upper_half = jnp.concatenate([real_part, imag_part], axis=-1)
    lower_half = jnp.concatenate([-imag_part, real_part], axis=-1)
    return jnp.concatenate([upper_half, lower_half], axis=-2)


def swap(x, bit):
    owners = lax.axis_size("bits")
    return lax.ppermute(x, "bits", [(i, i ^ bit) for i in range(owners)])


def after(x, others):
    return lax.optimization_barrier((x, others))[0]


def pack_kernel(planes, *refs):
    sources, outs = refs[:8], refs[8:10 + planes]
    plan, closed, *copied, sems = refs[10 + planes:]
    suffix_ref, cap_ref, first_ref, prefix_ref, *numbers = copied
    pair_prefix_ref, pair_suffix_ref, count_ref, routes_ref = numbers
    plane = lax.axis_index("bits") // PLANE
    copies = [pltpu.make_async_copy(source, ref, sems.at[n]) for n, (source, ref) in enumerate(zip(sources, copied))]
    for copy in copies:
        copy.start()
    merges, pieces = pair_prefix_ref.shape
    blocks, held, slots = first_ref.shape[0], prefix_ref.shape[0], planes * PLANE
    for copy in copies[4:]:
        copy.wait()
    me = lax.axis_index("bits")
    lane = lax.broadcasted_iota(jnp.int32, (pieces, LANES), 1)
    named = [jnp.zeros((pieces, LANES), jnp.int32)] * planes
    for slot in range(slots):
        hits = jnp.sum((routes_ref[...] == slot ^ me).astype(jnp.int32), axis=1, keepdims=True)
        named = [jnp.where(lane == slot ^ k * PLANE, hits, there) for k, there in enumerate(named)]
    own_lane = lax.broadcasted_iota(jnp.int32, (pieces, pieces), 0) == lax.broadcasted_iota(jnp.int32, (pieces, pieces), 1)
    picks = jnp.zeros((pieces, LANES), jnp.int32)
    for m in range(merges):
        pick = pair_suffix_ref[m:m + 1, :] * held + pair_prefix_ref[m:m + 1, :]
        pick = jnp.where(m < count_ref[...], slots + pick, -1)
        pick = jnp.sum(jnp.where(own_lane, jnp.broadcast_to(pick, (pieces, pieces)), 0), axis=1, keepdims=True)
        picks += (lane == pick).astype(jnp.int32)
    plan[...] = jnp.zeros_like(plan)
    routing = []
    for k in range(planes):
        plan[:pieces, :] = (named[k] + picks).astype(jnp.float32)
        routing.append(plan[...].astype(jnp.bfloat16))
    blocks, _, depth, width = first_ref.shape
    part, span = width // 2, width // (planes // 2)
    rows_piece, twice_width = prefix_ref.shape[1:]
    per = depth // rows_piece
    firsts = 2 * blocks * (part // LANES)
    relayed = [(firsts if k < 2 else 0) + part // depth for k in range(planes)]
    lows = [plane % 2 ^ k % 2 for k in range(planes)]
    copies[2].wait()
    for k in range(2):
        n = 0
        for a in range(blocks):
            for c in range(2):
                for start in range(0, part, LANES):
                    columns = pl.ds(pl.multiple_of(lows[k] * part + start, LANES), LANES)
                    outs[k][n] = first_ref[a, c, :, columns]
                    n += 1
    copies[3].wait()
    for k in range(planes):
        high = plane // 2 ^ k // 2
        tail = [routing[k]]
        for start in range(0, twice_width, width):
            for n in range(0, span, LANES):
                columns = pl.ds(pl.multiple_of(high * span + (start + n), LANES), LANES)
                for row in range(0, held, per):
                    tail.append(prefix_ref[row:row + per, :, columns].reshape(depth, LANES))
        for n, entry in enumerate(tail):
            if k < 2:
                outs[planes + k][n] = entry
            else:
                outs[k][relayed[k] + n] = entry
    copies[1].wait()
    upper = jnp.concatenate([cap_ref[0], cap_ref[1]], axis=0)
    lower = jnp.concatenate([-cap_ref[1], cap_ref[0]], axis=0)
    turned = (((1,), (1,)), ((), ()))
    copies[0].wait()
    both = lax.dot_general(suffix_ref[0], upper, turned, preferred_element_type=jnp.float32)
    both += lax.dot_general(suffix_ref[1], lower, turned, preferred_element_type=jnp.float32)
    closed[...] = both.astype(jnp.bfloat16)
    for k in range(planes):
        for n in range(part // depth):
            there = pl.ds(pl.multiple_of(lows[k] * part + n * depth, depth), depth)
            outs[k][relayed[k] - part // depth + n] = closed[there, :]


def own_kernel(*refs):
    count = len(refs) // 2
    for source, out in zip(refs[:count], refs[count:]):
        out[...] = source[...]


def own_copy(*arrays):
    vmem = pl.BlockSpec(memory_space=pltpu.VMEM)
    return pl.pallas_call(
        own_kernel,
        out_shape=[jax.ShapeDtypeStruct(a.shape, a.dtype) for a in arrays],
        in_specs=[vmem] * len(arrays),
        out_specs=[vmem] * len(arrays),
        compiler_params=pltpu.CompilerParams(vmem_limit_bytes=VMEM_BYTES),
        cost_estimate=pl.CostEstimate(flops=0, bytes_accessed=2 ** 12, transcendentals=0),
        name="own",
    )(*arrays)


def join_kernel(*refs):
    for k, ref in enumerate(refs[:-1]):
        refs[-1][k] = ref[:refs[-1].shape[1]]


def join(packs, size):
    vmem = pl.BlockSpec(memory_space=pltpu.VMEM)
    return pl.pallas_call(
        join_kernel,
        out_shape=jax.ShapeDtypeStruct((len(packs), size) + packs[0].shape[1:], packs[0].dtype),
        in_specs=[vmem] * len(packs),
        out_specs=vmem,
        compiler_params=pltpu.CompilerParams(vmem_limit_bytes=VMEM_BYTES),
        cost_estimate=pl.CostEstimate(flops=0, bytes_accessed=2 ** 12, transcendentals=0),
        name="join",
    )(*packs)


def front_kernel(planes, slots, order, blocks, pieces, rows_piece, held, *refs):
    relays, packs = refs[:2 * PLANE], refs[2 * PLANE:2 * PLANE + planes]
    closing = refs[2 * PLANE + planes:-7]
    state, named, sums, forms, high, low, wide = refs[-7:]
    me = lax.axis_index("bits")
    depth = packs[0].shape[1]
    span, twice_part = forms.shape[1:]
    part = twice_part // 2
    rows = held * rows_piece
    locals_ = []
    tail = 1 + 2 * (span // LANES) * (rows // depth)
    for k in range(planes):
        first = packs[k].shape[0] - tail
        numbers = packs[k][first].astype(jnp.float32)
        for n in range(pieces):
            here = slice((k * pieces + n) * rows_piece, (k * pieces + n + 1) * rows_piece)
            named[here, :] = jnp.broadcast_to(numbers[n:n + 1], (rows_piece, LANES))
        locals_.append(packs[k].at[first + 1:first + tail])
    shape = (LANES, blocks * rows)
    spread = lax.broadcasted_iota(jnp.int32, shape, 0) - slots == lax.broadcasted_iota(jnp.int32, shape, 1) // rows_piece
    spread = spread.astype(jnp.float32).astype(jnp.bfloat16)
    shape = (planes * pieces * rows_piece, blocks * rows)
    same_row = lax.broadcasted_iota(jnp.int32, shape, 0) % rows_piece == lax.broadcasted_iota(jnp.int32, shape, 1) % rows_piece
    picks = jnp.dot(named[...].astype(jnp.bfloat16), spread, preferred_element_type=jnp.float32)
    picks = jnp.where(same_row, picks, 0.0).astype(jnp.bfloat16)
    for j in range(2 * PLANE):
        there = pl.ds(pl.multiple_of((me ^ j) % (2 * PLANE) * depth, depth), depth)
        for a in range(blocks):
            for n in range(twice_part // LANES):
                forms[a, there, n * LANES:(n + 1) * LANES] = relays[j][0, a * (twice_part // LANES) + n]
    chunks = rows // depth
    left = []
    for c in range(2):
        for k in range(planes):
            columns = []
            for n in range(span // LANES):
                first = (c * (span // LANES) + n) * chunks
                columns.append(locals_[k][first:first + chunks].reshape(rows, LANES))
            left.append(jnp.concatenate(columns, axis=1))
    left = jnp.concatenate(left, axis=0)
    for a in range(blocks):
        both = jnp.dot(left, forms[a], preferred_element_type=jnp.float32)
        real, imag = both[:planes * rows], both[planes * rows:]
        product = jnp.concatenate([real[:, :part] - imag[:, part:], real[:, part:] + imag[:, :part]], axis=1)
        rounded = product.astype(jnp.bfloat16)
        rest = (product - rounded.astype(jnp.float32)).astype(jnp.bfloat16)
        for k in range(planes):
            high[k, a * rows:(a + 1) * rows, :] = rounded[k * rows:(k + 1) * rows]
            low[k, a * rows:(a + 1) * rows, :] = rest[k * rows:(k + 1) * rows]
    size = pieces * rows_piece
    for k in range(planes):
        pick = picks[k * size:(k + 1) * size]
        total = jnp.dot(pick, high[k], preferred_element_type=jnp.float32)
        total += jnp.dot(pick, low[k], preferred_element_type=jnp.float32)
        state[k * size:(k + 1) * size, :] = total.astype(jnp.bfloat16)
    close(order, named, state, relays + closing, sums, wide)


def close(order, named, state, relays, sums, wide):
    part, rows = wide.shape[0] // 2, state.shape[0]
    lane = lax.broadcasted_iota(jnp.int32, (part, LANES), 1)
    slot = 0
    for relay in relays:
        for k in range(relay.shape[0]):
            first = relay.shape[1] - part // relay.shape[2]
            real_rows = relay[k, first:].reshape(part, LANES)
            turned = pltpu.roll(real_rows.astype(jnp.float32), LANES // 2, 1)
            turned = jnp.where(lane < LANES // 2, -turned, turned)
            wide[:part, slot * LANES:(slot + 1) * LANES] = real_rows
            wide[part:, slot * LANES:(slot + 1) * LANES] = turned.astype(jnp.bfloat16)
            slot += 1
    for j in range(0, slot, 2):
        both = jnp.dot(state[...], wide[:, j * LANES:(j + 2) * LANES], preferred_element_type=jnp.float32)
        for side, slot in enumerate(order[j:j + 2]):
            factor = jnp.broadcast_to(named[:, slot:slot + 1], (rows, LANES))
            add = both[:, side * LANES:(side + 1) * LANES] * factor
            sums[...] = add if slot == 0 else sums[...] + add


def last_kernel(order, named, state, sums_in, relay, *refs):
    *outs, sums, wide = refs
    sums[...] = sums_in[...]
    close(order, named, state, [relay], sums, wide)
    size = sums.shape[0] // len(outs)
    for k, out in enumerate(outs):
        out[...] = sums[k * size:(k + 1) * size, :].reshape(out.shape).astype(out.dtype)


def in_planes(prefix, first_suffix, pair_prefix, pair_suffix, merge_count, suffix, routes, cap):
    owners = lax.axis_size("bits")
    planes = owners // PLANE
    pieces = pair_prefix.shape[0]
    held, rows_piece, twice_width = prefix.shape
    blocks, _, depth, width = first_suffix.shape
    part, span = width // 2, width // (planes // 2)
    vmem = pl.BlockSpec(memory_space=pltpu.VMEM)
    params = pltpu.CompilerParams(vmem_limit_bytes=VMEM_BYTES)
    forms_size, closed_size = 2 * blocks * (part // LANES), part // depth
    tail = 1 + 2 * (span // LANES) * (held * rows_piece // depth)
    sources = (
        suffix[0],
        jnp.swapaxes(cap, 1, 2),
        first_suffix,
        prefix,
        pair_prefix.T,
        pair_suffix.T,
        merge_count[None],
        routes,
    )
    sizes = [forms_size + closed_size] * 2 + [closed_size + tail] * (planes - 2) + [tail] * 2
    packs = pl.pallas_call(
        functools.partial(pack_kernel, planes),
        out_shape=[jax.ShapeDtypeStruct((size, depth, LANES), jnp.bfloat16) for size in sizes],
        in_specs=[pl.BlockSpec(memory_space=pl.ANY)] * len(sources),
        out_specs=[vmem] * len(sizes),
        scratch_shapes=[pltpu.VMEM((depth, LANES), jnp.float32), pltpu.VMEM((width, LANES), jnp.bfloat16)]
        + [pltpu.VMEM(source.shape, source.dtype) for source in sources]
        + [pltpu.SemaphoreType.DMA((len(sources),))],
        compiler_params=pltpu.CompilerParams(vmem_limit_bytes=PACK_BYTES),
        cost_estimate=pl.CostEstimate(flops=2 ** 20, bytes_accessed=2 ** 12, transcendentals=0),
        name="pack",
    )(*sources)
    far = [swap(packs[k], k * PLANE) for k in range(2, planes)]
    near = swap(packs[planes + 1], PLANE)
    relays = [packs[0][None], swap(packs[1], PLANE)[None], join([after(far[0], near)] + far[1:], closed_size)]
    own, local = own_copy(relays[0], packs[planes])
    across = [swap(r, 2) for r in relays[:2]]
    relays[0] = own
    packs = [local, near] + far
    beside = [swap(r, 1) for r in relays]
    corner = [swap(y, 1) for y in across]
    across.append(swap(relays[2], 2))
    corner.append(swap(across[2], 1))
    early = 2 * PLANE
    far_slots = range(early, owners, PLANE)
    order = list(range(early)) + [k + n for n in (0, 1, 2) for k in far_slots]
    last = [k + 3 for k in far_slots]
    relays = [group[n] for n in range(2) for group in (relays, beside, across, corner)] + [relays[2], beside[2], across[2]]
    tiny = pl.CostEstimate(flops=0, bytes_accessed=2 ** 12, transcendentals=0)

    def sums_of(chosen, dtype):
        count = len(chosen)
        rows = count * pieces * rows_piece
        operands = relays[:early] + [packs[k] for k in chosen] + relays[early:]
        state, named, sums = pl.pallas_call(
            functools.partial(front_kernel, count, owners, order, blocks, pieces, rows_piece, held),
            out_shape=[
                jax.ShapeDtypeStruct((rows, 2 * part), jnp.bfloat16),
                jax.ShapeDtypeStruct((rows, LANES), jnp.float32),
                jax.ShapeDtypeStruct((rows, LANES), jnp.float32),
            ],
            in_specs=[vmem] * len(operands),
            out_specs=[vmem] * 3,
            scratch_shapes=[
                pltpu.VMEM((blocks, span, 2 * part), jnp.bfloat16),
                pltpu.VMEM((count, blocks * held * rows_piece, 2 * part), jnp.bfloat16),
                pltpu.VMEM((count, blocks * held * rows_piece, 2 * part), jnp.bfloat16),
                pltpu.VMEM((2 * part, len(order) * LANES), jnp.bfloat16),
            ],
            compiler_params=params,
            cost_estimate=tiny,
            name="front",
        )(*operands)
        return pl.pallas_call(
            functools.partial(last_kernel, last),
            out_shape=[jax.ShapeDtypeStruct((pieces, rows_piece, LANES), dtype)] * count,
            in_specs=[vmem] * 4,
            out_specs=[vmem] * count,
            scratch_shapes=[
                pltpu.VMEM((rows, LANES), jnp.float32),
                pltpu.VMEM((2 * part, len(last) * LANES), jnp.bfloat16),
            ],
            compiler_params=params,
            cost_estimate=tiny,
            name="last",
        )(named, state, sums, corner[2])

    sent = sums_of(range(1, planes), jnp.bfloat16)
    total = sums_of([0], jnp.float32)[0]
    for k in range(1, planes):
        total = total + swap(sent[k - 1], k * PLANE).astype(jnp.float32)
    return total


def by_owner(prefix, first_suffix, pair_prefix, pair_suffix, merge_count, suffix, routes, cap):
    pieces = pair_prefix.shape[0]
    merges = pair_prefix.shape[1]
    held_blocks = prefix.shape[0]
    rows_piece = prefix.shape[1]
    twice_width = prefix.shape[2]
    half_width = twice_width // 2
    first_count = first_suffix.shape[0]
    listed = routes.shape[1]
    owners = lax.axis_size("bits")
    slot_count = min(pieces, max(2, (2 * pieces * listed + owners - 1) // owners))
    live_mask = lax.broadcasted_iota(jnp.int32, (pieces, merges), 1) < merge_count[:, None]
    matches = (
        pair_suffix[:, :, None] == lax.broadcasted_iota(jnp.int32, (pieces, merges, first_count), 2)
    ) & live_mask[:, :, None]
    which_block = pair_prefix[:, :, None] == lax.broadcasted_iota(
        jnp.int32, (pieces, merges, held_blocks), 2
    )
    prefix_picks = jnp.einsum(
        "ika,ikp->iap", matches.astype(jnp.float32), which_block.astype(jnp.float32)
    ).astype(jnp.bfloat16)
    selected = jnp.einsum(
        "iap,prc->airc", prefix_picks, prefix, preferred_element_type=jnp.float32
    ).astype(jnp.bfloat16)
    selected = selected.reshape(first_count, pieces * rows_piece, twice_width)
    portion = lax.all_gather(first_suffix, "bits", axis=2, tiled=True)
    count_rows = portion.shape[2]
    real_cols = lax.slice_in_dim(selected, 0, count_rows, axis=2)
    imag_cols = lax.dynamic_slice_in_dim(selected, half_width, count_rows, 2)
    left_side = jnp.concatenate([real_cols, imag_cols], axis=2)
    upper_half = jnp.concatenate([portion[:, 0], portion[:, 1]], axis=2)
    lower_half = jnp.concatenate([-portion[:, 1], portion[:, 0]], axis=2)
    right_side = jnp.concatenate([upper_half, lower_half], axis=1)
    state_rows = jnp.einsum(
        "arc,acw->rw", left_side, right_side, preferred_element_type=jnp.float32
    )
    state_rows = state_rows.astype(jnp.bfloat16).reshape(pieces, rows_piece, twice_width)
    named_by = jnp.sum(
        (routes[:, :, None] == lax.broadcasted_iota(jnp.int32, (pieces, listed, owners), 2)).astype(
            jnp.int32
        ),
        axis=1,
    )
    slot_rank = jnp.cumsum(named_by, axis=0) - named_by
    slot_hit = (
        slot_rank[:, :, None] == lax.broadcasted_iota(jnp.int32, (pieces, owners, slot_count), 2)
    ) & (named_by[:, :, None] > 0)
    dispatch = jnp.transpose(slot_hit, (1, 2, 0)).astype(jnp.bfloat16)
    outgoing = jnp.einsum(
        "dmi,irc->dmrc", dispatch, state_rows, preferred_element_type=jnp.float32
    ).astype(jnp.bfloat16)
    own_form = complex_form(suffix[0])
    cap_form = complex_form(cap)
    products = jnp.einsum(
        "smrc,cw->smrw",
        lax.all_to_all(outgoing, "bits", split_axis=0, concat_axis=0, tiled=True),
        own_form,
        preferred_element_type=jnp.float32,
    ).astype(jnp.bfloat16)
    capped_terms = jnp.einsum(
        "smrw,wv->smrv", products, cap_form, preferred_element_type=jnp.float32
    )
    returned = lax.all_to_all(
        capped_terms.astype(jnp.bfloat16), "bits", split_axis=0, concat_axis=0, tiled=True
    ).astype(capped_terms.dtype)
    return jnp.einsum(
        "dmi,dmrv->irv", dispatch.astype(jnp.float32), returned, precision=HIGHEST_PRECISION
    )


def on_device(*args):
    prefix, first_suffix, pair_prefix, routes, cap = args[0], args[1], args[2], args[6], args[7]
    owners = lax.axis_size("bits")
    planes = owners // PLANE
    depth, width = first_suffix.shape[2:]
    pieces = pair_prefix.shape[0]
    fits = (
        planes > 2
        and planes & (planes - 1) == 0
        and owners <= 256
        and width == owners * depth
        and width % (planes // 2 * LANES) == 0
        and width // 2 % LANES == 0
        and 2 * cap.shape[2] == LANES
        and depth % 16 == 0
        and LANES % depth == 0
        and depth % prefix.shape[1] == 0
        and prefix.shape[0] * prefix.shape[1] % depth == 0
        and prefix.shape[1] % 16 == 0
        and pieces <= min(depth, LANES)
        and owners + first_suffix.shape[0] * prefix.shape[0] <= LANES
    )
    return in_planes(*args) if fits else by_owner(*args)


def solution(mesh):
    return jax.shard_map(
        on_device,
        mesh=mesh,
        in_specs=(
            P(("grp", "bits"), None, None),
            P("grp", None, "bits", None),
            P(("grp", "bits"), None),
            P(("grp", "bits"), None),
            P(("grp", "bits")),
            P(("grp", "bits"), None, None, None),
            P(("grp", "bits"), None),
            P(),
        ),
        out_specs=P(("grp", "bits"), None, None),
        check_vma=False,
    )
```

```python
import functools

import jax
import jax.numpy as jnp
from jax import lax
from jax.experimental import pallas as pl
from jax.experimental.pallas import tpu as pltpu
from jax.sharding import PartitionSpec as P

HIGHEST_PRECISION = lax.Precision.HIGHEST
LANES = 128
PLANE = 4
VMEM_BYTES = 32 * 1024 * 1024
HEAD = 16
PACK_BYTES = 60 * 1024 * 1024


def complex_form(blocks):
    real_part = blocks[..., 0, :, :]
    imag_part = blocks[..., 1, :, :]
    upper_half = jnp.concatenate([real_part, imag_part], axis=-1)
    lower_half = jnp.concatenate([-imag_part, real_part], axis=-1)
    return jnp.concatenate([upper_half, lower_half], axis=-2)


def swap(x, bit):
    owners = lax.axis_size("bits")
    return lax.ppermute(x, "bits", [(i, i ^ bit) for i in range(owners)])


def after(x, others):
    return lax.optimization_barrier((x, others))[0]


def pack_kernel(planes, merges, held, *refs):
    sources, outs, stages, copied = refs[:8], refs[8:10 + planes], refs[10 + planes:12 + 2 * planes], refs[12 + 2 * planes:-1]
    sems = refs[-1]
    first_ref, prefix_ref, suffix_ref, cap_ref, pair_prefix_ref, pair_suffix_ref, count_ref, routes_ref = copied
    width = suffix_ref.shape[1]
    rows, twice_width = prefix_ref.shape
    part, span, slots = width // 2, width // (planes // 2), planes * PLANE
    me = lax.axis_index("bits")
    plane = me // PLANE
    inward = [pltpu.make_async_copy(source, ref, sems.at[n]) for n, (source, ref) in enumerate(zip(sources, copied))]
    for copy in inward:
        copy.start()
    outward = []

    def send(k, row, size):
        there = pl.ds(row, size)
        sem = sems.at[len(sources) + len(outward)]
        outward.append(pltpu.make_async_copy(stages[k].at[there, :], outs[k].at[there, :], sem))
        outward[-1].start()

    lows = [plane % 2 ^ k % 2 for k in range(planes)]
    firsts = [first_ref.shape[0] * (part // LANES) if k < 2 else 0 for k in range(planes)]
    inward[0].wait()
    for k in range(2):
        for n in range(part // LANES):
            columns = pl.ds(pl.multiple_of(lows[k] * part + n * LANES, LANES), LANES)
            stages[k][n * first_ref.shape[0]:(n + 1) * first_ref.shape[0], :] = first_ref[:, columns]
        send(k, 0, firsts[k])
    for copy in inward[4:]:
        copy.wait()
    pieces = routes_ref.shape[0]
    lane = lax.broadcasted_iota(jnp.int32, (pieces, LANES), 1)
    named = [jnp.zeros((pieces, LANES), jnp.int32)] * planes
    for slot in range(slots):
        hits = jnp.sum((routes_ref[...] == slot ^ me).astype(jnp.int32), axis=1, keepdims=True)
        named = [jnp.where(lane == slot ^ k * PLANE, hits, there) for k, there in enumerate(named)]
    own_lane = lax.broadcasted_iota(jnp.int32, (pieces, pieces), 0) == lax.broadcasted_iota(jnp.int32, (pieces, pieces), 1)
    picks = jnp.zeros((pieces, LANES), jnp.int32)
    for m in range(merges):
        pick = pair_suffix_ref[m:m + 1, :] * held + pair_prefix_ref[m:m + 1, :]
        pick = jnp.where(m < count_ref[...], slots + pick, -1)
        pick = jnp.sum(jnp.where(own_lane, jnp.broadcast_to(pick, (pieces, pieces)), 0), axis=1, keepdims=True)
        picks += (lane == pick).astype(jnp.int32)
    inward[1].wait()
    for k in range(planes):
        message, start = (planes + k, 0) if k < 2 else (k, part)
        stage, high = stages[message], plane // 2 ^ k // 2
        rest = jnp.zeros((HEAD - pieces, LANES), jnp.float32)
        routing = jnp.concatenate([(named[k] + picks).astype(jnp.float32), rest], axis=0)
        stage[start:start + HEAD, :] = routing.astype(jnp.bfloat16)
        row = start + HEAD
        for side in range(0, twice_width, width):
            for n in range(0, span, LANES):
                columns = pl.ds(pl.multiple_of(high * span + (side + n), LANES), LANES)
                stage[row:row + rows, :] = prefix_ref[:, columns]
                row += rows
        send(message, start, row - start)
    inward[3].wait()
    upper = jnp.concatenate([cap_ref[0], cap_ref[1]], axis=0)
    lower = jnp.concatenate([-cap_ref[1], cap_ref[0]], axis=0)
    turned = (((1,), (1,)), ((), ()))
    inward[2].wait()
    for low in range(2):
        there = pl.ds(pl.multiple_of((plane % 2 ^ low) * part, part), part)
        both = lax.dot_general(suffix_ref[0, there, :], upper, turned, preferred_element_type=jnp.float32)
        both += lax.dot_general(suffix_ref[1, there, :], lower, turned, preferred_element_type=jnp.float32)
        both = both.astype(jnp.bfloat16)
        for k in range(low, planes, 2):
            stages[k][firsts[k]:firsts[k] + part, :] = both
            send(k, firsts[k], part)
    for copy in outward:
        copy.wait()


def own_kernel(*refs):
    count = len(refs) // 2
    for source, out in zip(refs[:count], refs[count:]):
        out[...] = source[...]


def own_copy(*arrays):
    vmem = pl.BlockSpec(memory_space=pltpu.VMEM)
    return pl.pallas_call(
        own_kernel,
        out_shape=[jax.ShapeDtypeStruct(a.shape, a.dtype) for a in arrays],
        in_specs=[vmem] * len(arrays),
        out_specs=[vmem] * len(arrays),
        compiler_params=pltpu.CompilerParams(vmem_limit_bytes=VMEM_BYTES),
        cost_estimate=pl.CostEstimate(flops=0, bytes_accessed=2 ** 12, transcendentals=0),
        name="own",
    )(*arrays)


def join_kernel(*refs):
    for k, ref in enumerate(refs[:-1]):
        refs[-1][k] = ref[:refs[-1].shape[1]]


def join(packs, size):
    vmem = pl.BlockSpec(memory_space=pltpu.VMEM)
    return pl.pallas_call(
        join_kernel,
        out_shape=jax.ShapeDtypeStruct((len(packs), size) + packs[0].shape[1:], packs[0].dtype),
        in_specs=[vmem] * len(packs),
        out_specs=vmem,
        compiler_params=pltpu.CompilerParams(vmem_limit_bytes=VMEM_BYTES),
        cost_estimate=pl.CostEstimate(flops=0, bytes_accessed=2 ** 12, transcendentals=0),
        name="join",
    )(*packs)


def front_kernel(planes, slots, order, blocks, pieces, rows_piece, held, *refs):
    relays, packs = refs[:2 * PLANE], refs[2 * PLANE:2 * PLANE + planes]
    closing = refs[2 * PLANE + planes:-7]
    state, named, sums, forms, high, low, wide = refs[-7:]
    me = lax.axis_index("bits")
    span, twice_part = forms.shape[1:]
    depth = span // (2 * PLANE)
    part = twice_part // 2
    rows = held * rows_piece
    locals_ = []
    tail = HEAD + 2 * (span // LANES) * rows
    for k in range(planes):
        first = packs[k].shape[0] - tail
        numbers = packs[k][first:first + HEAD].astype(jnp.float32)
        for n in range(pieces):
            here = slice((k * pieces + n) * rows_piece, (k * pieces + n + 1) * rows_piece)
            named[here, :] = jnp.broadcast_to(numbers[n:n + 1], (rows_piece, LANES))
        locals_.append(packs[k].at[first + HEAD:first + tail])
    shape = (LANES, blocks * rows)
    spread = lax.broadcasted_iota(jnp.int32, shape, 0) - slots == lax.broadcasted_iota(jnp.int32, shape, 1) // rows_piece
    spread = spread.astype(jnp.float32).astype(jnp.bfloat16)
    shape = (planes * pieces * rows_piece, blocks * rows)
    same_row = lax.broadcasted_iota(jnp.int32, shape, 0) % rows_piece == lax.broadcasted_iota(jnp.int32, shape, 1) % rows_piece
    picks = jnp.dot(named[...].astype(jnp.bfloat16), spread, preferred_element_type=jnp.float32)
    picks = jnp.where(same_row, picks, 0.0).astype(jnp.bfloat16)
    for j in range(2 * PLANE):
        there = pl.ds(pl.multiple_of((me ^ j) % (2 * PLANE) * depth, depth), depth)
        for a in range(blocks):
            for c in range(2):
                for n in range(part // LANES):
                    row = ((n * blocks + a) * 2 + c) * depth
                    columns = slice(c * part + n * LANES, c * part + (n + 1) * LANES)
                    forms[a, there, columns] = relays[j][0, row:row + depth, :]
    left = []
    for c in range(2):
        for k in range(planes):
            columns = []
            for n in range(span // LANES):
                first = (c * (span // LANES) + n) * rows
                columns.append(locals_[k][first:first + rows])
            left.append(jnp.concatenate(columns, axis=1))
    left = jnp.concatenate(left, axis=0)
    for a in range(blocks):
        both = jnp.dot(left, forms[a], preferred_element_type=jnp.float32)
        real, imag = both[:planes * rows], both[planes * rows:]
        product = jnp.concatenate([real[:, :part] - imag[:, part:], real[:, part:] + imag[:, :part]], axis=1)
        rounded = product.astype(jnp.bfloat16)
        rest = (product - rounded.astype(jnp.float32)).astype(jnp.bfloat16)
        for k in range(planes):
            high[k, a * rows:(a + 1) * rows, :] = rounded[k * rows:(k + 1) * rows]
            low[k, a * rows:(a + 1) * rows, :] = rest[k * rows:(k + 1) * rows]
    size = pieces * rows_piece
    for k in range(planes):
        pick = picks[k * size:(k + 1) * size]
        total = jnp.dot(pick, high[k], preferred_element_type=jnp.float32)
        total += jnp.dot(pick, low[k], preferred_element_type=jnp.float32)
        state[k * size:(k + 1) * size, :] = total.astype(jnp.bfloat16)
    close(order, named, state, relays + closing, sums, wide)


def close(order, named, state, relays, sums, wide):
    part, rows = wide.shape[0] // 2, state.shape[0]
    lane = lax.broadcasted_iota(jnp.int32, (part, LANES), 1)
    slot = 0
    for relay in relays:
        for k in range(relay.shape[0]):
            real_rows = relay[k, relay.shape[1] - part:]
            turned = pltpu.roll(real_rows.astype(jnp.float32), LANES // 2, 1)
            turned = jnp.where(lane < LANES // 2, -turned, turned)
            wide[:part, slot * LANES:(slot + 1) * LANES] = real_rows
            wide[part:, slot * LANES:(slot + 1) * LANES] = turned.astype(jnp.bfloat16)
            slot += 1
    for j in range(0, slot, 2):
        both = jnp.dot(state[...], wide[:, j * LANES:(j + 2) * LANES], preferred_element_type=jnp.float32)
        for side, slot in enumerate(order[j:j + 2]):
            factor = jnp.broadcast_to(named[:, slot:slot + 1], (rows, LANES))
            add = both[:, side * LANES:(side + 1) * LANES] * factor
            sums[...] = add if slot == 0 else sums[...] + add


def last_kernel(order, named, state, sums_in, relay, *refs):
    *outs, sums, wide = refs
    sums[...] = sums_in[...]
    close(order, named, state, [relay], sums, wide)
    size = sums.shape[0] // len(outs)
    for k, out in enumerate(outs):
        out[...] = sums[k * size:(k + 1) * size, :].reshape(out.shape).astype(out.dtype)


def in_planes(prefix, first_suffix, pair_prefix, pair_suffix, merge_count, suffix, routes, cap):
    owners = lax.axis_size("bits")
    planes = owners // PLANE
    pieces = pair_prefix.shape[0]
    held, rows_piece, twice_width = prefix.shape
    blocks, _, depth, width = first_suffix.shape
    part, span = width // 2, width // (planes // 2)
    vmem = pl.BlockSpec(memory_space=pltpu.VMEM)
    params = pltpu.CompilerParams(vmem_limit_bytes=VMEM_BYTES)
    relayed = blocks * 2 * depth * (part // LANES) + part
    tail = HEAD + 2 * (span // LANES) * held * rows_piece
    sources = (
        first_suffix.reshape(blocks * 2 * depth, width),
        prefix.reshape(held * rows_piece, twice_width),
        suffix[0],
        jnp.swapaxes(cap, 1, 2),
        pair_prefix.T,
        pair_suffix.T,
        merge_count[None],
        routes,
    )
    sizes = [relayed] * 2 + [part + tail] * (planes - 2) + [tail] * 2
    anywhere = pl.BlockSpec(memory_space=pl.ANY)
    packs = pl.pallas_call(
        functools.partial(pack_kernel, planes, pair_prefix.shape[1], held),
        out_shape=[jax.ShapeDtypeStruct((size, LANES), jnp.bfloat16) for size in sizes],
        in_specs=[anywhere] * len(sources),
        out_specs=[anywhere] * len(sizes),
        scratch_shapes=[pltpu.VMEM((size, LANES), jnp.bfloat16) for size in sizes]
        + [pltpu.VMEM(source.shape, source.dtype) for source in sources]
        + [pltpu.SemaphoreType.DMA((len(sources) + 2 + 2 * planes,))],
        compiler_params=pltpu.CompilerParams(vmem_limit_bytes=PACK_BYTES),
        cost_estimate=pl.CostEstimate(flops=2 ** 20, bytes_accessed=2 ** 12, transcendentals=0),
        name="pack",
    )(*sources)
    far = [swap(packs[k], k * PLANE) for k in range(2, planes)]
    near = swap(packs[planes + 1], PLANE)
    relays = [packs[0][None], swap(packs[1], PLANE)[None], join([after(far[0], near)] + far[1:], part)]
    own, local = own_copy(relays[0], packs[planes])
    across = [swap(r, 2) for r in relays[:2]]
    relays[0] = own
    packs = [local, near] + far
    beside = [swap(r, 1) for r in relays]
    corner = [swap(y, 1) for y in across]
    across.append(swap(relays[2], 2))
    corner.append(swap(across[2], 1))
    early = 2 * PLANE
    far_slots = range(early, owners, PLANE)
    order = list(range(early)) + [k + n for n in (0, 1, 2) for k in far_slots]
    last = [k + 3 for k in far_slots]
    relays = [group[n] for n in range(2) for group in (relays, beside, across, corner)] + [relays[2], beside[2], across[2]]
    tiny = pl.CostEstimate(flops=0, bytes_accessed=2 ** 12, transcendentals=0)

    def sums_of(chosen, dtype):
        count = len(chosen)
        rows = count * pieces * rows_piece
        operands = relays[:early] + [packs[k] for k in chosen] + relays[early:]
        state, named, sums = pl.pallas_call(
            functools.partial(front_kernel, count, owners, order, blocks, pieces, rows_piece, held),
            out_shape=[
                jax.ShapeDtypeStruct((rows, 2 * part), jnp.bfloat16),
                jax.ShapeDtypeStruct((rows, LANES), jnp.float32),
                jax.ShapeDtypeStruct((rows, LANES), jnp.float32),
            ],
            in_specs=[vmem] * len(operands),
            out_specs=[vmem] * 3,
            scratch_shapes=[
                pltpu.VMEM((blocks, span, 2 * part), jnp.bfloat16),
                pltpu.VMEM((count, blocks * held * rows_piece, 2 * part), jnp.bfloat16),
                pltpu.VMEM((count, blocks * held * rows_piece, 2 * part), jnp.bfloat16),
                pltpu.VMEM((2 * part, len(order) * LANES), jnp.bfloat16),
            ],
            compiler_params=params,
            cost_estimate=tiny,
            name="front",
        )(*operands)
        return pl.pallas_call(
            functools.partial(last_kernel, last),
            out_shape=[jax.ShapeDtypeStruct((pieces, rows_piece, LANES), dtype)] * count,
            in_specs=[vmem] * 4,
            out_specs=[vmem] * count,
            scratch_shapes=[
                pltpu.VMEM((rows, LANES), jnp.float32),
                pltpu.VMEM((2 * part, len(last) * LANES), jnp.bfloat16),
            ],
            compiler_params=params,
            cost_estimate=tiny,
            name="last",
        )(named, state, sums, corner[2])

    sent = sums_of(range(1, planes), jnp.bfloat16)
    total = sums_of([0], jnp.float32)[0]
    for k in range(1, planes):
        total = total + swap(sent[k - 1], k * PLANE).astype(jnp.float32)
    return total


def by_owner(prefix, first_suffix, pair_prefix, pair_suffix, merge_count, suffix, routes, cap):
    pieces = pair_prefix.shape[0]
    merges = pair_prefix.shape[1]
    held_blocks = prefix.shape[0]
    rows_piece = prefix.shape[1]
    twice_width = prefix.shape[2]
    half_width = twice_width // 2
    first_count = first_suffix.shape[0]
    listed = routes.shape[1]
    owners = lax.axis_size("bits")
    slot_count = min(pieces, max(2, (2 * pieces * listed + owners - 1) // owners))
    live_mask = lax.broadcasted_iota(jnp.int32, (pieces, merges), 1) < merge_count[:, None]
    matches = (
        pair_suffix[:, :, None] == lax.broadcasted_iota(jnp.int32, (pieces, merges, first_count), 2)
    ) & live_mask[:, :, None]
    which_block = pair_prefix[:, :, None] == lax.broadcasted_iota(
        jnp.int32, (pieces, merges, held_blocks), 2
    )
    prefix_picks = jnp.einsum(
        "ika,ikp->iap", matches.astype(jnp.float32), which_block.astype(jnp.float32)
    ).astype(jnp.bfloat16)
    selected = jnp.einsum(
        "iap,prc->airc", prefix_picks, prefix, preferred_element_type=jnp.float32
    ).astype(jnp.bfloat16)
    selected = selected.reshape(first_count, pieces * rows_piece, twice_width)
    portion = lax.all_gather(first_suffix, "bits", axis=2, tiled=True)
    count_rows = portion.shape[2]
    real_cols = lax.slice_in_dim(selected, 0, count_rows, axis=2)
    imag_cols = lax.dynamic_slice_in_dim(selected, half_width, count_rows, 2)
    left_side = jnp.concatenate([real_cols, imag_cols], axis=2)
    upper_half = jnp.concatenate([portion[:, 0], portion[:, 1]], axis=2)
    lower_half = jnp.concatenate([-portion[:, 1], portion[:, 0]], axis=2)
    right_side = jnp.concatenate([upper_half, lower_half], axis=1)
    state_rows = jnp.einsum(
        "arc,acw->rw", left_side, right_side, preferred_element_type=jnp.float32
    )
    state_rows = state_rows.astype(jnp.bfloat16).reshape(pieces, rows_piece, twice_width)
    named_by = jnp.sum(
        (routes[:, :, None] == lax.broadcasted_iota(jnp.int32, (pieces, listed, owners), 2)).astype(
            jnp.int32
        ),
        axis=1,
    )
    slot_rank = jnp.cumsum(named_by, axis=0) - named_by
    slot_hit = (
        slot_rank[:, :, None] == lax.broadcasted_iota(jnp.int32, (pieces, owners, slot_count), 2)
    ) & (named_by[:, :, None] > 0)
    dispatch = jnp.transpose(slot_hit, (1, 2, 0)).astype(jnp.bfloat16)
    outgoing = jnp.einsum(
        "dmi,irc->dmrc", dispatch, state_rows, preferred_element_type=jnp.float32
    ).astype(jnp.bfloat16)
    own_form = complex_form(suffix[0])
    cap_form = complex_form(cap)
    products = jnp.einsum(
        "smrc,cw->smrw",
        lax.all_to_all(outgoing, "bits", split_axis=0, concat_axis=0, tiled=True),
        own_form,
        preferred_element_type=jnp.float32,
    ).astype(jnp.bfloat16)
    capped_terms = jnp.einsum(
        "smrw,wv->smrv", products, cap_form, preferred_element_type=jnp.float32
    )
    returned = lax.all_to_all(
        capped_terms.astype(jnp.bfloat16), "bits", split_axis=0, concat_axis=0, tiled=True
    ).astype(capped_terms.dtype)
    return jnp.einsum(
        "dmi,dmrv->irv", dispatch.astype(jnp.float32), returned, precision=HIGHEST_PRECISION
    )


def on_device(*args):
    prefix, first_suffix, pair_prefix, routes, cap = args[0], args[1], args[2], args[6], args[7]
    owners = lax.axis_size("bits")
    planes = owners // PLANE
    depth, width = first_suffix.shape[2:]
    pieces = pair_prefix.shape[0]
    fits = (
        planes > 2
        and planes & (planes - 1) == 0
        and owners <= 256
        and width == owners * depth
        and width % (planes // 2 * LANES) == 0
        and width // 2 % LANES == 0
        and 2 * cap.shape[2] == LANES
        and depth % 16 == 0
        and prefix.shape[1] % 16 == 0
        and pieces <= HEAD
        and owners + first_suffix.shape[0] * prefix.shape[0] <= LANES
    )
    return in_planes(*args) if fits else by_owner(*args)


def solution(mesh):
    return jax.shard_map(
        on_device,
        mesh=mesh,
        in_specs=(
            P(("grp", "bits"), None, None),
            P("grp", None, "bits", None),
            P(("grp", "bits"), None),
            P(("grp", "bits"), None),
            P(("grp", "bits")),
            P(("grp", "bits"), None, None, None),
            P(("grp", "bits"), None),
            P(),
        ),
        out_specs=P(("grp", "bits"), None, None),
        check_vma=False,
    )
```

```python
import functools

import jax
import jax.numpy as jnp
from jax import lax
from jax.experimental import pallas as pl
from jax.experimental.pallas import tpu as pltpu
from jax.sharding import PartitionSpec as P

HIGHEST_PRECISION = lax.Precision.HIGHEST
LANES = 128
PLANE = 4
VMEM_BYTES = 32 * 1024 * 1024
HEAD = 16
PACK_BYTES = 60 * 1024 * 1024


def complex_form(blocks):
    real_part = blocks[..., 0, :, :]
    imag_part = blocks[..., 1, :, :]
    upper_half = jnp.concatenate([real_part, imag_part], axis=-1)
    lower_half = jnp.concatenate([-imag_part, real_part], axis=-1)
    return jnp.concatenate([upper_half, lower_half], axis=-2)


def swap(x, bit):
    owners = lax.axis_size("bits")
    return lax.ppermute(x, "bits", [(i, i ^ bit) for i in range(owners)])


def after(x, others):
    return lax.optimization_barrier((x, others))[0]


def pack_kernel(planes, merges, held, *refs):
    sources, outs, stages, copied = refs[:8], refs[8:10 + planes], refs[10 + planes:12 + 2 * planes], refs[12 + 2 * planes:-1]
    sems = refs[-1]
    first_ref, prefix_ref, suffix_ref, cap_ref, pair_prefix_ref, pair_suffix_ref, count_ref, routes_ref = copied
    width = suffix_ref.shape[1]
    rows, twice_width = prefix_ref.shape
    part, span, slots = width // 2, width // (planes // 2), planes * PLANE
    me = lax.axis_index("bits")
    plane = me // PLANE
    inward = [pltpu.make_async_copy(source, ref, sems.at[n]) for n, (source, ref) in enumerate(zip(sources, copied))]
    for copy in inward:
        copy.start()
    outward = []

    def send(k, row, size):
        there = pl.ds(row, size)
        sem = sems.at[len(sources) + len(outward)]
        outward.append(pltpu.make_async_copy(stages[k].at[there, :], outs[k].at[there, :], sem))
        outward[-1].start()

    lows = [plane % 2 ^ k % 2 for k in range(planes)]
    firsts = [first_ref.shape[0] * (part // LANES) if k < 2 else 0 for k in range(planes)]
    inward[0].wait()
    for k in range(2):
        for n in range(part // LANES):
            columns = pl.ds(pl.multiple_of(lows[k] * part + n * LANES, LANES), LANES)
            stages[k][n * first_ref.shape[0]:(n + 1) * first_ref.shape[0], :] = first_ref[:, columns]
        send(k, 0, firsts[k])
    for copy in inward[4:]:
        copy.wait()
    pieces = routes_ref.shape[0]
    lane = lax.broadcasted_iota(jnp.int32, (pieces, LANES), 1)
    named = [jnp.zeros((pieces, LANES), jnp.int32)] * planes
    for slot in range(slots):
        hits = jnp.sum((routes_ref[...] == slot ^ me).astype(jnp.int32), axis=1, keepdims=True)
        named = [jnp.where(lane == slot ^ k * PLANE, hits, there) for k, there in enumerate(named)]
        handed_on = 2 * slots + (slot ^ (planes - 1) * PLANE)
        named[planes // 2] = jnp.where(lane == handed_on, hits, named[planes // 2])
    own_lane = lax.broadcasted_iota(jnp.int32, (pieces, pieces), 0) == lax.broadcasted_iota(jnp.int32, (pieces, pieces), 1)
    picks = jnp.zeros((pieces, LANES), jnp.int32)
    for m in range(merges):
        pick = pair_suffix_ref[m:m + 1, :] * held + pair_prefix_ref[m:m + 1, :]
        pick = jnp.where(m < count_ref[...], slots + pick, -1)
        pick = jnp.sum(jnp.where(own_lane, jnp.broadcast_to(pick, (pieces, pieces)), 0), axis=1, keepdims=True)
        picks += (lane == pick).astype(jnp.int32)
    inward[1].wait()
    for k in range(planes - 1):
        message, start = (planes + k, 0) if k < 2 else (k, part)
        stage, high = stages[message], plane // 2 ^ k // 2
        rest = jnp.zeros((HEAD - pieces, LANES), jnp.float32)
        routing = jnp.concatenate([(named[k] + picks).astype(jnp.float32), rest], axis=0)
        stage[start:start + HEAD, :] = routing.astype(jnp.bfloat16)
        row = start + HEAD
        for side in range(0, twice_width, width):
            for n in range(0, span, LANES):
                columns = pl.ds(pl.multiple_of(high * span + (side + n), LANES), LANES)
                stage[row:row + rows, :] = prefix_ref[:, columns]
                row += rows
        send(message, start, row - start)
    inward[3].wait()
    upper = jnp.concatenate([cap_ref[0], cap_ref[1]], axis=0)
    lower = jnp.concatenate([-cap_ref[1], cap_ref[0]], axis=0)
    turned = (((1,), (1,)), ((), ()))
    inward[2].wait()
    for low in range(2):
        there = pl.ds(pl.multiple_of((plane % 2 ^ low) * part, part), part)
        both = lax.dot_general(suffix_ref[0, there, :], upper, turned, preferred_element_type=jnp.float32)
        both += lax.dot_general(suffix_ref[1, there, :], lower, turned, preferred_element_type=jnp.float32)
        both = both.astype(jnp.bfloat16)
        for k in range(low, planes, 2):
            stages[k][firsts[k]:firsts[k] + part, :] = both
            send(k, firsts[k], part)
    for copy in outward:
        copy.wait()


def own_kernel(*refs):
    count = len(refs) // 2
    for source, out in zip(refs[:count], refs[count:]):
        out[...] = source[...]


def own_copy(*arrays):
    vmem = pl.BlockSpec(memory_space=pltpu.VMEM)
    return pl.pallas_call(
        own_kernel,
        out_shape=[jax.ShapeDtypeStruct(a.shape, a.dtype) for a in arrays],
        in_specs=[vmem] * len(arrays),
        out_specs=[vmem] * len(arrays),
        compiler_params=pltpu.CompilerParams(vmem_limit_bytes=VMEM_BYTES),
        cost_estimate=pl.CostEstimate(flops=0, bytes_accessed=2 ** 12, transcendentals=0),
        name="own",
    )(*arrays)


def join_kernel(*refs):
    *packs, group, rest = refs
    size = group.shape[1]
    for k, pack in enumerate(packs):
        group[k] = pack[:size]
    rest[...] = packs[0][size:]


def join(packs, size):
    vmem = pl.BlockSpec(memory_space=pltpu.VMEM)
    return pl.pallas_call(
        join_kernel,
        out_shape=[
            jax.ShapeDtypeStruct((len(packs), size) + packs[0].shape[1:], packs[0].dtype),
            jax.ShapeDtypeStruct((packs[0].shape[0] - size,) + packs[0].shape[1:], packs[0].dtype),
        ],
        in_specs=[vmem] * len(packs),
        out_specs=[vmem] * 2,
        compiler_params=pltpu.CompilerParams(vmem_limit_bytes=VMEM_BYTES),
        cost_estimate=pl.CostEstimate(flops=0, bytes_accessed=2 ** 12, transcendentals=0),
        name="join",
    )(*packs)


def front_kernel(planes, handed_on, slots, order, blocks, pieces, rows_piece, held, *refs):
    relays, packs = refs[:2 * PLANE], refs[2 * PLANE:2 * PLANE + planes]
    closing = refs[2 * PLANE + planes:-7]
    state, named, sums, forms, high, low, wide = refs[-7:]
    me = lax.axis_index("bits")
    span, twice_part = forms.shape[1:]
    depth = span // (2 * PLANE)
    part = twice_part // 2
    rows = held * rows_piece
    locals_ = []
    tail = HEAD + 2 * (span // LANES) * rows
    for k in range(planes):
        first = packs[k].shape[0] - tail
        numbers = packs[k][first:first + HEAD].astype(jnp.float32)
        if k == handed_on:
            lane = lax.broadcasted_iota(jnp.int32, numbers.shape, 1)
            numbers = jnp.where(lane < slots, pltpu.roll(numbers, LANES - 2 * slots, 1), numbers)
        for n in range(pieces):
            here = slice((k * pieces + n) * rows_piece, (k * pieces + n + 1) * rows_piece)
            named[here, :] = jnp.broadcast_to(numbers[n:n + 1], (rows_piece, LANES))
        locals_.append(packs[k].at[first + HEAD:first + tail])
    shape = (LANES, blocks * rows)
    spread = lax.broadcasted_iota(jnp.int32, shape, 0) - slots == lax.broadcasted_iota(jnp.int32, shape, 1) // rows_piece
    spread = spread.astype(jnp.float32).astype(jnp.bfloat16)
    shape = (planes * pieces * rows_piece, blocks * rows)
    same_row = lax.broadcasted_iota(jnp.int32, shape, 0) % rows_piece == lax.broadcasted_iota(jnp.int32, shape, 1) % rows_piece
    picks = jnp.dot(named[...].astype(jnp.bfloat16), spread, preferred_element_type=jnp.float32)
    picks = jnp.where(same_row, picks, 0.0).astype(jnp.bfloat16)
    for j in range(2 * PLANE):
        there = pl.ds(pl.multiple_of((me ^ j) % (2 * PLANE) * depth, depth), depth)
        for a in range(blocks):
            for c in range(2):
                for n in range(part // LANES):
                    row = ((n * blocks + a) * 2 + c) * depth
                    columns = slice(c * part + n * LANES, c * part + (n + 1) * LANES)
                    forms[a, there, columns] = relays[j][0, row:row + depth, :]
    left = []
    for c in range(2):
        for k in range(planes):
            columns = []
            for n in range(span // LANES):
                first = (c * (span // LANES) + n) * rows
                columns.append(locals_[k][first:first + rows])
            left.append(jnp.concatenate(columns, axis=1))
    left = jnp.concatenate(left, axis=0)
    for a in range(blocks):
        both = jnp.dot(left, forms[a], preferred_element_type=jnp.float32)
        real, imag = both[:planes * rows], both[planes * rows:]
        product = jnp.concatenate([real[:, :part] - imag[:, part:], real[:, part:] + imag[:, :part]], axis=1)
        rounded = product.astype(jnp.bfloat16)
        rest = (product - rounded.astype(jnp.float32)).astype(jnp.bfloat16)
        for k in range(planes):
            high[k, a * rows:(a + 1) * rows, :] = rounded[k * rows:(k + 1) * rows]
            low[k, a * rows:(a + 1) * rows, :] = rest[k * rows:(k + 1) * rows]
    size = pieces * rows_piece
    for k in range(planes):
        pick = picks[k * size:(k + 1) * size]
        total = jnp.dot(pick, high[k], preferred_element_type=jnp.float32)
        total += jnp.dot(pick, low[k], preferred_element_type=jnp.float32)
        state[k * size:(k + 1) * size, :] = total.astype(jnp.bfloat16)
    close(order, named, state, relays + closing, sums, wide)


def close(order, named, state, relays, sums, wide):
    part, rows = wide.shape[0] // 2, state.shape[0]
    lane = lax.broadcasted_iota(jnp.int32, (part, LANES), 1)
    sign = jnp.where(lane < LANES // 2, -1.0, 1.0).astype(jnp.bfloat16)
    slot = 0
    for relay in relays:
        for k in range(relay.shape[0]):
            real_rows = relay[k, relay.shape[1] - part:]
            turned = pltpu.roll(real_rows, LANES // 2, 1) * sign
            wide[:part, slot * LANES:(slot + 1) * LANES] = real_rows
            wide[part:, slot * LANES:(slot + 1) * LANES] = turned
            slot += 1
    for j in range(0, slot, 2):
        both = jnp.dot(state[...], wide[:, j * LANES:(j + 2) * LANES], preferred_element_type=jnp.float32)
        for side, slot in enumerate(order[j:j + 2]):
            factor = jnp.broadcast_to(named[:, slot:slot + 1], (rows, LANES))
            add = both[:, side * LANES:(side + 1) * LANES] * factor
            sums[...] = add if slot == 0 else sums[...] + add


def last_kernel(order, named, state, sums_in, relay, *refs):
    *outs, sums, wide = refs
    sums[...] = sums_in[...]
    close(order, named, state, [relay], sums, wide)
    size = sums.shape[0] // len(outs)
    for k, out in enumerate(outs):
        out[...] = sums[k * size:(k + 1) * size, :].reshape(out.shape).astype(out.dtype)


def in_planes(prefix, first_suffix, pair_prefix, pair_suffix, merge_count, suffix, routes, cap):
    owners = lax.axis_size("bits")
    planes = owners // PLANE
    pieces = pair_prefix.shape[0]
    held, rows_piece, twice_width = prefix.shape
    blocks, _, depth, width = first_suffix.shape
    part, span = width // 2, width // (planes // 2)
    vmem = pl.BlockSpec(memory_space=pltpu.VMEM)
    params = pltpu.CompilerParams(vmem_limit_bytes=VMEM_BYTES)
    relayed = blocks * 2 * depth * (part // LANES) + part
    tail = HEAD + 2 * (span // LANES) * held * rows_piece
    sources = (
        first_suffix.reshape(blocks * 2 * depth, width),
        prefix.reshape(held * rows_piece, twice_width),
        suffix[0],
        jnp.swapaxes(cap, 1, 2),
        pair_prefix.T,
        pair_suffix.T,
        merge_count[None],
        routes,
    )
    sizes = [relayed] * 2 + [part + tail, part] + [tail] * 2
    anywhere = pl.BlockSpec(memory_space=pl.ANY)
    packs = pl.pallas_call(
        functools.partial(pack_kernel, planes, pair_prefix.shape[1], held),
        out_shape=[jax.ShapeDtypeStruct((size, LANES), jnp.bfloat16) for size in sizes],
        in_specs=[anywhere] * len(sources),
        out_specs=[anywhere] * len(sizes),
        scratch_shapes=[pltpu.VMEM((size, LANES), jnp.bfloat16) for size in sizes]
        + [pltpu.VMEM(source.shape, source.dtype) for source in sources]
        + [pltpu.SemaphoreType.DMA((len(sources) + 1 + 2 * planes,))],
        compiler_params=pltpu.CompilerParams(vmem_limit_bytes=PACK_BYTES),
        cost_estimate=pl.CostEstimate(flops=2 ** 20, bytes_accessed=2 ** 12, transcendentals=0),
        name="pack",
    )(*sources)
    far = [swap(packs[k], k * PLANE) for k in range(2, planes)]
    near = swap(packs[planes + 1], PLANE)
    group, rest = join(far, part)
    handed = swap(rest, PLANE)
    relays = [packs[0][None], swap(packs[1], PLANE)[None], group]
    own, local = own_copy(relays[0], packs[planes])
    across = [swap(r, 2) for r in relays]
    relays[0] = own
    packs = [local, near, far[0], handed]
    beside = [swap(relays[0], 1), None, swap(after(relays[2], near), 1)]
    beside[1] = swap(after(relays[1], beside[2]), 1)
    corner = [swap(across[0], 1), swap(after(across[1], handed), 1), swap(across[2], 1)]
    early = 2 * PLANE
    far_slots = range(early, owners, PLANE)
    order = list(range(early)) + [k + n for n in (0, 1, 2) for k in far_slots]
    last = [k + 3 for k in far_slots]
    relays = [group[n] for n in range(2) for group in (relays, beside, across, corner)] + [relays[2], beside[2], across[2]]
    tiny = pl.CostEstimate(flops=0, bytes_accessed=2 ** 12, transcendentals=0)

    def sums_of(chosen, dtype):
        count = len(chosen)
        rows = count * pieces * rows_piece
        operands = relays[:early] + [packs[k] for k in chosen] + relays[early:]
        state, named, sums = pl.pallas_call(
            functools.partial(front_kernel, count, list(chosen).index(planes - 1) if planes - 1 in chosen else None, owners, order, blocks, pieces, rows_piece, held),
            out_shape=[
                jax.ShapeDtypeStruct((rows, 2 * part), jnp.bfloat16),
                jax.ShapeDtypeStruct((rows, LANES), jnp.float32),
                jax.ShapeDtypeStruct((rows, LANES), jnp.float32),
            ],
            in_specs=[vmem] * len(operands),
            out_specs=[vmem] * 3,
            scratch_shapes=[
                pltpu.VMEM((blocks, span, 2 * part), jnp.bfloat16),
                pltpu.VMEM((count, blocks * held * rows_piece, 2 * part), jnp.bfloat16),
                pltpu.VMEM((count, blocks * held * rows_piece, 2 * part), jnp.bfloat16),
                pltpu.VMEM((2 * part, len(order) * LANES), jnp.bfloat16),
            ],
            compiler_params=params,
            cost_estimate=tiny,
            name="front",
        )(*operands)
        return pl.pallas_call(
            functools.partial(last_kernel, last),
            out_shape=[jax.ShapeDtypeStruct((pieces, rows_piece, LANES), dtype)] * count,
            in_specs=[vmem] * 4,
            out_specs=[vmem] * count,
            scratch_shapes=[
                pltpu.VMEM((rows, LANES), jnp.float32),
                pltpu.VMEM((2 * part, len(last) * LANES), jnp.bfloat16),
            ],
            compiler_params=params,
            cost_estimate=tiny,
            name="last",
        )(named, state, sums, corner[2])

    sent = sums_of(range(1, planes), jnp.bfloat16)
    total = sums_of([0], jnp.float32)[0]
    for k in range(1, planes):
        total = total + swap(sent[k - 1], k * PLANE).astype(jnp.float32)
    return total


def by_owner(prefix, first_suffix, pair_prefix, pair_suffix, merge_count, suffix, routes, cap):
    pieces = pair_prefix.shape[0]
    merges = pair_prefix.shape[1]
    held_blocks = prefix.shape[0]
    rows_piece = prefix.shape[1]
    twice_width = prefix.shape[2]
    half_width = twice_width // 2
    first_count = first_suffix.shape[0]
    listed = routes.shape[1]
    owners = lax.axis_size("bits")
    slot_count = min(pieces, max(2, (2 * pieces * listed + owners - 1) // owners))
    live_mask = lax.broadcasted_iota(jnp.int32, (pieces, merges), 1) < merge_count[:, None]
    matches = (
        pair_suffix[:, :, None] == lax.broadcasted_iota(jnp.int32, (pieces, merges, first_count), 2)
    ) & live_mask[:, :, None]
    which_block = pair_prefix[:, :, None] == lax.broadcasted_iota(
        jnp.int32, (pieces, merges, held_blocks), 2
    )
    prefix_picks = jnp.einsum(
        "ika,ikp->iap", matches.astype(jnp.float32), which_block.astype(jnp.float32)
    ).astype(jnp.bfloat16)
    selected = jnp.einsum(
        "iap,prc->airc", prefix_picks, prefix, preferred_element_type=jnp.float32
    ).astype(jnp.bfloat16)
    selected = selected.reshape(first_count, pieces * rows_piece, twice_width)
    portion = lax.all_gather(first_suffix, "bits", axis=2, tiled=True)
    count_rows = portion.shape[2]
    real_cols = lax.slice_in_dim(selected, 0, count_rows, axis=2)
    imag_cols = lax.dynamic_slice_in_dim(selected, half_width, count_rows, 2)
    left_side = jnp.concatenate([real_cols, imag_cols], axis=2)
    upper_half = jnp.concatenate([portion[:, 0], portion[:, 1]], axis=2)
    lower_half = jnp.concatenate([-portion[:, 1], portion[:, 0]], axis=2)
    right_side = jnp.concatenate([upper_half, lower_half], axis=1)
    state_rows = jnp.einsum(
        "arc,acw->rw", left_side, right_side, preferred_element_type=jnp.float32
    )
    state_rows = state_rows.astype(jnp.bfloat16).reshape(pieces, rows_piece, twice_width)
    named_by = jnp.sum(
        (routes[:, :, None] == lax.broadcasted_iota(jnp.int32, (pieces, listed, owners), 2)).astype(
            jnp.int32
        ),
        axis=1,
    )
    slot_rank = jnp.cumsum(named_by, axis=0) - named_by
    slot_hit = (
        slot_rank[:, :, None] == lax.broadcasted_iota(jnp.int32, (pieces, owners, slot_count), 2)
    ) & (named_by[:, :, None] > 0)
    dispatch = jnp.transpose(slot_hit, (1, 2, 0)).astype(jnp.bfloat16)
    outgoing = jnp.einsum(
        "dmi,irc->dmrc", dispatch, state_rows, preferred_element_type=jnp.float32
    ).astype(jnp.bfloat16)
    own_form = complex_form(suffix[0])
    cap_form = complex_form(cap)
    products = jnp.einsum(
        "smrc,cw->smrw",
        lax.all_to_all(outgoing, "bits", split_axis=0, concat_axis=0, tiled=True),
        own_form,
        preferred_element_type=jnp.float32,
    ).astype(jnp.bfloat16)
    capped_terms = jnp.einsum(
        "smrw,wv->smrv", products, cap_form, preferred_element_type=jnp.float32
    )
    returned = lax.all_to_all(
        capped_terms.astype(jnp.bfloat16), "bits", split_axis=0, concat_axis=0, tiled=True
    ).astype(capped_terms.dtype)
    return jnp.einsum(
        "dmi,dmrv->irv", dispatch.astype(jnp.float32), returned, precision=HIGHEST_PRECISION
    )


def on_device(*args):
    prefix, first_suffix, pair_prefix, routes, cap = args[0], args[1], args[2], args[6], args[7]
    owners = lax.axis_size("bits")
    planes = owners // PLANE
    depth, width = first_suffix.shape[2:]
    pieces = pair_prefix.shape[0]
    fits = (
        planes == 4
        and owners == planes * PLANE
        and width == owners * depth
        and width % (planes // 2 * LANES) == 0
        and width // 2 % LANES == 0
        and 2 * cap.shape[2] == LANES
        and depth % 16 == 0
        and prefix.shape[1] % 16 == 0
        and pieces <= HEAD
        and first_suffix.shape[0] * prefix.shape[0] <= owners
        and 3 * owners <= LANES
    )
    return in_planes(*args) if fits else by_owner(*args)


def solution(mesh):
    return jax.shard_map(
        on_device,
        mesh=mesh,
        in_specs=(
            P(("grp", "bits"), None, None),
            P("grp", None, "bits", None),
            P(("grp", "bits"), None),
            P(("grp", "bits"), None),
            P(("grp", "bits")),
            P(("grp", "bits"), None, None, None),
            P(("grp", "bits"), None),
            P(),
        ),
        out_specs=P(("grp", "bits"), None, None),
        check_vma=False,
    )
```

```python
import functools

import jax
import jax.numpy as jnp
from jax import lax
from jax.experimental import pallas as pl
from jax.experimental.pallas import tpu as pltpu
from jax.sharding import PartitionSpec as P

HIGHEST_PRECISION = lax.Precision.HIGHEST
LANES = 128
PLANE = 4
VMEM_BYTES = 32 * 1024 * 1024
HEAD = 16
PACK_BYTES = 60 * 1024 * 1024


def complex_form(blocks):
    real_part = blocks[..., 0, :, :]
    imag_part = blocks[..., 1, :, :]
    upper_half = jnp.concatenate([real_part, imag_part], axis=-1)
    lower_half = jnp.concatenate([-imag_part, real_part], axis=-1)
    return jnp.concatenate([upper_half, lower_half], axis=-2)


def swap(x, bit):
    owners = lax.axis_size("bits")
    return lax.ppermute(x, "bits", [(i, i ^ bit) for i in range(owners)])


def after(x, others):
    return lax.optimization_barrier((x, others))[0]


def pack_kernel(planes, merges, held, *refs):
    sources, outs, stages, copied = refs[:8], refs[8:10 + planes], refs[10 + planes:12 + 2 * planes], refs[12 + 2 * planes:-1]
    sems = refs[-1]
    first_ref, prefix_ref, suffix_ref, cap_ref, pair_prefix_ref, pair_suffix_ref, count_ref, routes_ref = copied
    width = suffix_ref.shape[1]
    rows, twice_width = prefix_ref.shape
    part, span, slots = width // 2, width // (planes // 2), planes * PLANE
    me = lax.axis_index("bits")
    plane = me // PLANE
    inward = [pltpu.make_async_copy(source, ref, sems.at[n]) for n, (source, ref) in enumerate(zip(sources, copied))]
    for copy in inward:
        copy.start()
    outward = []

    def send(k, row, size):
        there = pl.ds(row, size)
        sem = sems.at[len(sources) + len(outward)]
        outward.append(pltpu.make_async_copy(stages[k].at[there, :], outs[k].at[there, :], sem))
        outward[-1].start()

    lows = [plane % 2 ^ k % 2 for k in range(planes)]
    firsts = [first_ref.shape[0] * (part // LANES) if k < 2 else 0 for k in range(planes)]
    inward[0].wait()
    for k in range(2):
        for n in range(part // LANES):
            columns = pl.ds(pl.multiple_of(lows[k] * part + n * LANES, LANES), LANES)
            stages[k][n * first_ref.shape[0]:(n + 1) * first_ref.shape[0], :] = first_ref[:, columns]
        send(k, 0, firsts[k])
    for copy in inward[4:]:
        copy.wait()
    pieces = routes_ref.shape[0]
    lane = lax.broadcasted_iota(jnp.int32, (pieces, LANES), 1)
    named = [jnp.zeros((pieces, LANES), jnp.int32)] * planes
    for slot in range(slots):
        hits = jnp.sum((routes_ref[...] == slot ^ me).astype(jnp.int32), axis=1, keepdims=True)
        named = [jnp.where(lane == slot ^ k * PLANE, hits, there) for k, there in enumerate(named)]
        handed_on = 2 * slots + (slot ^ (planes - 1) * PLANE)
        named[planes // 2] = jnp.where(lane == handed_on, hits, named[planes // 2])
    own_lane = lax.broadcasted_iota(jnp.int32, (pieces, pieces), 0) == lax.broadcasted_iota(jnp.int32, (pieces, pieces), 1)
    picks = jnp.zeros((pieces, LANES), jnp.int32)
    for m in range(merges):
        pick = pair_suffix_ref[m:m + 1, :] * held + pair_prefix_ref[m:m + 1, :]
        pick = jnp.where(m < count_ref[...], slots + pick, -1)
        pick = jnp.sum(jnp.where(own_lane, jnp.broadcast_to(pick, (pieces, pieces)), 0), axis=1, keepdims=True)
        picks += (lane == pick).astype(jnp.int32)
    inward[1].wait()
    for k in range(planes - 1):
        message, start = (planes + k, 0) if k < 2 else (k, part)
        stage, high = stages[message], plane // 2 ^ k // 2
        rest = jnp.zeros((HEAD - pieces, LANES), jnp.float32)
        routing = jnp.concatenate([(named[k] + picks).astype(jnp.float32), rest], axis=0)
        stage[start:start + HEAD, :] = routing.astype(jnp.bfloat16)
        row = start + HEAD
        for side in range(0, twice_width, width):
            for n in range(0, span, LANES):
                columns = pl.ds(pl.multiple_of(high * span + (side + n), LANES), LANES)
                stage[row:row + rows, :] = prefix_ref[:, columns]
                row += rows
        send(message, start, row - start)
    inward[3].wait()
    upper = jnp.concatenate([cap_ref[0], cap_ref[1]], axis=0)
    lower = jnp.concatenate([-cap_ref[1], cap_ref[0]], axis=0)
    turned = (((1,), (1,)), ((), ()))
    inward[2].wait()
    for low in range(2):
        there = pl.ds(pl.multiple_of((plane % 2 ^ low) * part, part), part)
        both = lax.dot_general(suffix_ref[0, there, :], upper, turned, preferred_element_type=jnp.float32)
        both += lax.dot_general(suffix_ref[1, there, :], lower, turned, preferred_element_type=jnp.float32)
        both = both.astype(jnp.bfloat16)
        for k in range(low, planes, 2):
            stages[k][firsts[k]:firsts[k] + part, :] = both
            send(k, firsts[k], part)
    for copy in outward:
        copy.wait()


def own_kernel(*refs):
    count = len(refs) // 2
    for source, out in zip(refs[:count], refs[count:]):
        out[...] = source[...]


def own_copy(*arrays):
    vmem = pl.BlockSpec(memory_space=pltpu.VMEM)
    return pl.pallas_call(
        own_kernel,
        out_shape=[jax.ShapeDtypeStruct(a.shape, a.dtype) for a in arrays],
        in_specs=[vmem] * len(arrays),
        out_specs=[vmem] * len(arrays),
        compiler_params=pltpu.CompilerParams(vmem_limit_bytes=VMEM_BYTES),
        cost_estimate=pl.CostEstimate(flops=0, bytes_accessed=2 ** 12, transcendentals=0),
        name="own",
    )(*arrays)


def join_kernel(*refs):
    *packs, group, rest = refs
    size = group.shape[1]
    for k, pack in enumerate(packs):
        group[k] = pack[:size]
    rest[...] = packs[0][size:]


def join(packs, size):
    vmem = pl.BlockSpec(memory_space=pltpu.VMEM)
    return pl.pallas_call(
        join_kernel,
        out_shape=[
            jax.ShapeDtypeStruct((len(packs), size) + packs[0].shape[1:], packs[0].dtype),
            jax.ShapeDtypeStruct((packs[0].shape[0] - size,) + packs[0].shape[1:], packs[0].dtype),
        ],
        in_specs=[vmem] * len(packs),
        out_specs=[vmem] * 2,
        compiler_params=pltpu.CompilerParams(vmem_limit_bytes=VMEM_BYTES),
        cost_estimate=pl.CostEstimate(flops=0, bytes_accessed=2 ** 12, transcendentals=0),
        name="join",
    )(*packs)


def front_kernel(planes, handed_on, slots, order, blocks, pieces, rows_piece, held, *refs):
    relays, packs = refs[:2 * PLANE], refs[2 * PLANE:2 * PLANE + planes]
    closing = refs[2 * PLANE + planes:-7]
    state, named, sums, forms, high, low, wide = refs[-7:]
    me = lax.axis_index("bits")
    span, twice_part = forms.shape[1:]
    depth = span // (2 * PLANE)
    part = twice_part // 2
    rows = held * rows_piece
    locals_ = []
    tail = HEAD + 2 * (span // LANES) * rows
    for k in range(planes):
        first = packs[k].shape[0] - tail
        numbers = packs[k][first:first + HEAD].astype(jnp.float32)
        if k == handed_on:
            lane = lax.broadcasted_iota(jnp.int32, numbers.shape, 1)
            numbers = jnp.where(lane < slots, pltpu.roll(numbers, LANES - 2 * slots, 1), numbers)
        for n in range(pieces):
            here = slice((k * pieces + n) * rows_piece, (k * pieces + n + 1) * rows_piece)
            named[here, :] = jnp.broadcast_to(numbers[n:n + 1], (rows_piece, LANES))
        locals_.append(packs[k].at[first + HEAD:first + tail])
    shape = (LANES, blocks * rows)
    spread = lax.broadcasted_iota(jnp.int32, shape, 0) - slots == lax.broadcasted_iota(jnp.int32, shape, 1) // rows_piece
    spread = spread.astype(jnp.float32).astype(jnp.bfloat16)
    shape = (planes * pieces * rows_piece, blocks * rows)
    same_row = lax.broadcasted_iota(jnp.int32, shape, 0) % rows_piece == lax.broadcasted_iota(jnp.int32, shape, 1) % rows_piece
    picks = jnp.dot(named[...].astype(jnp.bfloat16), spread, preferred_element_type=jnp.float32)
    picks = jnp.where(same_row, picks, 0.0).astype(jnp.bfloat16)
    for j in range(2 * PLANE):
        there = pl.ds(pl.multiple_of((me ^ j) % (2 * PLANE) * depth, depth), depth)
        for a in range(blocks):
            for c in range(2):
                for n in range(part // LANES):
                    row = ((n * blocks + a) * 2 + c) * depth
                    columns = slice(c * part + n * LANES, c * part + (n + 1) * LANES)
                    forms[a, there, columns] = relays[j][0, row:row + depth, :]
    left = []
    for c in range(2):
        for k in range(planes):
            columns = []
            for n in range(span // LANES):
                first = (c * (span // LANES) + n) * rows
                columns.append(locals_[k][first:first + rows])
            left.append(jnp.concatenate(columns, axis=1))
    left = jnp.concatenate(left, axis=0)
    for a in range(blocks):
        both = jnp.dot(left, forms[a], preferred_element_type=jnp.float32)
        real, imag = both[:planes * rows], both[planes * rows:]
        product = jnp.concatenate([real[:, :part] - imag[:, part:], real[:, part:] + imag[:, :part]], axis=1)
        rounded = product.astype(jnp.bfloat16)
        rest = (product - rounded.astype(jnp.float32)).astype(jnp.bfloat16)
        for k in range(planes):
            high[k, a * rows:(a + 1) * rows, :] = rounded[k * rows:(k + 1) * rows]
            low[k, a * rows:(a + 1) * rows, :] = rest[k * rows:(k + 1) * rows]
    size = pieces * rows_piece
    for k in range(planes):
        pick = picks[k * size:(k + 1) * size]
        total = jnp.dot(pick, high[k], preferred_element_type=jnp.float32)
        total += jnp.dot(pick, low[k], preferred_element_type=jnp.float32)
        state[k * size:(k + 1) * size, :] = total.astype(jnp.bfloat16)
    close(order, named, state, relays + closing, sums, wide)


def close(order, named, state, relays, sums, wide):
    part, rows = wide.shape[0] // 2, state.shape[0]
    lane = lax.broadcasted_iota(jnp.int32, (part, LANES), 1)
    sign = jnp.where(lane < LANES // 2, -1.0, 1.0).astype(jnp.bfloat16)
    slot = 0
    for relay in relays:
        for k in range(relay.shape[0]):
            real_rows = relay[k, relay.shape[1] - part:]
            turned = pltpu.roll(real_rows, LANES // 2, 1) * sign
            wide[:part, slot * LANES:(slot + 1) * LANES] = real_rows
            wide[part:, slot * LANES:(slot + 1) * LANES] = turned
            slot += 1
    for j in range(0, slot, 2):
        both = jnp.dot(state[...], wide[:, j * LANES:(j + 2) * LANES], preferred_element_type=jnp.float32)
        for side, slot in enumerate(order[j:j + 2]):
            factor = jnp.broadcast_to(named[:, slot:slot + 1], (rows, LANES))
            add = both[:, side * LANES:(side + 1) * LANES] * factor
            sums[...] = add if slot == 0 else sums[...] + add


def last_kernel(order, named, state, sums_in, relay, *refs):
    *outs, sums, wide = refs
    sums[...] = sums_in[...]
    close(order, named, state, [relay], sums, wide)
    size = sums.shape[0] // len(outs)
    for k, out in enumerate(outs):
        out[...] = sums[k * size:(k + 1) * size, :].reshape(out.shape).astype(out.dtype)


def in_planes(prefix, first_suffix, pair_prefix, pair_suffix, merge_count, suffix, routes, cap):
    owners = lax.axis_size("bits")
    planes = owners // PLANE
    pieces = pair_prefix.shape[0]
    held, rows_piece, twice_width = prefix.shape
    blocks, _, depth, width = first_suffix.shape
    part, span = width // 2, width // (planes // 2)
    vmem = pl.BlockSpec(memory_space=pltpu.VMEM)
    params = pltpu.CompilerParams(vmem_limit_bytes=VMEM_BYTES)
    relayed = blocks * 2 * depth * (part // LANES) + part
    tail = HEAD + 2 * (span // LANES) * held * rows_piece
    sources = (
        first_suffix.reshape(blocks * 2 * depth, width),
        prefix.reshape(held * rows_piece, twice_width),
        suffix[0],
        jnp.swapaxes(cap, 1, 2),
        pair_prefix.T,
        pair_suffix.T,
        merge_count[None],
        routes,
    )
    sizes = [relayed] * 2 + [part + tail, part] + [tail] * 2
    anywhere = pl.BlockSpec(memory_space=pl.ANY)
    packs = pl.pallas_call(
        functools.partial(pack_kernel, planes, pair_prefix.shape[1], held),
        out_shape=[jax.ShapeDtypeStruct((size, LANES), jnp.bfloat16) for size in sizes],
        in_specs=[anywhere] * len(sources),
        out_specs=[anywhere] * len(sizes),
        scratch_shapes=[pltpu.VMEM((size, LANES), jnp.bfloat16) for size in sizes]
        + [pltpu.VMEM(source.shape, source.dtype) for source in sources]
        + [pltpu.SemaphoreType.DMA((len(sources) + 1 + 2 * planes,))],
        compiler_params=pltpu.CompilerParams(vmem_limit_bytes=PACK_BYTES),
        cost_estimate=pl.CostEstimate(flops=2 ** 20, bytes_accessed=2 ** 12, transcendentals=0),
        name="pack",
    )(*sources)
    far = [swap(packs[k], k * PLANE) for k in range(2, planes)]
    near = swap(packs[planes + 1], PLANE)
    group, rest = join(far, part)
    handed = swap(rest, PLANE)
    relays = [packs[0][None], swap(packs[1], PLANE)[None], group]
    own, local = own_copy(relays[0], packs[planes])
    across = [swap(r, 2) for r in relays]
    relays[0] = own
    packs = [local, near, far[0], handed]
    far_beside = swap(after(relays[2], near), 1)
    beside = [swap(after(relays[0], far_beside), 1), swap(relays[1], 1), far_beside]
    corner = [swap(across[0], 1), swap(after(across[1], handed), 1), swap(across[2], 1)]
    early = 2 * PLANE
    far_slots = range(early, owners, PLANE)
    order = list(range(early)) + [k + n for n in (0, 1, 2) for k in far_slots]
    last = [k + 3 for k in far_slots]
    relays = [group[n] for n in range(2) for group in (relays, beside, across, corner)] + [relays[2], beside[2], across[2]]
    tiny = pl.CostEstimate(flops=0, bytes_accessed=2 ** 12, transcendentals=0)

    def sums_of(chosen, dtype):
        count = len(chosen)
        rows = count * pieces * rows_piece
        operands = relays[:early] + [packs[k] for k in chosen] + relays[early:]
        state, named, sums = pl.pallas_call(
            functools.partial(front_kernel, count, list(chosen).index(planes - 1) if planes - 1 in chosen else None, owners, order, blocks, pieces, rows_piece, held),
            out_shape=[
                jax.ShapeDtypeStruct((rows, 2 * part), jnp.bfloat16),
                jax.ShapeDtypeStruct((rows, LANES), jnp.float32),
                jax.ShapeDtypeStruct((rows, LANES), jnp.float32),
            ],
            in_specs=[vmem] * len(operands),
            out_specs=[vmem] * 3,
            scratch_shapes=[
                pltpu.VMEM((blocks, span, 2 * part), jnp.bfloat16),
                pltpu.VMEM((count, blocks * held * rows_piece, 2 * part), jnp.bfloat16),
                pltpu.VMEM((count, blocks * held * rows_piece, 2 * part), jnp.bfloat16),
                pltpu.VMEM((2 * part, len(order) * LANES), jnp.bfloat16),
            ],
            compiler_params=params,
            cost_estimate=tiny,
            name="front",
        )(*operands)
        return pl.pallas_call(
            functools.partial(last_kernel, last),
            out_shape=[jax.ShapeDtypeStruct((pieces, rows_piece, LANES), dtype)] * count,
            in_specs=[vmem] * 4,
            out_specs=[vmem] * count,
            scratch_shapes=[
                pltpu.VMEM((rows, LANES), jnp.float32),
                pltpu.VMEM((2 * part, len(last) * LANES), jnp.bfloat16),
            ],
            compiler_params=params,
            cost_estimate=tiny,
            name="last",
        )(named, state, sums, corner[2])

    sent = sums_of(range(1, planes), jnp.bfloat16)
    total = sums_of([0], jnp.float32)[0]
    for k in range(1, planes):
        total = total + swap(sent[k - 1], k * PLANE).astype(jnp.float32)
    return total


def by_owner(prefix, first_suffix, pair_prefix, pair_suffix, merge_count, suffix, routes, cap):
    pieces = pair_prefix.shape[0]
    merges = pair_prefix.shape[1]
    held_blocks = prefix.shape[0]
    rows_piece = prefix.shape[1]
    twice_width = prefix.shape[2]
    half_width = twice_width // 2
    first_count = first_suffix.shape[0]
    listed = routes.shape[1]
    owners = lax.axis_size("bits")
    slot_count = min(pieces, max(2, (2 * pieces * listed + owners - 1) // owners))
    live_mask = lax.broadcasted_iota(jnp.int32, (pieces, merges), 1) < merge_count[:, None]
    matches = (
        pair_suffix[:, :, None] == lax.broadcasted_iota(jnp.int32, (pieces, merges, first_count), 2)
    ) & live_mask[:, :, None]
    which_block = pair_prefix[:, :, None] == lax.broadcasted_iota(
        jnp.int32, (pieces, merges, held_blocks), 2
    )
    prefix_picks = jnp.einsum(
        "ika,ikp->iap", matches.astype(jnp.float32), which_block.astype(jnp.float32)
    ).astype(jnp.bfloat16)
    selected = jnp.einsum(
        "iap,prc->airc", prefix_picks, prefix, preferred_element_type=jnp.float32
    ).astype(jnp.bfloat16)
    selected = selected.reshape(first_count, pieces * rows_piece, twice_width)
    portion = lax.all_gather(first_suffix, "bits", axis=2, tiled=True)
    count_rows = portion.shape[2]
    real_cols = lax.slice_in_dim(selected, 0, count_rows, axis=2)
    imag_cols = lax.dynamic_slice_in_dim(selected, half_width, count_rows, 2)
    left_side = jnp.concatenate([real_cols, imag_cols], axis=2)
    upper_half = jnp.concatenate([portion[:, 0], portion[:, 1]], axis=2)
    lower_half = jnp.concatenate([-portion[:, 1], portion[:, 0]], axis=2)
    right_side = jnp.concatenate([upper_half, lower_half], axis=1)
    state_rows = jnp.einsum(
        "arc,acw->rw", left_side, right_side, preferred_element_type=jnp.float32
    )
    state_rows = state_rows.astype(jnp.bfloat16).reshape(pieces, rows_piece, twice_width)
    named_by = jnp.sum(
        (routes[:, :, None] == lax.broadcasted_iota(jnp.int32, (pieces, listed, owners), 2)).astype(
            jnp.int32
        ),
        axis=1,
    )
    slot_rank = jnp.cumsum(named_by, axis=0) - named_by
    slot_hit = (
        slot_rank[:, :, None] == lax.broadcasted_iota(jnp.int32, (pieces, owners, slot_count), 2)
    ) & (named_by[:, :, None] > 0)
    dispatch = jnp.transpose(slot_hit, (1, 2, 0)).astype(jnp.bfloat16)
    outgoing = jnp.einsum(
        "dmi,irc->dmrc", dispatch, state_rows, preferred_element_type=jnp.float32
    ).astype(jnp.bfloat16)
    own_form = complex_form(suffix[0])
    cap_form = complex_form(cap)
    products = jnp.einsum(
        "smrc,cw->smrw",
        lax.all_to_all(outgoing, "bits", split_axis=0, concat_axis=0, tiled=True),
        own_form,
        preferred_element_type=jnp.float32,
    ).astype(jnp.bfloat16)
    capped_terms = jnp.einsum(
        "smrw,wv->smrv", products, cap_form, preferred_element_type=jnp.float32
    )
    returned = lax.all_to_all(
        capped_terms.astype(jnp.bfloat16), "bits", split_axis=0, concat_axis=0, tiled=True
    ).astype(capped_terms.dtype)
    return jnp.einsum(
        "dmi,dmrv->irv", dispatch.astype(jnp.float32), returned, precision=HIGHEST_PRECISION
    )


def on_device(*args):
    prefix, first_suffix, pair_prefix, routes, cap = args[0], args[1], args[2], args[6], args[7]
    owners = lax.axis_size("bits")
    planes = owners // PLANE
    depth, width = first_suffix.shape[2:]
    pieces = pair_prefix.shape[0]
    fits = (
        planes == 4
        and owners == planes * PLANE
        and width == owners * depth
        and width % (planes // 2 * LANES) == 0
        and width // 2 % LANES == 0
        and 2 * cap.shape[2] == LANES
        and depth % 16 == 0
        and prefix.shape[1] % 16 == 0
        and pieces <= HEAD
        and first_suffix.shape[0] * prefix.shape[0] <= owners
        and 3 * owners <= LANES
    )
    return in_planes(*args) if fits else by_owner(*args)


def solution(mesh):
    return jax.shard_map(
        on_device,
        mesh=mesh,
        in_specs=(
            P(("grp", "bits"), None, None),
            P("grp", None, "bits", None),
            P(("grp", "bits"), None),
            P(("grp", "bits"), None),
            P(("grp", "bits")),
            P(("grp", "bits"), None, None, None),
            P(("grp", "bits"), None),
            P(),
        ),
        out_specs=P(("grp", "bits"), None, None),
        check_vma=False,
    )
```

```python
import functools

import jax
import jax.numpy as jnp
from jax import lax
from jax.experimental import pallas as pl
from jax.experimental.pallas import tpu as pltpu
from jax.sharding import PartitionSpec as P

HIGHEST_PRECISION = lax.Precision.HIGHEST
LANES = 128
PLANE = 4
VMEM_BYTES = 32 * 1024 * 1024
HEAD = 16
PACK_BYTES = 60 * 1024 * 1024


def complex_form(blocks):
    real_part = blocks[..., 0, :, :]
    imag_part = blocks[..., 1, :, :]
    upper_half = jnp.concatenate([real_part, imag_part], axis=-1)
    lower_half = jnp.concatenate([-imag_part, real_part], axis=-1)
    return jnp.concatenate([upper_half, lower_half], axis=-2)


def swap(x, bit):
    owners = lax.axis_size("bits")
    return lax.ppermute(x, "bits", [(i, i ^ bit) for i in range(owners)])


def after(x, others):
    return lax.optimization_barrier((x, others))[0]


def pack_kernel(planes, merges, held, *refs):
    sources, outs, stages, copied = refs[:8], refs[8:10 + planes], refs[10 + planes:12 + 2 * planes], refs[12 + 2 * planes:-1]
    sems = refs[-1]
    first_ref, prefix_ref, suffix_ref, cap_ref, pair_prefix_ref, pair_suffix_ref, count_ref, routes_ref = copied
    width = suffix_ref.shape[1]
    rows, twice_width = prefix_ref.shape
    part, span, slots = width // 2, width // (planes // 2), planes * PLANE
    me = lax.axis_index("bits")
    plane = me // PLANE
    inward = [pltpu.make_async_copy(source, ref, sems.at[n]) for n, (source, ref) in enumerate(zip(sources, copied))]
    for copy in inward:
        copy.start()
    outward = []

    def send(k, row, size):
        there = pl.ds(row, size)
        sem = sems.at[len(sources) + len(outward)]
        outward.append(pltpu.make_async_copy(stages[k].at[there, :], outs[k].at[there, :], sem))
        outward[-1].start()

    lows = [plane % 2 ^ k % 2 for k in range(planes)]
    firsts = [first_ref.shape[0] * (part // LANES) if k < 2 else 0 for k in range(planes)]
    inward[0].wait()
    for k in range(2):
        for n in range(part // LANES):
            columns = pl.ds(pl.multiple_of(lows[k] * part + n * LANES, LANES), LANES)
            stages[k][n * first_ref.shape[0]:(n + 1) * first_ref.shape[0], :] = first_ref[:, columns]
        send(k, 0, firsts[k])
    for copy in inward[4:]:
        copy.wait()
    pieces = routes_ref.shape[0]
    lane = lax.broadcasted_iota(jnp.int32, (pieces, LANES), 1)
    named = [jnp.zeros((pieces, LANES), jnp.int32)] * planes
    for slot in range(slots):
        hits = jnp.sum((routes_ref[...] == slot ^ me).astype(jnp.int32), axis=1, keepdims=True)
        named = [jnp.where(lane == slot ^ k * PLANE, hits, there) for k, there in enumerate(named)]
        handed_on = 2 * slots + (slot ^ (planes - 1) * PLANE)
        named[planes // 2] = jnp.where(lane == handed_on, hits, named[planes // 2])
    own_lane = lax.broadcasted_iota(jnp.int32, (pieces, pieces), 0) == lax.broadcasted_iota(jnp.int32, (pieces, pieces), 1)
    picks = jnp.zeros((pieces, LANES), jnp.int32)
    for m in range(merges):
        pick = pair_suffix_ref[m:m + 1, :] * held + pair_prefix_ref[m:m + 1, :]
        pick = jnp.where(m < count_ref[...], slots + pick, -1)
        pick = jnp.sum(jnp.where(own_lane, jnp.broadcast_to(pick, (pieces, pieces)), 0), axis=1, keepdims=True)
        picks += (lane == pick).astype(jnp.int32)
    inward[1].wait()
    for k in range(planes - 1):
        message, start = (planes + k, 0) if k < 2 else (k, part)
        stage, high = stages[message], plane // 2 ^ k // 2
        rest = jnp.zeros((HEAD - pieces, LANES), jnp.float32)
        routing = jnp.concatenate([(named[k] + picks).astype(jnp.float32), rest], axis=0)
        stage[start:start + HEAD, :] = routing.astype(jnp.bfloat16)
        row = start + HEAD
        for side in range(0, twice_width, width):
            for n in range(0, span, LANES):
                columns = pl.ds(pl.multiple_of(high * span + (side + n), LANES), LANES)
                stage[row:row + rows, :] = prefix_ref[:, columns]
                row += rows
        send(message, start, row - start)
    inward[3].wait()
    upper = jnp.concatenate([cap_ref[0], cap_ref[1]], axis=0)
    lower = jnp.concatenate([-cap_ref[1], cap_ref[0]], axis=0)
    turned = (((1,), (1,)), ((), ()))
    inward[2].wait()
    for low in range(2):
        there = pl.ds(pl.multiple_of((plane % 2 ^ low) * part, part), part)
        both = lax.dot_general(suffix_ref[0, there, :], upper, turned, preferred_element_type=jnp.float32)
        both += lax.dot_general(suffix_ref[1, there, :], lower, turned, preferred_element_type=jnp.float32)
        both = both.astype(jnp.bfloat16)
        for k in range(low, planes, 2):
            stages[k][firsts[k]:firsts[k] + part, :] = both
            send(k, firsts[k], part)
    for copy in outward:
        copy.wait()


def own_kernel(*refs):
    count = len(refs) // 2
    for source, out in zip(refs[:count], refs[count:]):
        out[...] = source[...]


def own_copy(*arrays):
    vmem = pl.BlockSpec(memory_space=pltpu.VMEM)
    return pl.pallas_call(
        own_kernel,
        out_shape=[jax.ShapeDtypeStruct(a.shape, a.dtype) for a in arrays],
        in_specs=[vmem] * len(arrays),
        out_specs=[vmem] * len(arrays),
        compiler_params=pltpu.CompilerParams(vmem_limit_bytes=VMEM_BYTES),
        cost_estimate=pl.CostEstimate(flops=0, bytes_accessed=2 ** 12, transcendentals=0),
        name="own",
    )(*arrays)


def join_kernel(*refs):
    *packs, group, rest = refs
    size = group.shape[1]
    for k, pack in enumerate(packs):
        group[k] = pack[:size]
    rest[...] = packs[0][size:]


def join(packs, size):
    vmem = pl.BlockSpec(memory_space=pltpu.VMEM)
    return pl.pallas_call(
        join_kernel,
        out_shape=[
            jax.ShapeDtypeStruct((len(packs), size) + packs[0].shape[1:], packs[0].dtype),
            jax.ShapeDtypeStruct((packs[0].shape[0] - size,) + packs[0].shape[1:], packs[0].dtype),
        ],
        in_specs=[vmem] * len(packs),
        out_specs=[vmem] * 2,
        compiler_params=pltpu.CompilerParams(vmem_limit_bytes=VMEM_BYTES),
        cost_estimate=pl.CostEstimate(flops=0, bytes_accessed=2 ** 12, transcendentals=0),
        name="join",
    )(*packs)


def front_kernel(planes, handed_on, slots, order, blocks, pieces, rows_piece, held, *refs):
    relays, packs = refs[:2 * PLANE], refs[2 * PLANE:2 * PLANE + planes]
    closing = refs[2 * PLANE + planes:-6]
    state, named, sums, forms, parts, wide = refs[-6:]
    me = lax.axis_index("bits")
    span, twice_part = forms.shape[1:]
    depth = span // (2 * PLANE)
    part = twice_part // 2
    rows = held * rows_piece
    locals_ = []
    tail = HEAD + 2 * (span // LANES) * rows
    for k in range(planes):
        first = packs[k].shape[0] - tail
        numbers = packs[k][first:first + HEAD].astype(jnp.float32)
        if k == handed_on:
            lane = lax.broadcasted_iota(jnp.int32, numbers.shape, 1)
            numbers = jnp.where(lane < slots, pltpu.roll(numbers, LANES - 2 * slots, 1), numbers)
        for n in range(pieces):
            here = slice((k * pieces + n) * rows_piece, (k * pieces + n + 1) * rows_piece)
            named[here, :] = jnp.broadcast_to(numbers[n:n + 1], (rows_piece, LANES))
        locals_.append(packs[k].at[first + HEAD:first + tail])
    shape = (LANES, blocks * rows)
    spread = lax.broadcasted_iota(jnp.int32, shape, 0) - slots == lax.broadcasted_iota(jnp.int32, shape, 1) // rows_piece
    spread = spread.astype(jnp.float32).astype(jnp.bfloat16)
    shape = (planes * pieces * rows_piece, blocks * rows)
    same_row = lax.broadcasted_iota(jnp.int32, shape, 0) % rows_piece == lax.broadcasted_iota(jnp.int32, shape, 1) % rows_piece
    picks = jnp.dot(named[...].astype(jnp.bfloat16), spread, preferred_element_type=jnp.float32)
    picks = jnp.where(same_row, picks, 0.0).astype(jnp.bfloat16)
    for j in range(2 * PLANE):
        there = pl.ds(pl.multiple_of((me ^ j) % (2 * PLANE) * depth, depth), depth)
        for a in range(blocks):
            for c in range(2):
                for n in range(part // LANES):
                    row = ((n * blocks + a) * 2 + c) * depth
                    columns = slice(c * part + n * LANES, c * part + (n + 1) * LANES)
                    forms[a, there, columns] = relays[j][0, row:row + depth, :]
    left = []
    for c in range(2):
        for k in range(planes):
            columns = []
            for n in range(span // LANES):
                first = (c * (span // LANES) + n) * rows
                columns.append(locals_[k][first:first + rows])
            left.append(jnp.concatenate(columns, axis=1))
    left = jnp.concatenate(left, axis=0)
    for a in range(blocks):
        both = jnp.dot(left, forms[a], preferred_element_type=jnp.float32)
        real, imag = both[:planes * rows], both[planes * rows:]
        product = jnp.concatenate([real[:, :part] - imag[:, part:], real[:, part:] + imag[:, :part]], axis=1)
        rounded = product.astype(jnp.bfloat16)
        rest = (product - rounded.astype(jnp.float32)).astype(jnp.bfloat16)
        for k in range(planes):
            parts[k, a * rows:(a + 1) * rows, :] = rounded[k * rows:(k + 1) * rows]
            parts[k, (blocks + a) * rows:(blocks + a + 1) * rows, :] = rest[k * rows:(k + 1) * rows]
    size = pieces * rows_piece
    for k in range(planes):
        pick = picks[k * size:(k + 1) * size]
        total = jnp.dot(jnp.concatenate([pick, pick], axis=1), parts[k], preferred_element_type=jnp.float32)
        state[k * size:(k + 1) * size, :] = total.astype(jnp.bfloat16)
    close(order, named, state, relays + closing, sums, wide)


def close(order, named, state, relays, sums, wide):
    part, rows = wide.shape[0] // 2, state.shape[0]
    lane = lax.broadcasted_iota(jnp.int32, (part, LANES), 1)
    sign = jnp.where(lane < LANES // 2, -1.0, 1.0).astype(jnp.bfloat16)
    slot = 0
    for relay in relays:
        for k in range(relay.shape[0]):
            real_rows = relay[k, relay.shape[1] - part:]
            turned = pltpu.roll(real_rows, LANES // 2, 1) * sign
            wide[:part, slot * LANES:(slot + 1) * LANES] = real_rows
            wide[part:, slot * LANES:(slot + 1) * LANES] = turned
            slot += 1
    for j in range(0, len(order), 4):
        both = jnp.dot(state[...], wide[:, j * LANES:min(j + 4, len(order)) * LANES], preferred_element_type=jnp.float32)
        for side, slot in enumerate(order[j:j + 4]):
            factor = jnp.broadcast_to(named[:, slot:slot + 1], (rows, LANES))
            add = both[:, side * LANES:(side + 1) * LANES] * factor
            sums[...] = add if slot == 0 else sums[...] + add


def last_kernel(order, named, state, sums_in, relay, *refs):
    *outs, sums, wide = refs
    sums[...] = sums_in[...]
    close(order, named, state, [relay], sums, wide)
    size = sums.shape[0] // len(outs)
    for k, out in enumerate(outs):
        out[...] = sums[k * size:(k + 1) * size, :].reshape(out.shape).astype(out.dtype)


def in_planes(prefix, first_suffix, pair_prefix, pair_suffix, merge_count, suffix, routes, cap):
    owners = lax.axis_size("bits")
    planes = owners // PLANE
    pieces = pair_prefix.shape[0]
    held, rows_piece, twice_width = prefix.shape
    blocks, _, depth, width = first_suffix.shape
    part, span = width // 2, width // (planes // 2)
    vmem = pl.BlockSpec(memory_space=pltpu.VMEM)
    params = pltpu.CompilerParams(vmem_limit_bytes=VMEM_BYTES)
    relayed = blocks * 2 * depth * (part // LANES) + part
    tail = HEAD + 2 * (span // LANES) * held * rows_piece
    sources = (
        first_suffix.reshape(blocks * 2 * depth, width),
        prefix.reshape(held * rows_piece, twice_width),
        suffix[0],
        jnp.swapaxes(cap, 1, 2),
        pair_prefix.T,
        pair_suffix.T,
        merge_count[None],
        routes,
    )
    sizes = [relayed] * 2 + [part + tail, part] + [tail] * 2
    anywhere = pl.BlockSpec(memory_space=pl.ANY)
    packs = pl.pallas_call(
        functools.partial(pack_kernel, planes, pair_prefix.shape[1], held),
        out_shape=[jax.ShapeDtypeStruct((size, LANES), jnp.bfloat16) for size in sizes],
        in_specs=[anywhere] * len(sources),
        out_specs=[anywhere] * len(sizes),
        scratch_shapes=[pltpu.VMEM((size, LANES), jnp.bfloat16) for size in sizes]
        + [pltpu.VMEM(source.shape, source.dtype) for source in sources]
        + [pltpu.SemaphoreType.DMA((len(sources) + 1 + 2 * planes,))],
        compiler_params=pltpu.CompilerParams(vmem_limit_bytes=PACK_BYTES),
        cost_estimate=pl.CostEstimate(flops=2 ** 20, bytes_accessed=2 ** 12, transcendentals=0),
        name="pack",
    )(*sources)
    far = [swap(packs[k], k * PLANE) for k in range(2, planes)]
    near = swap(packs[planes + 1], PLANE)
    group, rest = join(far, part)
    handed = swap(rest, PLANE)
    relays = [packs[0][None], swap(packs[1], PLANE)[None], group]
    own, local = own_copy(relays[0], packs[planes])
    across = [swap(r, 2) for r in relays]
    relays[0] = own
    packs = [local, near, far[0], handed]
    beside = [swap(relays[0], 1), None, swap(after(relays[2], near), 1)]
    beside[1] = swap(after(relays[1], beside[2]), 1)
    corner = [swap(across[0], 1), swap(after(across[1], handed), 1), swap(across[2], 1)]
    early = 2 * PLANE
    far_slots = range(early, owners, PLANE)
    order = list(range(early)) + [k + n for n in (0, 1, 2) for k in far_slots]
    last = [k + 3 for k in far_slots]
    relays = [group[n] for n in range(2) for group in (relays, beside, across, corner)] + [relays[2], beside[2], across[2]]
    tiny = pl.CostEstimate(flops=0, bytes_accessed=2 ** 12, transcendentals=0)

    def sums_of(chosen, dtype):
        count = len(chosen)
        rows = count * pieces * rows_piece
        operands = relays[:early] + [packs[k] for k in chosen] + relays[early:]
        state, named, sums = pl.pallas_call(
            functools.partial(front_kernel, count, list(chosen).index(planes - 1) if planes - 1 in chosen else None, owners, order, blocks, pieces, rows_piece, held),
            out_shape=[
                jax.ShapeDtypeStruct((rows, 2 * part), jnp.bfloat16),
                jax.ShapeDtypeStruct((rows, LANES), jnp.float32),
                jax.ShapeDtypeStruct((rows, LANES), jnp.float32),
            ],
            in_specs=[vmem] * len(operands),
            out_specs=[vmem] * 3,
            scratch_shapes=[
                pltpu.VMEM((blocks, span, 2 * part), jnp.bfloat16),
                pltpu.VMEM((count, 2 * blocks * held * rows_piece, 2 * part), jnp.bfloat16),
                pltpu.VMEM((2 * part, len(order) * LANES), jnp.bfloat16),
            ],
            compiler_params=params,
            cost_estimate=tiny,
            name="front",
        )(*operands)
        return pl.pallas_call(
            functools.partial(last_kernel, last),
            out_shape=[jax.ShapeDtypeStruct((pieces, rows_piece, LANES), dtype)] * count,
            in_specs=[vmem] * 4,
            out_specs=[vmem] * count,
            scratch_shapes=[
                pltpu.VMEM((rows, LANES), jnp.float32),
                pltpu.VMEM((2 * part, len(last) * LANES), jnp.bfloat16),
            ],
            compiler_params=params,
            cost_estimate=tiny,
            name="last",
        )(named, state, sums, corner[2])

    sent = sums_of(range(1, planes), jnp.bfloat16)
    total = sums_of([0], jnp.float32)[0]
    for k in range(1, planes):
        total = total + swap(sent[k - 1], k * PLANE).astype(jnp.float32)
    return total


def by_owner(prefix, first_suffix, pair_prefix, pair_suffix, merge_count, suffix, routes, cap):
    pieces = pair_prefix.shape[0]
    merges = pair_prefix.shape[1]
    held_blocks = prefix.shape[0]
    rows_piece = prefix.shape[1]
    twice_width = prefix.shape[2]
    half_width = twice_width // 2
    first_count = first_suffix.shape[0]
    listed = routes.shape[1]
    owners = lax.axis_size("bits")
    slot_count = min(pieces, max(2, (2 * pieces * listed + owners - 1) // owners))
    live_mask = lax.broadcasted_iota(jnp.int32, (pieces, merges), 1) < merge_count[:, None]
    matches = (
        pair_suffix[:, :, None] == lax.broadcasted_iota(jnp.int32, (pieces, merges, first_count), 2)
    ) & live_mask[:, :, None]
    which_block = pair_prefix[:, :, None] == lax.broadcasted_iota(
        jnp.int32, (pieces, merges, held_blocks), 2
    )
    prefix_picks = jnp.einsum(
        "ika,ikp->iap", matches.astype(jnp.float32), which_block.astype(jnp.float32)
    ).astype(jnp.bfloat16)
    selected = jnp.einsum(
        "iap,prc->airc", prefix_picks, prefix, preferred_element_type=jnp.float32
    ).astype(jnp.bfloat16)
    selected = selected.reshape(first_count, pieces * rows_piece, twice_width)
    portion = lax.all_gather(first_suffix, "bits", axis=2, tiled=True)
    count_rows = portion.shape[2]
    real_cols = lax.slice_in_dim(selected, 0, count_rows, axis=2)
    imag_cols = lax.dynamic_slice_in_dim(selected, half_width, count_rows, 2)
    left_side = jnp.concatenate([real_cols, imag_cols], axis=2)
    upper_half = jnp.concatenate([portion[:, 0], portion[:, 1]], axis=2)
    lower_half = jnp.concatenate([-portion[:, 1], portion[:, 0]], axis=2)
    right_side = jnp.concatenate([upper_half, lower_half], axis=1)
    state_rows = jnp.einsum(
        "arc,acw->rw", left_side, right_side, preferred_element_type=jnp.float32
    )
    state_rows = state_rows.astype(jnp.bfloat16).reshape(pieces, rows_piece, twice_width)
    named_by = jnp.sum(
        (routes[:, :, None] == lax.broadcasted_iota(jnp.int32, (pieces, listed, owners), 2)).astype(
            jnp.int32
        ),
        axis=1,
    )
    slot_rank = jnp.cumsum(named_by, axis=0) - named_by
    slot_hit = (
        slot_rank[:, :, None] == lax.broadcasted_iota(jnp.int32, (pieces, owners, slot_count), 2)
    ) & (named_by[:, :, None] > 0)
    dispatch = jnp.transpose(slot_hit, (1, 2, 0)).astype(jnp.bfloat16)
    outgoing = jnp.einsum(
        "dmi,irc->dmrc", dispatch, state_rows, preferred_element_type=jnp.float32
    ).astype(jnp.bfloat16)
    own_form = complex_form(suffix[0])
    cap_form = complex_form(cap)
    products = jnp.einsum(
        "smrc,cw->smrw",
        lax.all_to_all(outgoing, "bits", split_axis=0, concat_axis=0, tiled=True),
        own_form,
        preferred_element_type=jnp.float32,
    ).astype(jnp.bfloat16)
    capped_terms = jnp.einsum(
        "smrw,wv->smrv", products, cap_form, preferred_element_type=jnp.float32
    )
    returned = lax.all_to_all(
        capped_terms.astype(jnp.bfloat16), "bits", split_axis=0, concat_axis=0, tiled=True
    ).astype(capped_terms.dtype)
    return jnp.einsum(
        "dmi,dmrv->irv", dispatch.astype(jnp.float32), returned, precision=HIGHEST_PRECISION
    )


def on_device(*args):
    prefix, first_suffix, pair_prefix, routes, cap = args[0], args[1], args[2], args[6], args[7]
    owners = lax.axis_size("bits")
    planes = owners // PLANE
    depth, width = first_suffix.shape[2:]
    pieces = pair_prefix.shape[0]
    fits = (
        planes == 4
        and owners == planes * PLANE
        and width == owners * depth
        and width % (planes // 2 * LANES) == 0
        and width // 2 % LANES == 0
        and 2 * cap.shape[2] == LANES
        and depth % 16 == 0
        and prefix.shape[1] % 16 == 0
        and pieces <= HEAD
        and first_suffix.shape[0] * prefix.shape[0] <= owners
        and 3 * owners <= LANES
    )
    return in_planes(*args) if fits else by_owner(*args)


def solution(mesh):
    return jax.shard_map(
        on_device,
        mesh=mesh,
        in_specs=(
            P(("grp", "bits"), None, None),
            P("grp", None, "bits", None),
            P(("grp", "bits"), None),
            P(("grp", "bits"), None),
            P(("grp", "bits")),
            P(("grp", "bits"), None, None, None),
            P(("grp", "bits"), None),
            P(),
        ),
        out_specs=P(("grp", "bits"), None, None),
        check_vma=False,
    )
```

```python
import functools

import jax
import jax.numpy as jnp
from jax import lax
from jax.experimental import pallas as pl
from jax.experimental.pallas import tpu as pltpu
from jax.sharding import PartitionSpec as P

HIGHEST_PRECISION = lax.Precision.HIGHEST
LANES = 128
PLANE = 4
VMEM_BYTES = 32 * 1024 * 1024
HEAD = 16
PACK_BYTES = 60 * 1024 * 1024


def complex_form(blocks):
    real_part = blocks[..., 0, :, :]
    imag_part = blocks[..., 1, :, :]
    upper_half = jnp.concatenate([real_part, imag_part], axis=-1)
    lower_half = jnp.concatenate([-imag_part, real_part], axis=-1)
    return jnp.concatenate([upper_half, lower_half], axis=-2)


def swap(x, bit):
    owners = lax.axis_size("bits")
    return lax.ppermute(x, "bits", [(i, i ^ bit) for i in range(owners)])


def after(x, others):
    return lax.optimization_barrier((x, others))[0]


def pack_kernel(planes, merges, held, *refs):
    sources, outs, stages, copied = refs[:8], refs[8:10 + planes], refs[10 + planes:12 + 2 * planes], refs[12 + 2 * planes:-1]
    sems = refs[-1]
    first_ref, prefix_ref, suffix_ref, cap_ref, pair_prefix_ref, pair_suffix_ref, count_ref, routes_ref = copied
    width = suffix_ref.shape[1]
    rows, twice_width = prefix_ref.shape
    part, span, slots = width // 2, width // (planes // 2), planes * PLANE
    me = lax.axis_index("bits")
    plane = me // PLANE
    inward = [pltpu.make_async_copy(source, ref, sems.at[n]) for n, (source, ref) in enumerate(zip(sources, copied))]
    for copy in inward:
        copy.start()
    outward = []

    def send(k, row, size):
        there = pl.ds(row, size)
        sem = sems.at[len(sources) + len(outward)]
        outward.append(pltpu.make_async_copy(stages[k].at[there, :], outs[k].at[there, :], sem))
        outward[-1].start()

    lows = [plane % 2 ^ k % 2 for k in range(planes)]
    firsts = [first_ref.shape[0] * (part // LANES) if k < 2 else 0 for k in range(planes)]
    inward[0].wait()
    for k in range(2):
        for n in range(part // LANES):
            columns = pl.ds(pl.multiple_of(lows[k] * part + n * LANES, LANES), LANES)
            stages[k][n * first_ref.shape[0]:(n + 1) * first_ref.shape[0], :] = first_ref[:, columns]
        send(k, 0, firsts[k])
    for copy in inward[4:]:
        copy.wait()
    pieces = routes_ref.shape[0]
    lane = lax.broadcasted_iota(jnp.int32, (pieces, LANES), 1)
    named = [jnp.zeros((pieces, LANES), jnp.int32)] * planes
    for slot in range(slots):
        hits = jnp.sum((routes_ref[...] == slot ^ me).astype(jnp.int32), axis=1, keepdims=True)
        named = [jnp.where(lane == slot ^ k * PLANE, hits, there) for k, there in enumerate(named)]
        handed_on = 2 * slots + (slot ^ (planes - 1) * PLANE)
        named[planes // 2] = jnp.where(lane == handed_on, hits, named[planes // 2])
    own_lane = lax.broadcasted_iota(jnp.int32, (pieces, pieces), 0) == lax.broadcasted_iota(jnp.int32, (pieces, pieces), 1)
    picks = jnp.zeros((pieces, LANES), jnp.int32)
    for m in range(merges):
        pick = pair_suffix_ref[m:m + 1, :] * held + pair_prefix_ref[m:m + 1, :]
        pick = jnp.where(m < count_ref[...], slots + pick, -1)
        pick = jnp.sum(jnp.where(own_lane, jnp.broadcast_to(pick, (pieces, pieces)), 0), axis=1, keepdims=True)
        picks += (lane == pick).astype(jnp.int32)
    inward[1].wait()
    for k in range(planes - 1):
        message, start = (planes + k, 0) if k < 2 else (k, part)
        stage, high = stages[message], plane // 2 ^ k // 2
        rest = jnp.zeros((HEAD - pieces, LANES), jnp.float32)
        routing = jnp.concatenate([(named[k] + picks).astype(jnp.float32), rest], axis=0)
        stage[start:start + HEAD, :] = routing.astype(jnp.bfloat16)
        row = start + HEAD
        for side in range(0, twice_width, width):
            for n in range(0, span, LANES):
                columns = pl.ds(pl.multiple_of(high * span + (side + n), LANES), LANES)
                stage[row:row + rows, :] = prefix_ref[:, columns]
                row += rows
        send(message, start, row - start)
    inward[3].wait()
    upper = jnp.concatenate([cap_ref[0], cap_ref[1]], axis=0)
    lower = jnp.concatenate([-cap_ref[1], cap_ref[0]], axis=0)
    turned = (((1,), (1,)), ((), ()))
    inward[2].wait()
    for low in range(2):
        there = pl.ds(pl.multiple_of((plane % 2 ^ low) * part, part), part)
        both = lax.dot_general(suffix_ref[0, there, :], upper, turned, preferred_element_type=jnp.float32)
        both += lax.dot_general(suffix_ref[1, there, :], lower, turned, preferred_element_type=jnp.float32)
        both = both.astype(jnp.bfloat16)
        for k in range(low, planes, 2):
            stages[k][firsts[k]:firsts[k] + part, :] = both
            send(k, firsts[k], part)
    for copy in outward:
        copy.wait()


def own_kernel(*refs):
    count = len(refs) // 2
    for source, out in zip(refs[:count], refs[count:]):
        out[...] = source[...]


def own_copy(*arrays):
    vmem = pl.BlockSpec(memory_space=pltpu.VMEM)
    return pl.pallas_call(
        own_kernel,
        out_shape=[jax.ShapeDtypeStruct(a.shape, a.dtype) for a in arrays],
        in_specs=[vmem] * len(arrays),
        out_specs=[vmem] * len(arrays),
        compiler_params=pltpu.CompilerParams(vmem_limit_bytes=VMEM_BYTES),
        cost_estimate=pl.CostEstimate(flops=0, bytes_accessed=2 ** 12, transcendentals=0),
        name="own",
    )(*arrays)


def join_kernel(*refs):
    *packs, group, rest = refs
    size = group.shape[1]
    for k, pack in enumerate(packs):
        group[k] = pack[:size]
    rest[...] = packs[0][size:]


def join(packs, size):
    vmem = pl.BlockSpec(memory_space=pltpu.VMEM)
    return pl.pallas_call(
        join_kernel,
        out_shape=[
            jax.ShapeDtypeStruct((len(packs), size) + packs[0].shape[1:], packs[0].dtype),
            jax.ShapeDtypeStruct((packs[0].shape[0] - size,) + packs[0].shape[1:], packs[0].dtype),
        ],
        in_specs=[vmem] * len(packs),
        out_specs=[vmem] * 2,
        compiler_params=pltpu.CompilerParams(vmem_limit_bytes=VMEM_BYTES),
        cost_estimate=pl.CostEstimate(flops=0, bytes_accessed=2 ** 12, transcendentals=0),
        name="join",
    )(*packs)


def front_kernel(planes, handed_on, slots, order, blocks, pieces, rows_piece, held, *refs):
    relays, packs = refs[:2 * PLANE], refs[2 * PLANE:2 * PLANE + planes]
    closing = refs[2 * PLANE + planes:-7]
    state, named, sums, forms, high, low, wide = refs[-7:]
    me = lax.axis_index("bits")
    span, twice_part = forms.shape[1:]
    depth = span // (2 * PLANE)
    part = twice_part // 2
    rows = held * rows_piece
    locals_ = []
    tail = HEAD + 2 * (span // LANES) * rows
    for k in range(planes):
        first = packs[k].shape[0] - tail
        numbers = packs[k][first:first + HEAD].astype(jnp.float32)
        if k == handed_on:
            lane = lax.broadcasted_iota(jnp.int32, numbers.shape, 1)
            numbers = jnp.where(lane < slots, pltpu.roll(numbers, LANES - 2 * slots, 1), numbers)
        for n in range(pieces):
            here = slice((k * pieces + n) * rows_piece, (k * pieces + n + 1) * rows_piece)
            named[here, :] = jnp.broadcast_to(numbers[n:n + 1], (rows_piece, LANES))
        locals_.append(packs[k].at[first + HEAD:first + tail])
    shape = (LANES, blocks * rows)
    spread = lax.broadcasted_iota(jnp.int32, shape, 0) - slots == lax.broadcasted_iota(jnp.int32, shape, 1) // rows_piece
    spread = spread.astype(jnp.float32).astype(jnp.bfloat16)
    shape = (planes * pieces * rows_piece, blocks * rows)
    same_row = lax.broadcasted_iota(jnp.int32, shape, 0) % rows_piece == lax.broadcasted_iota(jnp.int32, shape, 1) % rows_piece
    picks = jnp.dot(named[...].astype(jnp.bfloat16), spread, preferred_element_type=jnp.float32)
    picks = jnp.where(same_row, picks, 0.0).astype(jnp.bfloat16)
    for j in range(2 * PLANE):
        there = pl.ds(pl.multiple_of((me ^ j) % (2 * PLANE) * depth, depth), depth)
        for a in range(blocks):
            for c in range(2):
                for n in range(part // LANES):
                    row = ((n * blocks + a) * 2 + c) * depth
                    columns = slice(c * part + n * LANES, c * part + (n + 1) * LANES)
                    forms[a, there, columns] = relays[j][0, row:row + depth, :]
    left = []
    for c in range(2):
        for k in range(planes):
            columns = []
            for n in range(span // LANES):
                first = (c * (span // LANES) + n) * rows
                columns.append(locals_[k][first:first + rows])
            left.append(jnp.concatenate(columns, axis=1))
    left = jnp.concatenate(left, axis=0)
    for a in range(blocks):
        both = jnp.dot(left, forms[a], preferred_element_type=jnp.float32)
        real, imag = both[:planes * rows], both[planes * rows:]
        product = jnp.concatenate([real[:, :part] - imag[:, part:], real[:, part:] + imag[:, :part]], axis=1)
        rounded = product.astype(jnp.bfloat16)
        rest = (product - rounded.astype(jnp.float32)).astype(jnp.bfloat16)
        for k in range(planes):
            high[k, a * rows:(a + 1) * rows, :] = rounded[k * rows:(k + 1) * rows]
            low[k, a * rows:(a + 1) * rows, :] = rest[k * rows:(k + 1) * rows]
    size = pieces * rows_piece
    for k in range(planes):
        pick = picks[k * size:(k + 1) * size]
        total = jnp.dot(pick, high[k], preferred_element_type=jnp.float32)
        total += jnp.dot(pick, low[k], preferred_element_type=jnp.float32)
        state[k * size:(k + 1) * size, :] = total.astype(jnp.bfloat16)
    close(order, named, state, relays + closing, sums, wide)


def close(order, named, state, relays, sums, wide):
    part, rows = wide.shape[0] // 2, state.shape[0]
    lane = lax.broadcasted_iota(jnp.int32, (part, LANES), 1)
    sign = jnp.where(lane < LANES // 2, -1.0, 1.0).astype(jnp.bfloat16)
    slot = 0
    for relay in relays:
        for k in range(relay.shape[0]):
            real_rows = relay[k, relay.shape[1] - part:]
            turned = pltpu.roll(real_rows, LANES // 2, 1) * sign
            wide[:part, slot * LANES:(slot + 1) * LANES] = real_rows
            wide[part:, slot * LANES:(slot + 1) * LANES] = turned
            slot += 1
    for j in range(0, slot, 2):
        both = jnp.dot(state[...], wide[:, j * LANES:(j + 2) * LANES], preferred_element_type=jnp.float32)
        for side, slot in enumerate(order[j:j + 2]):
            factor = jnp.broadcast_to(named[:, slot:slot + 1], (rows, LANES))
            add = both[:, side * LANES:(side + 1) * LANES] * factor
            sums[...] = add if slot == 0 else sums[...] + add


def last_kernel(order, named, state, sums_in, relay, *refs):
    *outs, sums, wide = refs
    sums[...] = sums_in[...]
    close(order, named, state, [relay], sums, wide)
    size = sums.shape[0] // len(outs)
    for k, out in enumerate(outs):
        out[...] = sums[k * size:(k + 1) * size, :].reshape(out.shape).astype(out.dtype)


def in_planes(prefix, first_suffix, pair_prefix, pair_suffix, merge_count, suffix, routes, cap):
    owners = lax.axis_size("bits")
    planes = owners // PLANE
    pieces = pair_prefix.shape[0]
    held, rows_piece, twice_width = prefix.shape
    blocks, _, depth, width = first_suffix.shape
    part, span = width // 2, width // (planes // 2)
    vmem = pl.BlockSpec(memory_space=pltpu.VMEM)
    params = pltpu.CompilerParams(vmem_limit_bytes=VMEM_BYTES)
    relayed = blocks * 2 * depth * (part // LANES) + part
    tail = HEAD + 2 * (span // LANES) * held * rows_piece
    sources = (
        first_suffix.reshape(blocks * 2 * depth, width),
        prefix.reshape(held * rows_piece, twice_width),
        suffix[0],
        jnp.swapaxes(cap, 1, 2),
        pair_prefix.T,
        pair_suffix.T,
        merge_count[None],
        routes,
    )
    sizes = [relayed] * 2 + [part + tail, part] + [tail] * 2
    anywhere = pl.BlockSpec(memory_space=pl.ANY)
    packs = pl.pallas_call(
        functools.partial(pack_kernel, planes, pair_prefix.shape[1], held),
        out_shape=[jax.ShapeDtypeStruct((size, LANES), jnp.bfloat16) for size in sizes],
        in_specs=[anywhere] * len(sources),
        out_specs=[anywhere] * len(sizes),
        scratch_shapes=[pltpu.VMEM((size, LANES), jnp.bfloat16) for size in sizes]
        + [pltpu.VMEM(source.shape, source.dtype) for source in sources]
        + [pltpu.SemaphoreType.DMA((len(sources) + 1 + 2 * planes,))],
        compiler_params=pltpu.CompilerParams(vmem_limit_bytes=PACK_BYTES),
        cost_estimate=pl.CostEstimate(flops=2 ** 20, bytes_accessed=2 ** 12, transcendentals=0),
        name="pack",
    )(*sources)
    far = [swap(packs[k], k * PLANE) for k in range(2, planes)]
    near = swap(packs[planes + 1], PLANE)
    group, rest = join(far, part)
    handed = swap(rest, PLANE)
    relays = [packs[0][None], swap(packs[1], PLANE)[None], group]
    own, local = own_copy(relays[0], packs[planes])
    across = [swap(r, 2) for r in relays]
    relays[0] = own
    packs = [local, near, far[0], handed]
    far_beside = swap(after(relays[2], near), 1)
    beside = [swap(relays[0], 1), swap(relays[1], 1), far_beside]
    corner = [swap(after(across[0], far_beside), 1), swap(after(across[1], handed), 1), swap(across[2], 1)]
    early = 2 * PLANE
    far_slots = range(early, owners, PLANE)
    order = list(range(early)) + [k + n for n in (0, 1, 2) for k in far_slots]
    last = [k + 3 for k in far_slots]
    relays = [group[n] for n in range(2) for group in (relays, beside, across, corner)] + [relays[2], beside[2], across[2]]
    tiny = pl.CostEstimate(flops=0, bytes_accessed=2 ** 12, transcendentals=0)

    def sums_of(chosen, dtype):
        count = len(chosen)
        rows = count * pieces * rows_piece
        operands = relays[:early] + [packs[k] for k in chosen] + relays[early:]
        state, named, sums = pl.pallas_call(
            functools.partial(front_kernel, count, list(chosen).index(planes - 1) if planes - 1 in chosen else None, owners, order, blocks, pieces, rows_piece, held),
            out_shape=[
                jax.ShapeDtypeStruct((rows, 2 * part), jnp.bfloat16),
                jax.ShapeDtypeStruct((rows, LANES), jnp.float32),
                jax.ShapeDtypeStruct((rows, LANES), jnp.float32),
            ],
            in_specs=[vmem] * len(operands),
            out_specs=[vmem] * 3,
            scratch_shapes=[
                pltpu.VMEM((blocks, span, 2 * part), jnp.bfloat16),
                pltpu.VMEM((count, blocks * held * rows_piece, 2 * part), jnp.bfloat16),
                pltpu.VMEM((count, blocks * held * rows_piece, 2 * part), jnp.bfloat16),
                pltpu.VMEM((2 * part, len(order) * LANES), jnp.bfloat16),
            ],
            compiler_params=params,
            cost_estimate=tiny,
            name="front",
        )(*operands)
        return pl.pallas_call(
            functools.partial(last_kernel, last),
            out_shape=[jax.ShapeDtypeStruct((pieces, rows_piece, LANES), dtype)] * count,
            in_specs=[vmem] * 4,
            out_specs=[vmem] * count,
            scratch_shapes=[
                pltpu.VMEM((rows, LANES), jnp.float32),
                pltpu.VMEM((2 * part, len(last) * LANES), jnp.bfloat16),
            ],
            compiler_params=params,
            cost_estimate=tiny,
            name="last",
        )(named, state, sums, corner[2])

    sent = sums_of(range(1, planes), jnp.bfloat16)
    total = sums_of([0], jnp.float32)[0]
    for k in range(1, planes):
        total = total + swap(sent[k - 1], k * PLANE).astype(jnp.float32)
    return total


def by_owner(prefix, first_suffix, pair_prefix, pair_suffix, merge_count, suffix, routes, cap):
    pieces = pair_prefix.shape[0]
    merges = pair_prefix.shape[1]
    held_blocks = prefix.shape[0]
    rows_piece = prefix.shape[1]
    twice_width = prefix.shape[2]
    half_width = twice_width // 2
    first_count = first_suffix.shape[0]
    listed = routes.shape[1]
    owners = lax.axis_size("bits")
    slot_count = min(pieces, max(2, (2 * pieces * listed + owners - 1) // owners))
    live_mask = lax.broadcasted_iota(jnp.int32, (pieces, merges), 1) < merge_count[:, None]
    matches = (
        pair_suffix[:, :, None] == lax.broadcasted_iota(jnp.int32, (pieces, merges, first_count), 2)
    ) & live_mask[:, :, None]
    which_block = pair_prefix[:, :, None] == lax.broadcasted_iota(
        jnp.int32, (pieces, merges, held_blocks), 2
    )
    prefix_picks = jnp.einsum(
        "ika,ikp->iap", matches.astype(jnp.float32), which_block.astype(jnp.float32)
    ).astype(jnp.bfloat16)
    selected = jnp.einsum(
        "iap,prc->airc", prefix_picks, prefix, preferred_element_type=jnp.float32
    ).astype(jnp.bfloat16)
    selected = selected.reshape(first_count, pieces * rows_piece, twice_width)
    portion = lax.all_gather(first_suffix, "bits", axis=2, tiled=True)
    count_rows = portion.shape[2]
    real_cols = lax.slice_in_dim(selected, 0, count_rows, axis=2)
    imag_cols = lax.dynamic_slice_in_dim(selected, half_width, count_rows, 2)
    left_side = jnp.concatenate([real_cols, imag_cols], axis=2)
    upper_half = jnp.concatenate([portion[:, 0], portion[:, 1]], axis=2)
    lower_half = jnp.concatenate([-portion[:, 1], portion[:, 0]], axis=2)
    right_side = jnp.concatenate([upper_half, lower_half], axis=1)
    state_rows = jnp.einsum(
        "arc,acw->rw", left_side, right_side, preferred_element_type=jnp.float32
    )
    state_rows = state_rows.astype(jnp.bfloat16).reshape(pieces, rows_piece, twice_width)
    named_by = jnp.sum(
        (routes[:, :, None] == lax.broadcasted_iota(jnp.int32, (pieces, listed, owners), 2)).astype(
            jnp.int32
        ),
        axis=1,
    )
    slot_rank = jnp.cumsum(named_by, axis=0) - named_by
    slot_hit = (
        slot_rank[:, :, None] == lax.broadcasted_iota(jnp.int32, (pieces, owners, slot_count), 2)
    ) & (named_by[:, :, None] > 0)
    dispatch = jnp.transpose(slot_hit, (1, 2, 0)).astype(jnp.bfloat16)
    outgoing = jnp.einsum(
        "dmi,irc->dmrc", dispatch, state_rows, preferred_element_type=jnp.float32
    ).astype(jnp.bfloat16)
    own_form = complex_form(suffix[0])
    cap_form = complex_form(cap)
    products = jnp.einsum(
        "smrc,cw->smrw",
        lax.all_to_all(outgoing, "bits", split_axis=0, concat_axis=0, tiled=True),
        own_form,
        preferred_element_type=jnp.float32,
    ).astype(jnp.bfloat16)
    capped_terms = jnp.einsum(
        "smrw,wv->smrv", products, cap_form, preferred_element_type=jnp.float32
    )
    returned = lax.all_to_all(
        capped_terms.astype(jnp.bfloat16), "bits", split_axis=0, concat_axis=0, tiled=True
    ).astype(capped_terms.dtype)
    return jnp.einsum(
        "dmi,dmrv->irv", dispatch.astype(jnp.float32), returned, precision=HIGHEST_PRECISION
    )


def on_device(*args):
    prefix, first_suffix, pair_prefix, routes, cap = args[0], args[1], args[2], args[6], args[7]
    owners = lax.axis_size("bits")
    planes = owners // PLANE
    depth, width = first_suffix.shape[2:]
    pieces = pair_prefix.shape[0]
    fits = (
        planes == 4
        and owners == planes * PLANE
        and width == owners * depth
        and width % (planes // 2 * LANES) == 0
        and width // 2 % LANES == 0
        and 2 * cap.shape[2] == LANES
        and depth % 16 == 0
        and prefix.shape[1] % 16 == 0
        and pieces <= HEAD
        and first_suffix.shape[0] * prefix.shape[0] <= owners
        and 3 * owners <= LANES
    )
    return in_planes(*args) if fits else by_owner(*args)


def solution(mesh):
    return jax.shard_map(
        on_device,
        mesh=mesh,
        in_specs=(
            P(("grp", "bits"), None, None),
            P("grp", None, "bits", None),
            P(("grp", "bits"), None),
            P(("grp", "bits"), None),
            P(("grp", "bits")),
            P(("grp", "bits"), None, None, None),
            P(("grp", "bits"), None),
            P(),
        ),
        out_specs=P(("grp", "bits"), None, None),
        check_vma=False,
    )
```
